32 devices in a mesh: inst: 16 (over z, x, core), tp: 2 (over y).
Axes of the slice: x: 2, y: 2, z: 4, core: 2. Of those that a mesh axis runs over, the one named last changes fastest.
Arguments:
- prompt_query: bfloat16 [10240, 8192], P('inst', 'tp'), may hold values from -40 to 40
- prompt_pairs: bfloat16 [10240, 2048], P('inst', 'tp'), may hold values from -40 to 40
- decode_query: bfloat16 [64, 8192], P('inst'), may hold values from -40 to 40
- arrival_query: bfloat16 [16, 8192], P('inst'), may hold values from -40 to 40
- cache_pool: bfloat16 [160, 64, 2048], P(('inst', 'tp')), may hold values from -40 to 40
- page_table: int32 [64, 16], P('inst', 'tp'), may hold values from 0 to 4
- lengths: int32 [64], P('inst'), may hold values from 1 to 1024, as said below
- assignment: int32 [8], replicated, may hold values from 0 to 7, each once
Outputs:
- prefill_out: bfloat16 [10240, 8192], P('inst', 'tp')
- handed: bfloat16 [10240, 2048], P(('inst', 'tp'))
- decode_out: bfloat16 [64, 8192], P('inst')
- arrival_out: bfloat16 [16, 8192], P('inst')
The draws below stay inside these ranges and needn't reach their ends.
Inputs may be any that keep to these rules, and one draw needn't show every extreme that they name: `lengths`: some cached request of a decode instance has length 1024 in every draw. `assignment`: each decode instance receives the request of exactly one prefill instance.
All inputs are finite; a program needn't handle non-finite values.
Results may differ from the reference program's by a relative error of at most 0.0075.
Values may be sent and summed in bfloat16 or wider, within the bound.
No kernel may reach another device: no remote copies, remote signals or barrier semaphores. Data moves between devices by JAX's collectives and lax.ppermute only.
A program may use at most 128 MiB of HBM per device.

```python
import jax
import jax.numpy as jnp
from jax import lax

QHEADS = 64
KVHEADS = 8
HEADDIM = 128
PROMPT = 640
DEC_ROWS = 4
PAGE_LEN = 64
PAGES_DEV = 8
POOL_DEV = 5
PREFILL = 8
TOKENS = 10240
DECODE_ROWS = 64
POOL_PAGES = 160
MAXLEN = 1024
N_INST = 16
N_TP = 2


def draw_prompt_query(key, part):
    key = jax.random.fold_in(key, 1)
    values = jnp.clip(jax.random.normal(key, (TOKENS, QHEADS, HEADDIM), jnp.float32), -6.0, 6.0)
    return values.reshape(TOKENS, QHEADS * HEADDIM).astype(jnp.bfloat16)


def draw_prompt_pairs(key, part):
    key = jax.random.fold_in(key, 2)
    values = jnp.clip(jax.random.normal(key, (TOKENS, KVHEADS, 2, HEADDIM), jnp.float32), -6.0, 6.0)
    return values.reshape(TOKENS, KVHEADS * 2 * HEADDIM).astype(jnp.bfloat16)


def draw_decode_query(key, part):
    key = jax.random.fold_in(key, 3)
    values = jnp.clip(jax.random.normal(key, (DECODE_ROWS, QHEADS, HEADDIM), jnp.float32), -6.0, 6.0)
    return values.reshape(DECODE_ROWS, QHEADS * HEADDIM).astype(jnp.bfloat16)


def draw_arrival_query(key, part):
    key = jax.random.fold_in(key, 4)
    values = jnp.clip(jax.random.normal(key, (N_INST, QHEADS, HEADDIM), jnp.float32), -6.0, 6.0)
    return values.reshape(N_INST, QHEADS * HEADDIM).astype(jnp.bfloat16)


def draw_cache_pool(key, part):
    key = jax.random.fold_in(key, 5)
    values = jnp.clip(jax.random.normal(key, (POOL_PAGES, PAGE_LEN, KVHEADS, 2, HEADDIM), jnp.float32), -6.0, 6.0)
    return values.reshape(POOL_PAGES, PAGE_LEN, KVHEADS * 2 * HEADDIM).astype(jnp.bfloat16)


def draw_lengths(key, part):
    key = jax.random.fold_in(key, 6)
    values = jax.random.randint(key, (DECODE_ROWS,), 1, MAXLEN + 1, jnp.int32)
    spot = jax.random.randint(jax.random.fold_in(key, 1), (), PREFILL * DEC_ROWS, DECODE_ROWS, jnp.int32)
    return jnp.where(jnp.arange(DECODE_ROWS, dtype=jnp.int32) == spot, MAXLEN, values).astype(jnp.int32)


def with_ends(entries, stream_key, low, largest):
    spot = [jax.random.randint(jax.random.fold_in(stream_key, axis), (), 0, length) for axis, length in enumerate(entries.shape)]
    longest = entries.shape.index(max(entries.shape))
    next_to = spot[:longest] + [(spot[longest] + 1) % entries.shape[longest]] + spot[longest + 1:]
    return entries.at[tuple(spot)].set(low).at[tuple(next_to)].set(largest)


def setup_inputs(seed: int = 0) -> dict:
    seeds = jax.random.split(jax.random.key(seed), 9)
    prompt_query = draw_prompt_query(jax.random.fold_in(seeds[8], 71), 0)
    prompt_pairs = draw_prompt_pairs(jax.random.fold_in(seeds[8], 71), 0)
    decode_query = draw_decode_query(jax.random.fold_in(seeds[8], 71), 0)
    arrival_query = draw_arrival_query(jax.random.fold_in(seeds[8], 71), 0)
    cache_pool = draw_cache_pool(jax.random.fold_in(seeds[8], 71), 0)
    page_table = with_ends(jax.random.randint(seeds[5], (DECODE_ROWS, N_TP * PAGES_DEV), 0, POOL_DEV), jax.random.fold_in(seeds[5], 1), 0, POOL_DEV - 1).astype(jnp.int32)
    lengths = draw_lengths(jax.random.fold_in(seeds[8], 71), 0)
    assignment = jax.random.permutation(seeds[7], PREFILL).astype(jnp.int32)
    return dict(prompt_query=prompt_query, prompt_pairs=prompt_pairs, decode_query=decode_query, arrival_query=arrival_query, cache_pool=cache_pool, page_table=page_table, lengths=lengths, assignment=assignment)


NEG_FILL = -1e30


def prompt_attention(queries, pairs, group_size):
    length = queries.shape[0]
    head_count = queries.shape[1] // HEADDIM
    pair_heads = pairs.shape[1] // (2 * HEADDIM)
    score_scale = HEADDIM ** -0.5
    shaped = pairs.reshape(length, pair_heads, 2, HEADDIM)
    key_heads = jnp.transpose(shaped[:, :, 0], (1, 0, 2))
    value_heads = jnp.transpose(shaped[:, :, 1], (1, 0, 2))
    query_heads = jnp.transpose(queries.reshape(length, head_count, HEADDIM), (1, 0, 2))
    places = jnp.arange(length, dtype=jnp.int32)
    causal = places[:, None] >= places[None, :]

    def one_head(record):
        query_head, number = record
        keys = lax.dynamic_index_in_dim(key_heads, number // group_size, 0, False)
        values = lax.dynamic_index_in_dim(value_heads, number // group_size, 0, False)
        scores = jnp.dot(query_head, keys.T, preferred_element_type=jnp.float32) * score_scale
        scores = jnp.where(causal, scores, NEG_FILL)
        peak = jnp.max(scores, axis=1, keepdims=True)
        weights = jnp.exp(scores - peak)
        total = jnp.sum(weights, axis=1, keepdims=True)
        mixed = jnp.dot(weights.astype(jnp.bfloat16), values, preferred_element_type=jnp.float32)
        return (mixed / total).astype(jnp.bfloat16)

    heads_out = lax.map(one_head, (query_heads, jnp.arange(head_count, dtype=jnp.int32)))
    return jnp.transpose(heads_out, (1, 0, 2)).reshape(length, head_count * HEADDIM)


def decode_attention(query, keys, values, valid):
    score_scale = HEADDIM ** -0.5
    scores = jnp.einsum("rkgd,rtkd->rkgt", query.astype(jnp.float32), keys.astype(jnp.float32)) * score_scale
    mask = valid[:, None, None, :]
    scores = jnp.where(mask, scores, NEG_FILL)
    peak = jnp.max(scores, axis=3, keepdims=True)
    weights = jnp.where(mask, jnp.exp(scores - peak), 0.0)
    total = jnp.sum(weights, axis=3)
    rounded = lax.optimization_barrier(weights.astype(jnp.bfloat16))
    mixed = jnp.einsum("rkgt,rtkd->rkgd", rounded.astype(jnp.float32), values.astype(jnp.float32))
    return (mixed / total[..., None]).astype(jnp.bfloat16)


def reference(prompt_query, prompt_pairs, decode_query, arrival_query, cache_pool, page_table, lengths, assignment):
    width = KVHEADS * 2 * HEADDIM
    qwidth = QHEADS * HEADDIM
    group_size = QHEADS // KVHEADS
    prefill_count = N_INST // 2
    decode_count = N_INST - prefill_count
    queries = prompt_query.reshape(N_INST, PROMPT, qwidth)[:prefill_count]
    pairs = prompt_pairs.reshape(N_INST, PROMPT, width)
    made = lax.map(lambda record: prompt_attention(record[0], record[1], group_size), (queries, pairs[:prefill_count]))
    prefill_out = jnp.concatenate([made.reshape(prefill_count * PROMPT, qwidth), jnp.zeros((decode_count * PROMPT, qwidth), jnp.bfloat16)], axis=0)
    decode_ids = jnp.arange(prefill_count, dtype=jnp.int32)
    matches = assignment[None, :] == decode_ids[:, None]
    source = jnp.sum(jnp.where(matches, decode_ids[None, :], 0), axis=1).astype(jnp.int32)
    arrived = jnp.take(pairs, source, axis=0)
    handed = jnp.concatenate([jnp.zeros((prefill_count * PROMPT, width), jnp.bfloat16), arrived.reshape(decode_count * PROMPT, width)], axis=0)
    span = PAGES_DEV * PAGE_LEN
    places = jnp.arange(MAXLEN, dtype=jnp.int32)
    device_of = places // span
    column = device_of * PAGES_DEV + (places // PAGE_LEN) % PAGES_DEV
    offset = places % PAGE_LEN
    flat_pool = cache_pool.reshape(POOL_PAGES * PAGE_LEN, width)
    tables = page_table.reshape(N_INST, DEC_ROWS, N_TP * PAGES_DEV)[prefill_count:]
    row_lengths = lengths.reshape(N_INST, DEC_ROWS)[prefill_count:]
    cached_query = decode_query.reshape(N_INST, DEC_ROWS, KVHEADS, group_size, HEADDIM)[prefill_count:]
    first_query = arrival_query.reshape(N_INST, 1, KVHEADS, group_size, HEADDIM)[prefill_count:]
    instance_ids = jnp.arange(prefill_count, N_INST, dtype=jnp.int32)

    def decode_instance(record):
        table, length, query, received, first, instance = record
        pages = jnp.take(table, column, axis=1)
        index = ((instance * N_TP + device_of)[None, :] * POOL_DEV + pages) * PAGE_LEN + offset[None, :]
        rows_pairs = jnp.take(flat_pool, index.astype(jnp.int32), axis=0).reshape(DEC_ROWS, MAXLEN, KVHEADS, 2, HEADDIM)
        valid = places[None, :] < length[:, None]
        cached = decode_attention(query, rows_pairs[:, :, :, 0], rows_pairs[:, :, :, 1], valid)
        fresh_pairs = received.reshape(1, PROMPT, KVHEADS, 2, HEADDIM)
        fresh = decode_attention(first, fresh_pairs[:, :, :, 0], fresh_pairs[:, :, :, 1], jnp.ones((1, PROMPT), bool))
        return cached, fresh

    cached, fresh = lax.map(decode_instance, (tables, row_lengths, cached_query, arrived, first_query, instance_ids))
    decode_out = jnp.concatenate([jnp.zeros((prefill_count * DEC_ROWS, qwidth), jnp.bfloat16), cached.reshape(decode_count * DEC_ROWS, qwidth)], axis=0)
    arrival_out = jnp.concatenate([jnp.zeros((prefill_count, qwidth), jnp.bfloat16), fresh.reshape(decode_count, qwidth)], axis=0)
    return prefill_out, handed, decode_out, arrival_out
```

```python
import functools

import jax
import jax.numpy as jnp
from jax import lax
from jax.experimental import pallas as pl
from jax.experimental.pallas import tpu as pltpu
from jax.sharding import PartitionSpec as P

QHEADS = 64
KVHEADS = 8
HEADDIM = 128
GROUP = QHEADS // KVHEADS
SCALE = HEADDIM ** (-0.5)
LOG2E = 1.4426950408889634
NEG_FILL = -1e30
TILE = 128
VMEM = 48 * 1024 * 1024


def dot_t(a, b):
    return lax.dot_general(a, b, (((1,), (1,)), ((), ())), preferred_element_type=jnp.float32)


def dot(a, b):
    return lax.dot_general(a, b, (((1,), (0,)), ((), ())), preferred_element_type=jnp.float32)


def prompt_kernel(heads, flag_ref, q_ref, kv_ref, *rest):
    out_ref = rest[-1]
    length = q_ref.shape[0]

    @pl.when(flag_ref[0] == 0)
    def _():
        out_ref[...] = jnp.zeros_like(out_ref)

    @pl.when(flag_ref[0] != 0)
    def _():
        rows_all = lax.broadcasted_iota(jnp.int32, (TILE, TILE), 0)
        cols_all = lax.broadcasted_iota(jnp.int32, (TILE, TILE), 1)
        below = jnp.concatenate([rows_all >= cols_all] * heads, axis=0)
        ones = jnp.ones((length, HEADDIM), jnp.bfloat16)
        values = jnp.concatenate([kv_ref[:, HEADDIM:], ones], axis=1)
        for start in range(0, length, TILE):
            stop = start + TILE
            queries = jnp.concatenate(
                [q_ref[start:stop, h * HEADDIM : (h + 1) * HEADDIM] for h in range(heads)], axis=0
            )
            scores = dot_t(queries, kv_ref[:stop, :HEADDIM])
            last = jnp.where(below, scores[:, start:], NEG_FILL)
            scores = jnp.concatenate([scores[:, :start], last], axis=1) if start else last
            peak = jnp.max(scores, axis=1, keepdims=True)
            weights = jnp.exp2((scores - peak) * (SCALE * LOG2E)).astype(jnp.bfloat16)
            mixed = dot(weights, values[:stop])
            result = (mixed[:, :HEADDIM] / mixed[:, HEADDIM:]).astype(jnp.bfloat16)
            for h in range(heads):
                out_ref[start:stop, h * HEADDIM : (h + 1) * HEADDIM] = result[
                    h * TILE : (h + 1) * TILE
                ]


def prompt_attention(flag, queries, pairs, first, steps, heads, earlier):
    length, width = queries.shape
    per_kv = GROUP // heads

    def q_map(i, flag_ref):
        return (0, jnp.where(flag_ref[0] != 0, i + first, 0))

    def kv_map(i, flag_ref):
        return (0, jnp.where(flag_ref[0] != 0, (i + first) // per_kv, 0))

    in_specs = [
        pl.BlockSpec((length, heads * HEADDIM), q_map),
        pl.BlockSpec((length, 2 * HEADDIM), kv_map),
    ]
    operands = [flag, queries, pairs]
    aliases = {}
    if earlier is not None:
        in_specs.append(pl.BlockSpec(memory_space=pl.ANY))
        operands.append(earlier)
        aliases = {3: 0}
    return pl.pallas_call(
        functools.partial(prompt_kernel, heads),
        out_shape=jax.ShapeDtypeStruct((length, width), jnp.bfloat16),
        grid_spec=pltpu.PrefetchScalarGridSpec(
            num_scalar_prefetch=1,
            grid=(steps,),
            in_specs=in_specs,
            out_specs=pl.BlockSpec((length, heads * HEADDIM), lambda i, flag_ref: (0, i + first)),
        ),
        input_output_aliases=aliases,
        compiler_params=pltpu.CompilerParams(vmem_limit_bytes=VMEM),
        cost_estimate=pl.CostEstimate(
            flops=steps * heads * 4 * length * length * HEADDIM,
            bytes_accessed=steps * heads * length * HEADDIM * 4,
            transcendentals=steps * heads * length * length // 2,
        ),
        name="prompt_attention",
    )(*operands)


def cache_kernel(q_ref, kv_ref, count_ref, mixed_ref, stats_ref):
    count = count_ref[...]
    here = count > 0.0
    scores = dot_t(q_ref[0], kv_ref[:, :HEADDIM]) * SCALE
    scores = jnp.where(here, scores, NEG_FILL)
    peak = jnp.max(scores, axis=1, keepdims=True)
    weights = jnp.where(here, jnp.exp(scores - peak), 0.0)
    total = jnp.sum(weights * count, axis=1, keepdims=True)
    rounded = weights.astype(jnp.bfloat16).astype(jnp.float32) * count
    mixed_ref[0] = dot(rounded.astype(jnp.bfloat16), kv_ref[:, HEADDIM:])
    lane = lax.broadcasted_iota(jnp.int32, stats_ref.shape[1:], 1)
    stats_ref[0] = jnp.where(lane < HEADDIM // 2, peak, total)


def cache_attention(queries, pool, count):
    rows = queries.shape[1]
    tokens = pool.shape[0]
    shape = jax.ShapeDtypeStruct((KVHEADS, rows, HEADDIM), jnp.float32)
    block = pl.BlockSpec((1, rows, HEADDIM), lambda h: (h, 0, 0))
    return pl.pallas_call(
        cache_kernel,
        out_shape=(shape, shape),
        grid=(KVHEADS,),
        in_specs=[
            block,
            pl.BlockSpec((tokens, 2 * HEADDIM), lambda h: (0, h)),
            pl.BlockSpec((rows, tokens), lambda h: (0, 0)),
        ],
        out_specs=(block, block),
        compiler_params=pltpu.CompilerParams(vmem_limit_bytes=VMEM),
        name="cache_attention",
    )(queries, pool, count)


def fresh_kernel(q_ref, kv_ref, out_ref):
    scores = dot_t(q_ref[0], kv_ref[:, :HEADDIM]) * SCALE
    peak = jnp.max(scores, axis=1, keepdims=True)
    weights = jnp.exp(scores - peak)
    total = jnp.sum(weights, axis=1, keepdims=True)
    mixed = dot(weights.astype(jnp.bfloat16), kv_ref[:, HEADDIM:])
    out_ref[0] = (mixed / total).astype(jnp.bfloat16)


def fresh_attention(queries, pairs):
    length, width = pairs.shape
    block = pl.BlockSpec((1, GROUP, HEADDIM), lambda h: (h, 0, 0))
    return pl.pallas_call(
        fresh_kernel,
        out_shape=jax.ShapeDtypeStruct(queries.shape, jnp.bfloat16),
        grid=(queries.shape[0],),
        in_specs=[block, pl.BlockSpec((length, 2 * HEADDIM), lambda h: (0, h))],
        out_specs=block,
        compiler_params=pltpu.CompilerParams(vmem_limit_bytes=VMEM),
        name="fresh_attention",
    )(queries, pairs)


def relay_handoff(pairs, source, inst_count):
    half = inst_count // 2
    moved = lax.all_to_all(pairs, "tp", split_axis=0, concat_axis=1, tiled=True)
    lanes = 1024 if moved.size % (inst_count * 1024) == 0 else HEADDIM
    pieces = moved.reshape(inst_count, -1, lanes)
    spread = lax.all_to_all(pieces, "inst", split_axis=0, concat_axis=0, tiled=True)
    chosen = jnp.stack(
        [lax.dynamic_index_in_dim(spread, source[d], 0, False) for d in range(half)], axis=0
    )
    outgoing = jnp.concatenate([jnp.zeros_like(chosen), chosen], axis=0)
    delivered = lax.all_to_all(outgoing, "inst", split_axis=0, concat_axis=0, tiled=True)
    return delivered.reshape(moved.shape)


def shards(
    prompt_query,
    prompt_pairs,
    decode_query,
    arrival_query,
    cache_pool,
    page_table,
    lengths,
    assignment,
):
    inst_count = lax.axis_size("inst")
    tp_count = lax.axis_size("tp")
    half = inst_count // 2
    inst = lax.axis_index("inst")
    tp_index = lax.axis_index("tp")
    is_prefill = inst < half
    flag = is_prefill.astype(jnp.int32).reshape(1)
    groups = [list(range(half)), list(range(half, inst_count))]
    decode_ids = jnp.arange(half, dtype=jnp.int32)
    matches = assignment[None, :] == decode_ids[:, None]
    source = jnp.sum(jnp.where(matches, decode_ids[None, :], 0), axis=1).astype(jnp.int32)

    handed = relay_handoff(prompt_pairs, source, inst_count)

    sent = lax.ppermute(arrival_query, "inst", [(i + half, i) for i in range(half)])
    every = lax.all_gather(sent, "inst", axis=0, tiled=True, axis_index_groups=groups)
    target = lax.dynamic_index_in_dim(assignment, lax.rem(inst, half), 0, False)
    kv_here = prompt_pairs.shape[1] // (2 * HEADDIM)
    width = kv_here * GROUP * HEADDIM
    mine = lax.dynamic_slice(every, (target, tp_index * width), (1, width))
    fresh = fresh_attention(mine.reshape(kv_here, GROUP, HEADDIM), prompt_pairs)
    fresh = lax.ppermute(fresh.reshape(1, width), "inst", [(i, i + half) for i in range(half)])
    results = lax.all_gather(fresh, "inst", axis=0, tiled=True, axis_index_groups=groups)
    from_inst = lax.dynamic_index_in_dim(source, lax.rem(inst, half), 0, False)
    part = lax.dynamic_index_in_dim(results, from_inst, 0, True)
    arrival_out = lax.all_gather(part, "tp", axis=1, tiled=True)
    arrival_out = jnp.where(is_prefill, jnp.zeros_like(arrival_out), arrival_out)

    rows = decode_query.shape[0]
    pages, page_len = cache_pool.shape[0], cache_pool.shape[1]
    slots = page_table.shape[1]
    places = tp_index * slots * page_len + jnp.arange(slots * page_len, dtype=jnp.int32)
    valid = (places.reshape(1, slots, page_len) < lengths[:, None, None])[:, None]
    same = page_table[:, None, :] == jnp.arange(pages, dtype=jnp.int32)[None, :, None]
    count = jnp.sum(jnp.where(valid & same[..., None], 1.0, 0.0), axis=2)
    count = count.reshape(rows, 1, pages * page_len)
    count = jnp.broadcast_to(count, (rows, GROUP, pages * page_len)).reshape(rows * GROUP, -1)
    queries = decode_query.reshape(rows, KVHEADS, GROUP, HEADDIM).transpose(1, 0, 2, 3)
    mixed, stats = cache_attention(
        queries.reshape(KVHEADS, rows * GROUP, HEADDIM),
        cache_pool.reshape(pages * page_len, -1),
        count,
    )
    parts = lax.all_gather(jnp.concatenate([mixed, stats], axis=2), "tp")
    peaks = parts[:, :, :, HEADDIM : HEADDIM + 1]
    totals = parts[:, :, :, -1:]
    factors = jnp.exp(peaks - jnp.max(peaks, axis=0, keepdims=True))
    summed = jnp.sum(parts[:, :, :, :HEADDIM] * factors, axis=0)
    total = jnp.sum(totals * factors, axis=0)
    finished = (summed / total).astype(jnp.bfloat16)
    finished = finished.reshape(KVHEADS, rows, GROUP, HEADDIM).transpose(1, 0, 2, 3)
    finished = finished.reshape(rows, QHEADS * HEADDIM)
    decode_out = jnp.where(is_prefill, jnp.zeros_like(finished), finished)

    heads = GROUP // 2
    steps = prompt_query.shape[1] // (heads * HEADDIM)
    prefill_out = prompt_attention(flag, prompt_query, prompt_pairs, 0, steps, heads, None)
    return (prefill_out, handed, decode_out, arrival_out)


def solution(mesh):
    return jax.shard_map(
        shards,
        mesh=mesh,
        in_specs=(
            P("inst", "tp"),
            P("inst", "tp"),
            P("inst", None),
            P("inst", None),
            P(("inst", "tp"), None, None),
            P("inst", "tp"),
            P("inst"),
            P(),
        ),
        out_specs=(P("inst", "tp"), P(("inst", "tp"), None), P("inst", None), P("inst", None)),
        check_vma=False,
    )
```

```python
import functools

import jax
import jax.numpy as jnp
from jax import lax
from jax.experimental import pallas as pl
from jax.experimental.pallas import tpu as pltpu
from jax.sharding import PartitionSpec as P

QHEADS = 64
KVHEADS = 8
HEADDIM = 128
GROUP = QHEADS // KVHEADS
SCALE = HEADDIM ** (-0.5)
LOG2E = 1.4426950408889634
NEG_FILL = -1e30
TILE = 128
VMEM = 24 * 1024 * 1024
SMALL = 1024 * 1024
LARGE = 57 * 1024 * 1024
COST = pl.CostEstimate(flops=1, bytes_accessed=1, transcendentals=0)


def dot_t(a, b):
    return lax.dot_general(a, b, (((1,), (1,)), ((), ())), preferred_element_type=jnp.float32)


def dot(a, b):
    return lax.dot_general(a, b, (((1,), (0,)), ((), ())), preferred_element_type=jnp.float32)


def prompt_kernel(heads, flag_ref, q_ref, kv_ref, *rest):
    out_ref = rest[-2]
    length = q_ref.shape[0]

    @pl.when(flag_ref[0] == 0)
    def _():
        out_ref[...] = jnp.zeros_like(out_ref)

    @pl.when(flag_ref[0] != 0)
    def _():
        rows_all = lax.broadcasted_iota(jnp.int32, (TILE, TILE), 0)
        cols_all = lax.broadcasted_iota(jnp.int32, (TILE, TILE), 1)
        below = jnp.concatenate([rows_all >= cols_all] * heads, axis=0)
        ones = jnp.ones((length, HEADDIM), jnp.bfloat16)
        values = jnp.concatenate([kv_ref[:, HEADDIM:], ones], axis=1)
        for start in range(0, length, TILE):
            stop = start + TILE
            queries = jnp.concatenate(
                [q_ref[start:stop, h * HEADDIM : (h + 1) * HEADDIM] for h in range(heads)], axis=0
            )
            scores = dot_t(queries, kv_ref[:stop, :HEADDIM])
            last = jnp.where(below, scores[:, start:], NEG_FILL)
            scores = jnp.concatenate([scores[:, :start], last], axis=1) if start else last
            peak = jnp.max(scores, axis=1, keepdims=True)
            weights = jnp.exp2((scores - peak) * (SCALE * LOG2E)).astype(jnp.bfloat16)
            mixed = dot(weights, values[:stop])
            result = (mixed[:, :HEADDIM] / mixed[:, HEADDIM:]).astype(jnp.bfloat16)
            for h in range(heads):
                out_ref[start:stop, h * HEADDIM : (h + 1) * HEADDIM] = result[
                    h * TILE : (h + 1) * TILE
                ]


MARK = jax.ShapeDtypeStruct((8, 128), jnp.float32)
IN_HBM = pl.BlockSpec(memory_space=pltpu.HBM)
ANYWHERE = pl.BlockSpec(memory_space=pl.ANY)


def prompt_attention(flag, queries, pairs, first, steps, heads, earlier, after):
    length, width = queries.shape
    per_kv = GROUP // heads

    def q_map(i, flag_ref):
        return (0, jnp.where(flag_ref[0] != 0, i + first, 0))

    def kv_map(i, flag_ref):
        return (0, jnp.where(flag_ref[0] != 0, (i + first) // per_kv, 0))

    in_specs = [
        pl.BlockSpec((length, heads * HEADDIM), q_map),
        pl.BlockSpec((length, 2 * HEADDIM), kv_map),
    ]
    operands = [flag, queries, pairs]
    aliases = {}
    if earlier is not None:
        in_specs.append(ANYWHERE)
        operands.append(earlier)
        aliases = {3: 0}
    return pl.pallas_call(
        functools.partial(prompt_kernel, heads),
        out_shape=(jax.ShapeDtypeStruct((length, width), jnp.bfloat16), MARK),
        grid_spec=pltpu.PrefetchScalarGridSpec(
            num_scalar_prefetch=1,
            grid=(steps,),
            in_specs=in_specs + [IN_HBM] * len(after),
            out_specs=(
                pl.BlockSpec((length, heads * HEADDIM), lambda i, flag_ref: (0, i + first)),
                IN_HBM,
            ),
        ),
        input_output_aliases=aliases,
        compiler_params=pltpu.CompilerParams(vmem_limit_bytes=LARGE),
        cost_estimate=COST,
        name="prompt_attention",
    )(*operands, *after)


def cache_kernel(flag_ref, q_ref, kv_ref, count_ref, *rest):
    out_ref = rest[-2]

    @pl.when(flag_ref[0] != 0)
    def _():
        out_ref[...] = jnp.zeros_like(out_ref)

    @pl.when(flag_ref[0] == 0)
    def _():
        rows, tokens = count_ref.shape
        count = jnp.broadcast_to(count_ref[...][:, None, :], (rows, GROUP, tokens))
        count = count.reshape(rows * GROUP, tokens)
        here = count > 0.0
        queries = q_ref[...].astype(jnp.float32).reshape(rows * GROUP, HEADDIM)
        scores = dot_t(queries.astype(jnp.bfloat16), kv_ref[:, :HEADDIM]) * SCALE
        scores = jnp.where(here, scores, NEG_FILL)
        peak = jnp.max(scores, axis=1, keepdims=True)
        weights = jnp.where(here, jnp.exp(scores - peak), 0.0)
        total = jnp.sum(weights * count, axis=1, keepdims=True)
        rounded = weights.astype(jnp.bfloat16).astype(jnp.float32) * count
        out_ref[0, :, :HEADDIM] = dot(rounded.astype(jnp.bfloat16), kv_ref[:, HEADDIM:])
        lane = lax.broadcasted_iota(jnp.int32, (rows * GROUP, HEADDIM), 1)
        out_ref[0, :, HEADDIM:] = jnp.where(lane < HEADDIM // 2, peak, total)


def cache_attention(flag, queries, pool, count, after):
    rows = queries.shape[0]
    tokens = pool.shape[0]
    return pl.pallas_call(
        cache_kernel,
        out_shape=(
            jax.ShapeDtypeStruct((KVHEADS, rows * GROUP, 2 * HEADDIM), jnp.float32),
            MARK,
        ),
        grid_spec=pltpu.PrefetchScalarGridSpec(
            num_scalar_prefetch=1,
            grid=(KVHEADS,),
            in_specs=[
                pl.BlockSpec((rows, GROUP, HEADDIM), lambda h, flag_ref: (0, h, 0)),
                pl.BlockSpec((tokens, 2 * HEADDIM), lambda h, flag_ref: (0, h * (1 - flag_ref[0]))),
                pl.BlockSpec((rows, tokens), lambda h, flag_ref: (0, 0)),
            ]
            + [IN_HBM] * len(after),
            out_specs=(
                pl.BlockSpec((1, rows * GROUP, 2 * HEADDIM), lambda h, flag_ref: (h, 0, 0)),
                IN_HBM,
            ),
        ),
        compiler_params=pltpu.CompilerParams(vmem_limit_bytes=VMEM),
        cost_estimate=COST,
        name="cache_attention",
    )(flag, queries, pool, count, *after)


def combine_kernel(count, flag_ref, *refs):
    part_refs, out_ref = refs[:count], refs[-2]

    @pl.when(flag_ref[0] != 0)
    def _():
        out_ref[...] = jnp.zeros_like(out_ref)

    @pl.when(flag_ref[0] == 0)
    def _():
        parts = [ref[n] for ref in part_refs for n in range(ref.shape[0])]
        peaks = [part[:, HEADDIM : HEADDIM + 1] for part in parts]
        peak = functools.reduce(jnp.maximum, peaks)
        factors = [jnp.exp(p - peak) for p in peaks]
        total = sum(part[:, -1:] * f for part, f in zip(parts, factors))
        mixed = sum(part[:, :HEADDIM] * f for part, f in zip(parts, factors))
        out_ref[...] = (mixed / total).reshape(out_ref.shape).astype(jnp.bfloat16)


def combine_parts(flag, parts, rows, after):
    return pl.pallas_call(
        functools.partial(combine_kernel, len(parts)),
        out_shape=(jax.ShapeDtypeStruct((rows, QHEADS, HEADDIM), jnp.bfloat16), MARK),
        grid_spec=pltpu.PrefetchScalarGridSpec(
            num_scalar_prefetch=1,
            grid=(KVHEADS,),
            in_specs=[
                pl.BlockSpec(
                    (part.shape[0], None, rows * GROUP, 2 * HEADDIM),
                    lambda h, flag_ref: (0, h, 0, 0),
                )
                for part in parts
            ]
            + [IN_HBM] * len(after),
            out_specs=(
                pl.BlockSpec((rows, GROUP, HEADDIM), lambda h, flag_ref: (0, h, 0)),
                IN_HBM,
            ),
        ),
        compiler_params=pltpu.CompilerParams(vmem_limit_bytes=VMEM),
        cost_estimate=COST,
        name="combine_parts",
    )(flag, *parts, *after)


def fresh_kernel(q_ref, kv_ref, *rest):
    out_ref = rest[-1]
    scores = dot_t(q_ref[0], kv_ref[:, :HEADDIM]) * SCALE
    peak = jnp.max(scores, axis=1, keepdims=True)
    weights = jnp.exp(scores - peak)
    total = jnp.sum(weights, axis=1, keepdims=True)
    mixed = dot(weights.astype(jnp.bfloat16), kv_ref[:, HEADDIM:])
    out_ref[...] = (mixed / total).astype(jnp.bfloat16)


def fresh_attention(queries, pairs, after=()):
    length, width = pairs.shape
    return pl.pallas_call(
        fresh_kernel,
        out_shape=jax.ShapeDtypeStruct((GROUP, width // 2), jnp.bfloat16),
        grid=(queries.shape[0],),
        in_specs=[
            pl.BlockSpec((1, GROUP, HEADDIM), lambda h: (h, 0, 0)),
            pl.BlockSpec((length, 2 * HEADDIM), lambda h: (0, h)),
        ]
        + [IN_HBM] * len(after),
        out_specs=pl.BlockSpec((GROUP, HEADDIM), lambda h: (0, h)),
        compiler_params=pltpu.CompilerParams(vmem_limit_bytes=VMEM),
        cost_estimate=COST,
        name="fresh_attention",
    )(queries, pairs, *after)


def relay_handoff(pairs, source, inst_count):
    half = inst_count // 2
    moved = lax.all_to_all(pairs, "tp", split_axis=0, concat_axis=1, tiled=True)
    lanes = 1024 if moved.size % (inst_count * 1024) == 0 else HEADDIM
    pieces = moved.reshape(inst_count, -1, lanes)
    spread = lax.all_to_all(pieces, "inst", split_axis=0, concat_axis=0, tiled=True)
    chosen = jnp.stack(
        [lax.dynamic_index_in_dim(spread, source[d], 0, False) for d in range(half)], axis=0
    )
    outgoing = jnp.concatenate([jnp.zeros_like(chosen), chosen], axis=0)
    delivered = lax.all_to_all(outgoing, "inst", split_axis=0, concat_axis=0, tiled=True)
    return delivered.reshape(moved.shape)


UNIT = 8
PAIRS = 4


def copy_kernel(plan, counts, prefetch_ref, *refs):
    inputs, marks, outputs = counts
    sources, targets, sems = refs[:inputs], refs[inputs + marks : inputs + marks + outputs], refs[-1]
    started = []
    for source, target in plan(prefetch_ref, sources, targets):
        started.append(pltpu.make_async_copy(source, target, sems.at[len(started)]))
    for copy in started:
        copy.start()
    for copy in started:
        copy.wait()


def copies(plan, number, prefetch, operands, shapes, name, after=()):
    return pl.pallas_call(
        functools.partial(copy_kernel, plan, (len(operands), len(after), len(shapes))),
        out_shape=tuple(jax.ShapeDtypeStruct(shape, jnp.bfloat16) for shape in shapes) + (MARK,),
        grid_spec=pltpu.PrefetchScalarGridSpec(
            num_scalar_prefetch=1,
            grid=(1,),
            in_specs=[ANYWHERE] * len(operands) + [IN_HBM] * len(after),
            out_specs=tuple([ANYWHERE] * len(shapes)) + (IN_HBM,),
            scratch_shapes=[pltpu.SemaphoreType.DMA((number,))],
        ),
        compiler_params=pltpu.CompilerParams(vmem_limit_bytes=SMALL),
        cost_estimate=COST,
        name=name,
    )(prefetch, *operands, *after)


def relay_slots_kernel(far, prefetch_ref, keep_ref, recv_ref, fresh_ref, out_ref, mark_ref, sems, fresh_sems):
    half = 2 * PAIRS
    waits = []
    for d in range(half):
        pair = lax.div(prefetch_ref[3 + d], 2)
        same = lax.rem(prefetch_ref[3 + d], 2) == prefetch_ref[1]
        shift = lax.rem(prefetch_ref[0] + PAIRS - pair, PAIRS)
        for tau in range(2):
            slot = tau * half + d
            target = out_ref.at[slot, pl.ds(0, far)]
            mine = pltpu.make_async_copy(keep_ref.at[shift, tau], target, sems.at[slot])
            other = pltpu.make_async_copy(recv_ref.at[shift, tau], target, sems.at[slot])
            pl.when(same)(mine.start)
            pl.when(jnp.logical_not(same))(other.start)
            extra = pltpu.make_async_copy(fresh_ref, out_ref.at[slot, far], fresh_sems.at[slot])
            extra.start()
            waits += [mine, extra]
    for copy in waits:
        copy.wait()


def rows_kernel(near, far, prefetch_ref, slots_ref, *refs):
    *parts, out_ref, zero_ref, sems = refs
    half = 2 * PAIRS
    width = slots_ref.shape[-1]
    near_all = near * half

    @pl.when(prefetch_ref[2] == 0)
    def _():
        waits = []
        for t in range(2):
            columns = pl.ds(t * width, width)
            for s, part in enumerate(parts):
                pair = lax.rem(prefetch_ref[0] + PAIRS - s, PAIRS)
                target = out_ref.at[pl.ds(pair * 2 * near, 2 * near), :, columns]
                waits.append(pltpu.make_async_copy(part.at[t], target, sems.at[len(waits)]))
            for i in range(half):
                source = slots_ref.at[t * half + i, pl.ds(0, far)]
                target = out_ref.at[pl.ds(near_all + i * far, far), :, columns]
                waits.append(pltpu.make_async_copy(source, target, sems.at[len(waits)]))
        for copy in waits:
            copy.start()
        for copy in waits:
            copy.wait()

    @pl.when(prefetch_ref[2] != 0)
    def _():
        zero_ref[...] = jnp.zeros_like(zero_ref)
        size = zero_ref.shape[0]
        waits = []
        for n in range(out_ref.shape[0] // size):
            target = out_ref.at[pl.ds(n * size, size)]
            waits.append(pltpu.make_async_copy(zero_ref, target, sems.at[n]))
        for copy in waits:
            copy.start()
        for copy in waits:
            copy.wait()


def two_way_handoff(pairs, source, flag, always, arrival_query, fresh_of, prompt_part, extra):
    half = 2 * PAIRS
    rows, width = pairs.shape
    units = rows // (2 * UNIT)
    far_all = -(-units * 3 // (5 * half)) * half
    near_all = units - far_all
    near, far = near_all // half, far_all // half
    inst = lax.axis_index("inst")
    pair, side = lax.div(lax.rem(inst, half), 2), lax.rem(inst, 2)
    prefetch = jnp.concatenate([jnp.stack([pair, side, flag[0]]), source])
    block = (UNIT, width)
    by_unit = pairs.reshape((rows // UNIT,) + block)
    groups = [[base + 2 * i + tau for tau in range(2) for i in range(half)] for base in (0, 2 * half)]

    def crossing(array, s):
        hops = [
            (2 * p + k, half + 2 * ((p + s) % PAIRS) + k) for p in range(PAIRS) for k in range(2)
        ]
        return lax.ppermute(array, "inst", hops)

    def beside(array, base):
        return lax.ppermute(array, "inst", [(base + i, base + (i ^ 1)) for i in range(half)])

    def spread_out(array):
        return lax.all_to_all(
            array, ("inst", "tp"), 0, 0, axis_index_groups=groups, tiled=True
        )

    def cut(pre, sources, targets):
        plan = []
        for s in range(PAIRS):
            start = near_all + lax.rem(pre[0] + s, PAIRS) * (2 * far)
            for tau in range(2):
                plan.append((sources[0].at[pl.ds(tau * units + start, 2 * far)], targets[s].at[tau]))
        return plan

    def near_slots(pre, sources, targets):
        plan = []
        for tau in range(2):
            for i in range(half):
                slot = tau * half + i
                rows_here = sources[0].at[pl.ds(tau * units + i * near, near)]
                plan.append((rows_here, targets[0].at[slot, pl.ds(0, near)]))
                plan.append((sources[1], targets[0].at[slot, near]))
        return plan

    def for_neighbour(pre, sources, targets):
        plan = []
        for s in range(PAIRS):
            receiver = lax.rem(pre[0] + s, PAIRS) * 2 + 1 - pre[1]
            for t in range(2):
                origin = t * half + pre[3 + receiver]
                plan.append((sources[0].at[origin, pl.ds(0, near)], targets[0].at[s, t]))
        return plan

    def for_receivers(pre, sources, targets):
        plan = []
        for s in range(PAIRS):
            receiver = lax.rem(pre[0] + s, PAIRS) * 2 + pre[1]
            for t in range(2):
                origin = t * half + pre[3 + receiver]
                mine = targets[s].at[t, pl.ds(pre[1] * near, near)]
                other = targets[s].at[t, pl.ds((1 - pre[1]) * near, near)]
                plan.append((sources[0].at[origin, pl.ds(0, near)], mine))
                plan.append((sources[1].at[s, t], other))
        return plan

    def split(pre, sources, targets):
        plan = []
        for s in range(PAIRS):
            for tau in range(2):
                mine = sources[s].at[tau, pl.ds(pre[1] * far, far)]
                other = sources[s].at[tau, pl.ds((1 - pre[1]) * far, far)]
                plan.append((mine, targets[0].at[s, tau]))
                plan.append((other, targets[1].at[s, tau]))
        return plan

    near_shape = (2, 2 * near) + block

    def first_stage(by_unit, asked):
        spread, mark = copies(
            near_slots,
            8 * PAIRS,
            prefetch,
            [by_unit, asked.reshape(block)],
            [(2 * half, near + 1) + block],
            "near_slots",
        )
        spread = spread_out(spread)
        part, mark = extra[0]([mark])
        prompt, mark = prompt_part(0, None, [mark])
        more, mark = extra[1](part, [mark])
        outgoing, mark = copies(
            for_neighbour,
            2 * PAIRS,
            prefetch,
            [spread],
            [(PAIRS, 2, near) + block],
            "for_neighbour",
            [mark],
        )
        incoming = beside(outgoing, 0)
        *near_parts, mark = copies(
            for_receivers, 4 * PAIRS, prefetch, [spread, incoming], [near_shape] * PAIRS, "for_receivers"
        )
        fresh = fresh_of(spread.reshape((2, half, near + 1) + block)[0, :, near], [mark])
        return *near_parts, prompt, fresh, more

    def second_stage(prompt, fresh, *far_here):
        keep, give, mark = copies(
            split, 4 * PAIRS, prefetch, list(far_here), [(PAIRS, 2, far) + block] * 2, "split_relays"
        )
        taken = beside(give, half)
        slots, mark = pl.pallas_call(
            functools.partial(relay_slots_kernel, far),
            out_shape=(jax.ShapeDtypeStruct((2 * half, far + 1) + block, jnp.bfloat16), MARK),
            grid_spec=pltpu.PrefetchScalarGridSpec(
                num_scalar_prefetch=1,
                grid=(1,),
                in_specs=[ANYWHERE] * 3,
                out_specs=(ANYWHERE, IN_HBM),
                scratch_shapes=[pltpu.SemaphoreType.DMA((2 * half,))] * 2,
            ),
            compiler_params=pltpu.CompilerParams(vmem_limit_bytes=SMALL),
            cost_estimate=COST,
            name="relay_slots",
        )(prefetch, keep, taken, jnp.pad(fresh, ((0, 0), (0, width // 2))))
        slots = spread_out(slots)
        prompt, mark = prompt_part(1, prompt, [mark])
        return prompt, slots

    def staged(stage, *operands):
        def never(*operands):
            outs = [jnp.zeros(out.shape, out.dtype) for out in jax.eval_shape(stage, *operands)]
            return tuple(outs) if stage is first_stage else (operands[0], *outs[1:])

        return lax.cond(always, lambda *operands: tuple(stage(*operands)), never, *operands)

    asked = lax.ppermute(arrival_query, "inst", [(i + half, i) for i in range(half)])
    *far_parts, _ = copies(
        cut, 2 * PAIRS, prefetch, [by_unit], [(2, 2 * far) + block] * PAIRS, "cut_far"
    )
    far_here = [crossing(part, s) for s, part in enumerate(far_parts)]
    *near_parts, prompt, fresh, more = staged(first_stage, by_unit, asked)
    near_here = [crossing(part, s) for s, part in enumerate(near_parts)]
    prompt, slots = staged(second_stage, prompt, fresh, *far_here)
    handed = pl.pallas_call(
        functools.partial(rows_kernel, near, far),
        out_shape=jax.ShapeDtypeStruct((units, UNIT, 2 * width), jnp.bfloat16),
        grid_spec=pltpu.PrefetchScalarGridSpec(
            num_scalar_prefetch=1,
            grid=(1,),
            in_specs=[ANYWHERE] * (PAIRS + 1),
            out_specs=ANYWHERE,
            scratch_shapes=[
                pltpu.VMEM((half, UNIT, 2 * width), jnp.bfloat16),
                pltpu.SemaphoreType.DMA((2 * (half + PAIRS),)),
            ],
        ),
        compiler_params=pltpu.CompilerParams(vmem_limit_bytes=SMALL),
        cost_estimate=COST,
        name="rows",
    )(prefetch, slots, *near_here)
    results = slots.reshape((2, half, far + 1) + block)[:, :, far]
    return handed.reshape(rows // 2, 2 * width), results, prompt, more


def shards(
    prompt_query,
    prompt_pairs,
    decode_query,
    arrival_query,
    cache_pool,
    page_table,
    lengths,
    assignment,
):
    inst_count = lax.axis_size("inst")
    tp_count = lax.axis_size("tp")
    half = inst_count // 2
    inst = lax.axis_index("inst")
    tp_index = lax.axis_index("tp")
    is_prefill = inst < half
    flag = is_prefill.astype(jnp.int32).reshape(1)
    groups = [list(range(half)), list(range(half, inst_count))]
    decode_ids = jnp.arange(half, dtype=jnp.int32)
    matches = assignment[None, :] == decode_ids[:, None]
    source = jnp.sum(jnp.where(matches, decode_ids[None, :], 0), axis=1).astype(jnp.int32)
    rows = decode_query.shape[0]
    pages, page_len = cache_pool.shape[0], cache_pool.shape[1]
    slots = page_table.shape[1]
    places = tp_index * slots * page_len + jnp.arange(slots * page_len, dtype=jnp.int32)
    valid = (places.reshape(1, slots, page_len) < lengths[:, None, None])[:, None]
    same = page_table[:, None, :] == jnp.arange(pages, dtype=jnp.int32)[None, :, None]
    count = jnp.sum(jnp.where(valid & same[..., None], 1.0, 0.0), axis=2)
    by_token = cache_pool.reshape(pages * page_len, -1)
    by_head = decode_query.reshape(rows, QHEADS, HEADDIM)
    count = count.reshape(rows, pages * page_len)

    def cached(after=()):
        part, mark = cache_attention(flag, by_head, by_token, count, after)
        part = part[None]
        if tp_count == 2:
            return (part, lax.ppermute(part, "tp", [(0, 1), (1, 0)])), mark
        return (lax.all_gather(part, "tp", axis=0, tiled=True),), mark

    def combined(parts, after=()):
        if tp_count == 2:
            here, there = parts
            parts = jnp.where(tp_index == 0, here, there), jnp.where(tp_index == 0, there, here)
        out, mark = combine_parts(flag, parts, rows, after)
        return out.reshape(rows, QHEADS * HEADDIM), mark

    heads = GROUP // 2
    steps = prompt_query.shape[1] // (heads * HEADDIM)
    kv_here = prompt_pairs.shape[1] // (2 * HEADDIM)
    width = kv_here * GROUP * HEADDIM
    from_inst = lax.dynamic_index_in_dim(source, lax.rem(inst, half), 0, False)
    target = lax.dynamic_index_in_dim(assignment, lax.rem(inst, half), 0, False)

    def fresh_of(queries, after=()):
        mine = lax.dynamic_index_in_dim(queries.reshape(half, -1), target, 0, True)
        mine = lax.dynamic_slice(mine, (0, tp_index * width), (1, width))
        fresh = fresh_attention(mine.reshape(kv_here, GROUP, HEADDIM), prompt_pairs, after)
        return lax.ppermute(fresh, "inst", [(i, i + half) for i in range(half)])

    def prompt_part(first, last, earlier, after=()):
        return prompt_attention(
            flag, prompt_query, prompt_pairs, first, last - first, heads, earlier, after
        )

    row_units = prompt_pairs.shape[0] // (2 * UNIT)
    if inst_count == 4 * PAIRS and tp_count == 2 and row_units == 5 * half and steps == 8:
        cuts = (0, 5, 8)
        handed, results, prefill_out, decode_out = two_way_handoff(
            prompt_pairs,
            source,
            flag,
            assignment[0] >= 0,
            arrival_query,
            fresh_of,
            lambda n, earlier, after: prompt_part(cuts[n], cuts[n + 1], earlier, after),
            (cached, combined),
        )
        part = lax.dynamic_index_in_dim(results, from_inst, 1, False)
        part = part[:, :, : kv_here * HEADDIM].reshape(tp_count, GROUP, kv_here, HEADDIM)
        arrival_out = part.transpose(0, 2, 1, 3).reshape(1, QHEADS * HEADDIM)
    else:
        handed = relay_handoff(prompt_pairs, source, inst_count)
        sent = lax.ppermute(arrival_query, "inst", [(i + half, i) for i in range(half)])
        every = lax.all_gather(sent, "inst", axis=0, tiled=True, axis_index_groups=groups)
        results = lax.all_gather(fresh_of(every), "inst", axis_index_groups=groups)
        part = lax.dynamic_index_in_dim(results, from_inst, 0, True)
        part = part[:, :, : kv_here * HEADDIM].reshape(1, GROUP, kv_here, HEADDIM)
        part = part.transpose(0, 2, 1, 3).reshape(1, width)
        arrival_out = lax.all_gather(part, "tp", axis=1, tiled=True)
        prefill_out, _ = prompt_part(0, steps, None)
        decode_out, _ = combined(cached()[0])
    arrival_out = jnp.where(is_prefill, jnp.zeros_like(arrival_out), arrival_out)
    return (prefill_out, handed, decode_out, arrival_out)


def solution(mesh):
    return jax.shard_map(
        shards,
        mesh=mesh,
        in_specs=(
            P("inst", "tp"),
            P("inst", "tp"),
            P("inst", None),
            P("inst", None),
            P(("inst", "tp"), None, None),
            P("inst", "tp"),
            P("inst"),
            P(),
        ),
        out_specs=(P("inst", "tp"), P(("inst", "tp"), None), P("inst", None), P("inst", None)),
        check_vma=False,
    )
```

```python
import functools

import jax
import jax.numpy as jnp
from jax import lax
from jax.experimental import pallas as pl
from jax.experimental.pallas import tpu as pltpu
from jax.sharding import PartitionSpec as P

QHEADS = 64
KVHEADS = 8
HEADDIM = 128
GROUP = QHEADS // KVHEADS
SCALE = HEADDIM ** (-0.5)
LOG2E = 1.4426950408889634
NEG_FILL = -1e30
TILE = 128
VMEM = 24 * 1024 * 1024
SMALL = 1024 * 1024
MEDIUM = 8 * 1024 * 1024
LARGE = 57 * 1024 * 1024
COST = pl.CostEstimate(flops=1, bytes_accessed=1, transcendentals=0)


def dot_t(a, b):
    return lax.dot_general(a, b, (((1,), (1,)), ((), ())), preferred_element_type=jnp.float32)


def dot(a, b):
    return lax.dot_general(a, b, (((1,), (0,)), ((), ())), preferred_element_type=jnp.float32)


def prompt_kernel(heads, flag_ref, q_ref, kv_ref, *rest):
    out_ref = rest[-2]
    length = q_ref.shape[0]

    @pl.when(flag_ref[0] == 0)
    def _():
        out_ref[...] = jnp.zeros_like(out_ref)

    @pl.when(flag_ref[0] != 0)
    def _():
        rows_all = lax.broadcasted_iota(jnp.int32, (TILE, TILE), 0)
        cols_all = lax.broadcasted_iota(jnp.int32, (TILE, TILE), 1)
        below = jnp.concatenate([rows_all >= cols_all] * heads, axis=0)
        ones = jnp.ones((length, HEADDIM), jnp.bfloat16)
        values = jnp.concatenate([kv_ref[:, HEADDIM:], ones], axis=1)
        for start in range(0, length, TILE):
            stop = start + TILE
            queries = jnp.concatenate(
                [q_ref[start:stop, h * HEADDIM : (h + 1) * HEADDIM] for h in range(heads)], axis=0
            )
            scores = dot_t(queries, kv_ref[:stop, :HEADDIM])
            last = jnp.where(below, scores[:, start:], NEG_FILL)
            scores = jnp.concatenate([scores[:, :start], last], axis=1) if start else last
            peak = jnp.max(scores, axis=1, keepdims=True)
            weights = jnp.exp2((scores - peak) * (SCALE * LOG2E)).astype(jnp.bfloat16)
            mixed = dot(weights, values[:stop])
            result = (mixed[:, :HEADDIM] / mixed[:, HEADDIM:]).astype(jnp.bfloat16)
            for h in range(heads):
                out_ref[start:stop, h * HEADDIM : (h + 1) * HEADDIM] = result[
                    h * TILE : (h + 1) * TILE
                ]


MARK = jax.ShapeDtypeStruct((8, 128), jnp.float32)
IN_HBM = pl.BlockSpec(memory_space=pltpu.HBM)
ANYWHERE = pl.BlockSpec(memory_space=pl.ANY)
IN_VMEM = pl.BlockSpec(memory_space=pltpu.VMEM)


def prompt_attention(flag, queries, pairs, first, steps, heads, earlier, after):
    length, width = queries.shape
    per_kv = GROUP // heads

    def q_map(i, flag_ref):
        return (0, jnp.where(flag_ref[0] != 0, i + first, 0))

    def kv_map(i, flag_ref):
        return (0, jnp.where(flag_ref[0] != 0, (i + first) // per_kv, 0))

    in_specs = [
        pl.BlockSpec((length, heads * HEADDIM), q_map),
        pl.BlockSpec((length, 2 * HEADDIM), kv_map),
    ]
    operands = [flag, queries, pairs]
    aliases = {}
    if earlier is not None:
        in_specs.append(ANYWHERE)
        operands.append(earlier)
        aliases = {3: 0}
    return pl.pallas_call(
        functools.partial(prompt_kernel, heads),
        out_shape=(jax.ShapeDtypeStruct((length, width), jnp.bfloat16), MARK),
        grid_spec=pltpu.PrefetchScalarGridSpec(
            num_scalar_prefetch=1,
            grid=(steps,),
            in_specs=in_specs + [IN_HBM] * len(after),
            out_specs=(
                pl.BlockSpec((length, heads * HEADDIM), lambda i, flag_ref: (0, i + first)),
                IN_HBM,
            ),
        ),
        input_output_aliases=aliases,
        compiler_params=pltpu.CompilerParams(vmem_limit_bytes=LARGE),
        cost_estimate=COST,
        name="prompt_attention",
    )(*operands, *after)


def cache_kernel(page_len, info_ref, table_ref, lengths_ref, q_ref, kv_ref, *rest):
    out_ref, _, count_ref = rest[-3:]
    rows, slots = table_ref.shape

    @pl.when(info_ref[0] != 0)
    def _():
        out_ref[...] = jnp.zeros_like(out_ref)

    @pl.when(jnp.logical_and(info_ref[0] == 0, pl.program_id(0) == 0))
    def _():
        token = lax.broadcasted_iota(jnp.int32, (GROUP, count_ref.shape[1]), 1)
        page, offset = token // page_len, token % page_len
        for r in range(rows):
            count = jnp.zeros(token.shape, jnp.float32)
            for slot in range(slots):
                left = lengths_ref[r] - (info_ref[1] * slots + slot) * page_len
                valid = jnp.logical_and(page == table_ref[r, slot], offset < left)
                count = count + jnp.where(valid, 1.0, 0.0)
            count_ref[r * GROUP : (r + 1) * GROUP] = count

    @pl.when(info_ref[0] == 0)
    def _():
        count = count_ref[...]
        here = count > 0.0
        queries = q_ref[...].astype(jnp.float32).reshape(rows * GROUP, HEADDIM)
        scores = dot_t(queries.astype(jnp.bfloat16), kv_ref[:, :HEADDIM]) * SCALE
        scores = jnp.where(here, scores, NEG_FILL)
        peak = jnp.max(scores, axis=1, keepdims=True)
        weights = jnp.where(here, jnp.exp(scores - peak), 0.0)
        total = jnp.sum(weights * count, axis=1, keepdims=True)
        rounded = weights.astype(jnp.bfloat16).astype(jnp.float32) * count
        out_ref[0, :, :HEADDIM] = dot(rounded.astype(jnp.bfloat16), kv_ref[:, HEADDIM:])
        lane = lax.broadcasted_iota(jnp.int32, (rows * GROUP, HEADDIM), 1)
        out_ref[0, :, HEADDIM:] = jnp.where(lane < HEADDIM // 2, peak, total)


def cache_attention(info, table, lengths, queries, pool, page_len, after):
    rows = queries.shape[0]
    tokens = pool.shape[0]
    return pl.pallas_call(
        functools.partial(cache_kernel, page_len),
        out_shape=(
            jax.ShapeDtypeStruct((KVHEADS, rows * GROUP, 2 * HEADDIM), jnp.float32),
            MARK,
        ),
        grid_spec=pltpu.PrefetchScalarGridSpec(
            num_scalar_prefetch=3,
            grid=(KVHEADS,),
            in_specs=[
                pl.BlockSpec((rows, GROUP, HEADDIM), lambda h, *_: (0, h, 0)),
                pl.BlockSpec((tokens, 2 * HEADDIM), lambda h, info, *_: (0, h * (1 - info[0]))),
            ]
            + [IN_HBM] * len(after),
            out_specs=(
                pl.BlockSpec((1, rows * GROUP, 2 * HEADDIM), lambda h, *_: (h, 0, 0)),
                IN_HBM,
            ),
            scratch_shapes=[pltpu.VMEM((rows * GROUP, tokens), jnp.float32)],
        ),
        compiler_params=pltpu.CompilerParams(vmem_limit_bytes=VMEM),
        cost_estimate=COST,
        name="cache_attention",
    )(info, table, lengths, queries, pool, *after)


def combine_kernel(count, flag_ref, *refs):
    part_refs, out_ref = refs[:count], refs[-2]

    @pl.when(flag_ref[0] != 0)
    def _():
        out_ref[...] = jnp.zeros_like(out_ref)

    @pl.when(flag_ref[0] == 0)
    def _():
        parts = [ref[n] for ref in part_refs for n in range(ref.shape[0])]
        peaks = [part[:, HEADDIM : HEADDIM + 1] for part in parts]
        peak = functools.reduce(jnp.maximum, peaks)
        factors = [jnp.exp(p - peak) for p in peaks]
        total = sum(part[:, -1:] * f for part, f in zip(parts, factors))
        mixed = sum(part[:, :HEADDIM] * f for part, f in zip(parts, factors))
        out_ref[...] = (mixed / total).reshape(out_ref.shape).astype(jnp.bfloat16)


def combine_parts(flag, parts, rows, after):
    return pl.pallas_call(
        functools.partial(combine_kernel, len(parts)),
        out_shape=(jax.ShapeDtypeStruct((rows, QHEADS, HEADDIM), jnp.bfloat16), MARK),
        grid_spec=pltpu.PrefetchScalarGridSpec(
            num_scalar_prefetch=1,
            grid=(KVHEADS,),
            in_specs=[
                pl.BlockSpec(
                    (part.shape[0], None, rows * GROUP, 2 * HEADDIM),
                    lambda h, flag_ref: (0, h, 0, 0),
                )
                for part in parts
            ]
            + [IN_HBM] * len(after),
            out_specs=(
                pl.BlockSpec((rows, GROUP, HEADDIM), lambda h, flag_ref: (0, h, 0)),
                IN_HBM,
            ),
        ),
        compiler_params=pltpu.CompilerParams(vmem_limit_bytes=VMEM),
        cost_estimate=COST,
        name="combine_parts",
    )(flag, *parts, *after)


def fresh_kernel(info_ref, q_ref, kv_ref, *rest):
    out_ref = rest[-1]
    units = q_ref[...].astype(jnp.float32)
    row = lax.broadcasted_iota(jnp.int32, units.shape, 0)
    mine = jnp.where(row == info_ref[1] + pl.program_id(0), units, 0.0)
    mine = jnp.sum(mine, axis=0, keepdims=True)
    queries = jnp.concatenate(
        [mine[:, g * HEADDIM : (g + 1) * HEADDIM] for g in range(GROUP)], axis=0
    )
    scores = dot_t(queries.astype(jnp.bfloat16), kv_ref[:, :HEADDIM]) * SCALE
    peak = jnp.max(scores, axis=1, keepdims=True)
    weights = jnp.exp(scores - peak)
    total = jnp.sum(weights, axis=1, keepdims=True)
    mixed = dot(weights.astype(jnp.bfloat16), kv_ref[:, HEADDIM:])
    out_ref[:, :HEADDIM] = (mixed / total).astype(jnp.bfloat16)
    out_ref[:, HEADDIM:] = jnp.zeros_like(mixed).astype(jnp.bfloat16)


def fresh_attention(info, queries, pairs, after=()):
    length, width = pairs.shape
    unit = (None, None) + queries.shape[2:]
    return pl.pallas_call(
        fresh_kernel,
        out_shape=jax.ShapeDtypeStruct((GROUP, width), jnp.bfloat16),
        grid_spec=pltpu.PrefetchScalarGridSpec(
            num_scalar_prefetch=1,
            grid=(width // (2 * HEADDIM),),
            in_specs=[
                pl.BlockSpec(unit, lambda h, info_ref: (info_ref[0], info_ref[2], 0, 0)),
                pl.BlockSpec((length, 2 * HEADDIM), lambda h, info_ref: (0, h)),
            ]
            + [IN_HBM] * len(after),
            out_specs=pl.BlockSpec((GROUP, 2 * HEADDIM), lambda h, info_ref: (0, h)),
        ),
        compiler_params=pltpu.CompilerParams(vmem_limit_bytes=VMEM),
        cost_estimate=COST,
        name="fresh_attention",
    )(info, queries, pairs, *after)


def results_kernel(info_ref, unit_ref, out_ref):
    heads = out_ref.shape[0] // GROUP
    for h in range(heads):
        result = unit_ref[:, 2 * h * HEADDIM : (2 * h + 1) * HEADDIM].astype(jnp.float32)
        result = jnp.where(info_ref[1] != 0, 0.0, result)
        out_ref[h * GROUP : (h + 1) * GROUP] = result


def arrival_results(info, slots):
    devices, _, units, _, width = slots.shape
    heads = width // (2 * HEADDIM)
    return pl.pallas_call(
        results_kernel,
        out_shape=jax.ShapeDtypeStruct((QHEADS, HEADDIM), jnp.float32),
        grid_spec=pltpu.PrefetchScalarGridSpec(
            num_scalar_prefetch=1,
            grid=(devices,),
            in_specs=[
                pl.BlockSpec(
                    (None, None, None, GROUP, width),
                    lambda t, info_ref: (t, info_ref[0], units - 1, 0, 0),
                )
            ],
            out_specs=pl.BlockSpec((heads * GROUP, HEADDIM), lambda t, info_ref: (t, 0)),
        ),
        compiler_params=pltpu.CompilerParams(vmem_limit_bytes=SMALL),
        cost_estimate=COST,
        name="arrival_results",
    )(info, slots)


def relay_handoff(pairs, source, inst_count):
    half = inst_count // 2
    moved = lax.all_to_all(pairs, "tp", split_axis=0, concat_axis=1, tiled=True)
    lanes = 1024 if moved.size % (inst_count * 1024) == 0 else HEADDIM
    pieces = moved.reshape(inst_count, -1, lanes)
    spread = lax.all_to_all(pieces, "inst", split_axis=0, concat_axis=0, tiled=True)
    chosen = jnp.stack(
        [lax.dynamic_index_in_dim(spread, source[d], 0, False) for d in range(half)], axis=0
    )
    outgoing = jnp.concatenate([jnp.zeros_like(chosen), chosen], axis=0)
    delivered = lax.all_to_all(outgoing, "inst", split_axis=0, concat_axis=0, tiled=True)
    return delivered.reshape(moved.shape)


UNIT = 8
PAIRS = 4
PREFILL, DECODE = 1, 0


def copy_kernel(plan, side, counts, prefetch_ref, *refs):
    inputs, marks, outputs = counts
    sources, targets, sems = refs[:inputs], refs[inputs + marks : inputs + marks + outputs], refs[-1]

    @pl.when(prefetch_ref[2] == side)
    def _():
        started = []
        for source, target in plan(prefetch_ref, sources, targets):
            started.append(pltpu.make_async_copy(source, target, sems.at[len(started)]))
        for copy in started:
            copy.start()
        for copy in started:
            copy.wait()


def copies(plan, number, prefetch, operands, shapes, name, after=(), inside=True, side=PREFILL):
    place = IN_VMEM if inside else ANYWHERE
    return pl.pallas_call(
        functools.partial(copy_kernel, plan, side, (len(operands), len(after), len(shapes))),
        out_shape=tuple(jax.ShapeDtypeStruct(shape, jnp.bfloat16) for shape in shapes) + (MARK,),
        grid_spec=pltpu.PrefetchScalarGridSpec(
            num_scalar_prefetch=1,
            grid=(1,),
            in_specs=[place] * len(operands) + [IN_HBM] * len(after),
            out_specs=tuple([ANYWHERE] * len(shapes)) + (IN_HBM,),
            scratch_shapes=[pltpu.SemaphoreType.DMA((number,))],
        ),
        compiler_params=pltpu.CompilerParams(vmem_limit_bytes=MEDIUM if inside else SMALL),
        cost_estimate=COST,
        name=name,
    )(prefetch, *operands, *after)


def relay_slots_kernel(far, prefetch_ref, keep_ref, recv_ref, fresh_ref, out_ref, mark_ref, sems, fresh_sems):
    half = 2 * PAIRS

    @pl.when(prefetch_ref[2] == DECODE)
    def _():
        waits = []
        for d in range(half):
            pair = lax.div(prefetch_ref[3 + d], 2)
            same = lax.rem(prefetch_ref[3 + d], 2) == prefetch_ref[1]
            shift = lax.rem(prefetch_ref[0] + PAIRS - pair, PAIRS)
            for tau in range(2):
                slot = tau * half + d
                target = out_ref.at[slot, pl.ds(0, far)]
                mine = pltpu.make_async_copy(keep_ref.at[shift, tau], target, sems.at[slot])
                other = pltpu.make_async_copy(recv_ref.at[shift, tau], target, sems.at[slot])
                pl.when(same)(mine.start)
                pl.when(jnp.logical_not(same))(other.start)
                extra = pltpu.make_async_copy(fresh_ref, out_ref.at[slot, far], fresh_sems.at[slot])
                extra.start()
                waits += [mine, extra]
        for copy in waits:
            copy.wait()


def rows_kernel(near, far, prefetch_ref, slots_ref, *refs):
    *parts, out_ref, zero_ref, sems = refs
    half = 2 * PAIRS
    width = slots_ref.shape[-1]
    near_all = near * half

    @pl.when(prefetch_ref[2] == 0)
    def _():
        waits = []
        for t in range(2):
            columns = pl.ds(t * width, width)
            for s, part in enumerate(parts):
                pair = lax.rem(prefetch_ref[0] + PAIRS - s, PAIRS)
                target = out_ref.at[pl.ds(pair * 2 * near, 2 * near), :, columns]
                waits.append(pltpu.make_async_copy(part.at[t], target, sems.at[len(waits)]))
            for i in range(half):
                source = slots_ref.at[t * half + i, pl.ds(0, far)]
                target = out_ref.at[pl.ds(near_all + i * far, far), :, columns]
                waits.append(pltpu.make_async_copy(source, target, sems.at[len(waits)]))
        for copy in waits:
            copy.start()
        for copy in waits:
            copy.wait()

    @pl.when(prefetch_ref[2] != 0)
    def _():
        zero_ref[...] = jnp.zeros_like(zero_ref)
        size = zero_ref.shape[0]
        waits = []
        for n in range(out_ref.shape[0] // size):
            target = out_ref.at[pl.ds(n * size, size)]
            waits.append(pltpu.make_async_copy(zero_ref, target, sems.at[n]))
        for copy in waits:
            copy.start()
        for copy in waits:
            copy.wait()


def two_way_handoff(pairs, source, flag, always, arrival_query, fresh_of, results_of, prompt_part, extra):
    half = 2 * PAIRS
    rows, width = pairs.shape
    units = rows // (2 * UNIT)
    far_all = -(-units * 3 // (5 * half)) * half
    near_all = units - far_all
    near, far = near_all // half, far_all // half
    inst = lax.axis_index("inst")
    pair, side = lax.div(lax.rem(inst, half), 2), lax.rem(inst, 2)
    prefetch = jnp.concatenate([jnp.stack([pair, side, flag[0]]), source])
    block = (UNIT, width)
    by_unit = pairs.reshape((rows // UNIT,) + block)
    groups = [[base + 2 * i + tau for tau in range(2) for i in range(half)] for base in (0, 2 * half)]

    def crossing(array, s):
        hops = [
            (2 * p + k, half + 2 * ((p + s) % PAIRS) + k) for p in range(PAIRS) for k in range(2)
        ]
        return lax.ppermute(array, "inst", hops + [(there, here) for here, there in hops])

    def beside(array, base):
        return lax.ppermute(array, "inst", [(base + i, base + (i ^ 1)) for i in range(half)])

    def spread_out(array):
        return lax.all_to_all(
            array, ("inst", "tp"), 0, 0, axis_index_groups=groups, tiled=True
        )

    def cut(pre, sources, targets):
        plan = []
        for s in range(PAIRS):
            start = near_all + lax.rem(pre[0] + s, PAIRS) * (2 * far)
            for tau in range(2):
                plan.append((sources[0].at[pl.ds(tau * units + start, 2 * far)], targets[s].at[tau]))
        return plan

    def near_slots(pre, sources, targets):
        plan = []
        for tau in range(2):
            for i in range(half):
                slot = tau * half + i
                rows_here = sources[0].at[pl.ds(tau * units + i * near, near)]
                plan.append((rows_here, targets[0].at[slot, pl.ds(0, near)]))
                plan.append((sources[1], targets[0].at[slot, near]))
        return plan

    def for_neighbour(pre, sources, targets):
        plan = []
        for s in range(PAIRS):
            receiver = lax.rem(pre[0] + s, PAIRS) * 2 + 1 - pre[1]
            for t in range(2):
                origin = t * half + pre[3 + receiver]
                plan.append((sources[0].at[origin, pl.ds(0, near)], targets[0].at[s, t]))
        return plan

    def for_receivers(pre, sources, targets):
        plan = []
        for s in range(PAIRS):
            receiver = lax.rem(pre[0] + s, PAIRS) * 2 + pre[1]
            for t in range(2):
                origin = t * half + pre[3 + receiver]
                mine = targets[s].at[t, pl.ds(pre[1] * near, near)]
                other = targets[s].at[t, pl.ds((1 - pre[1]) * near, near)]
                plan.append((sources[0].at[origin, pl.ds(0, near)], mine))
                plan.append((sources[1].at[s, t], other))
        return plan

    def split(pre, sources, targets):
        plan = []
        for s in range(PAIRS):
            for tau in range(2):
                mine = sources[s].at[tau, pl.ds(pre[1] * far, far)]
                other = sources[s].at[tau, pl.ds((1 - pre[1]) * far, far)]
                plan.append((mine, targets[0].at[s, tau]))
                plan.append((other, targets[1].at[s, tau]))
        return plan

    near_shape = (2, 2 * near) + block

    def first_stage(by_unit, asked):
        spread, mark = copies(
            near_slots,
            8 * PAIRS,
            prefetch,
            [by_unit, asked.reshape(block)],
            [(2 * half, near + 1) + block],
            "near_slots",
        )
        spread = spread_out(spread)
        part, mark = extra[0]([mark])
        prompt, mark = prompt_part(0, None, [mark])
        more, mark = extra[1](part, [mark])
        outgoing, mark = copies(
            for_neighbour,
            2 * PAIRS,
            prefetch,
            [spread],
            [(PAIRS, 2, near) + block],
            "for_neighbour",
            [mark],
        )
        incoming = beside(outgoing, 0)
        *near_parts, mark = copies(
            for_receivers, 4 * PAIRS, prefetch, [spread, incoming], [near_shape] * PAIRS, "for_receivers"
        )
        return *near_parts, prompt, spread, more

    def second_stage(prompt, spread, *far_here):
        fresh = fresh_of(spread, near)
        keep, give, mark = copies(
            split, 4 * PAIRS, prefetch, list(far_here), [(PAIRS, 2, far) + block] * 2, "split_relays", [fresh], side=DECODE
        )
        taken = beside(give, half)
        slots, mark = pl.pallas_call(
            functools.partial(relay_slots_kernel, far),
            out_shape=(jax.ShapeDtypeStruct((2 * half, far + 1) + block, jnp.bfloat16), MARK),
            grid_spec=pltpu.PrefetchScalarGridSpec(
                num_scalar_prefetch=1,
                grid=(1,),
                in_specs=[IN_VMEM] * 3,
                out_specs=(ANYWHERE, IN_HBM),
                scratch_shapes=[pltpu.SemaphoreType.DMA((2 * half,))] * 2,
            ),
            compiler_params=pltpu.CompilerParams(vmem_limit_bytes=MEDIUM),
            cost_estimate=COST,
            name="relay_slots",
        )(prefetch, keep, taken, fresh)
        slots = spread_out(slots)
        prompt, mark = prompt_part(1, prompt, [mark])
        return prompt, slots, results_of(slots.reshape((2, half, far + 1) + block))

    def staged(stage, *operands):
        def never(*operands):
            outs = [jnp.zeros(out.shape, out.dtype) for out in jax.eval_shape(stage, *operands)]
            return tuple(outs) if stage is first_stage else (operands[0], *outs[1:])

        return lax.cond(always, lambda *operands: tuple(stage(*operands)), never, *operands)

    asked = lax.ppermute(arrival_query, "inst", [(i + half, i) for i in range(half)])
    *far_parts, _ = copies(
        cut, 2 * PAIRS, prefetch, [by_unit], [(2, 2 * far) + block] * PAIRS, "cut_far", inside=False
    )
    far_here = [crossing(part, s) for s, part in enumerate(far_parts)]
    *near_parts, prompt, spread, more = staged(first_stage, by_unit, asked)
    near_here = [crossing(part, s) for s, part in enumerate(near_parts)]
    prompt, slots, results = staged(second_stage, prompt, spread, *far_here)
    handed = pl.pallas_call(
        functools.partial(rows_kernel, near, far),
        out_shape=jax.ShapeDtypeStruct((units, UNIT, 2 * width), jnp.bfloat16),
        grid_spec=pltpu.PrefetchScalarGridSpec(
            num_scalar_prefetch=1,
            grid=(1,),
            in_specs=[IN_VMEM] * (PAIRS + 1),
            out_specs=ANYWHERE,
            scratch_shapes=[
                pltpu.VMEM((half, UNIT, 2 * width), jnp.bfloat16),
                pltpu.SemaphoreType.DMA((2 * (half + PAIRS),)),
            ],
        ),
        compiler_params=pltpu.CompilerParams(vmem_limit_bytes=MEDIUM),
        cost_estimate=COST,
        name="rows",
    )(prefetch, slots, *near_here)
    return handed.reshape(rows // 2, 2 * width), results, prompt, more


def shards(
    prompt_query,
    prompt_pairs,
    decode_query,
    arrival_query,
    cache_pool,
    page_table,
    lengths,
    assignment,
):
    inst_count = lax.axis_size("inst")
    tp_count = lax.axis_size("tp")
    half = inst_count // 2
    inst = lax.axis_index("inst")
    tp_index = lax.axis_index("tp")
    is_prefill = inst < half
    flag = is_prefill.astype(jnp.int32).reshape(1)
    groups = [list(range(half)), list(range(half, inst_count))]
    decode_ids = jnp.arange(half, dtype=jnp.int32)
    matches = assignment[None, :] == decode_ids[:, None]
    source = jnp.sum(jnp.where(matches, decode_ids[None, :], 0), axis=1).astype(jnp.int32)
    rows = decode_query.shape[0]
    pages, page_len = cache_pool.shape[0], cache_pool.shape[1]
    by_token = cache_pool.reshape(pages * page_len, -1)
    by_head = decode_query.reshape(rows, QHEADS, HEADDIM)
    info = jnp.stack([flag[0], tp_index])

    def cached(after=()):
        part, mark = cache_attention(info, page_table, lengths, by_head, by_token, page_len, after)
        part = part[None]
        if tp_count == 2:
            return (part, lax.ppermute(part, "tp", [(0, 1), (1, 0)])), mark
        return (lax.all_gather(part, "tp", axis=0, tiled=True),), mark

    def combined(parts, after=()):
        if tp_count == 2:
            here, there = parts
            parts = jnp.where(tp_index == 0, here, there), jnp.where(tp_index == 0, there, here)
        out, mark = combine_parts(flag, parts, rows, after)
        return out.reshape(rows, QHEADS * HEADDIM), mark

    heads = GROUP // 2
    steps = prompt_query.shape[1] // (heads * HEADDIM)
    kv_here = prompt_pairs.shape[1] // (2 * HEADDIM)
    width = kv_here * GROUP * HEADDIM
    from_inst = lax.dynamic_index_in_dim(source, lax.rem(inst, half), 0, False)
    target = lax.dynamic_index_in_dim(assignment, lax.rem(inst, half), 0, False)

    def fresh_of(queries, unit):
        info = jnp.stack([target, tp_index * kv_here, jnp.int32(unit)])
        fresh = fresh_attention(info, queries, prompt_pairs)
        return lax.ppermute(fresh, "inst", [(i, i + half) for i in range(half)])

    def results_of(slots):
        found = arrival_results(jnp.stack([from_inst, flag[0]]), slots)
        return found.astype(jnp.bfloat16).reshape(1, QHEADS * HEADDIM)

    def prompt_part(first, last, earlier, after=()):
        return prompt_attention(
            flag, prompt_query, prompt_pairs, first, last - first, heads, earlier, after
        )

    row_units = prompt_pairs.shape[0] // (2 * UNIT)
    if inst_count == 4 * PAIRS and tp_count == 2 and row_units == 5 * half and steps == 8:
        cuts = (0, 3, 8)
        handed, arrival_out, prefill_out, decode_out = two_way_handoff(
            prompt_pairs,
            source,
            flag,
            assignment[0] >= 0,
            arrival_query,
            fresh_of,
            results_of,
            lambda n, earlier, after: prompt_part(cuts[n], cuts[n + 1], earlier, after),
            (cached, combined),
        )
    else:
        handed = relay_handoff(prompt_pairs, source, inst_count)
        sent = lax.ppermute(arrival_query, "inst", [(i + half, i) for i in range(half)])
        every = lax.all_gather(sent, "inst", axis=0, tiled=True, axis_index_groups=groups)
        fresh = fresh_of(every.reshape(half, 1, KVHEADS, GROUP * HEADDIM), 0)
        results = lax.all_gather(fresh, "inst", axis_index_groups=groups)
        arrival_out = results_of(lax.all_gather(results, "tp")[:, :, None])
        prefill_out, _ = prompt_part(0, steps, None)
        decode_out, _ = combined(cached()[0])
    return (prefill_out, handed, decode_out, arrival_out)


def solution(mesh):
    return jax.shard_map(
        shards,
        mesh=mesh,
        in_specs=(
            P("inst", "tp"),
            P("inst", "tp"),
            P("inst", None),
            P("inst", None),
            P(("inst", "tp"), None, None),
            P("inst", "tp"),
            P("inst"),
            P(),
        ),
        out_specs=(P("inst", "tp"), P(("inst", "tp"), None), P("inst", None), P("inst", None)),
        check_vma=False,
    )
```

```python
import functools

import jax
import jax.numpy as jnp
from jax import lax
from jax.experimental import pallas as pl
from jax.experimental.pallas import tpu as pltpu
from jax.sharding import PartitionSpec as P

QHEADS = 64
KVHEADS = 8
HEADDIM = 128
GROUP = QHEADS // KVHEADS
SCALE = HEADDIM ** (-0.5)
LOG2E = 1.4426950408889634
NEG_FILL = -1e30
TILE = 128
VMEM = 24 * 1024 * 1024
SMALL = 1024 * 1024
MEDIUM = 8 * 1024 * 1024
LARGE = 57 * 1024 * 1024
COST = pl.CostEstimate(flops=1, bytes_accessed=1, transcendentals=0)


INST, TP, FIRST = 0, 1, 2


def on_prefill(info):
    return info[INST] < info.shape[0] - FIRST


def order(info):
    half = info.shape[0] - FIRST
    return info[INST] - jnp.where(on_prefill(info), 0, half)


def source_of(info, receiver):
    half = info.shape[0] - FIRST
    found = jnp.int32(0)
    for p in range(half):
        found = jnp.where(info[FIRST + p] == receiver, p, found)
    return found


def dot_t(a, b):
    return lax.dot_general(a, b, (((1,), (1,)), ((), ())), preferred_element_type=jnp.float32)


def dot(a, b):
    return lax.dot_general(a, b, (((1,), (0,)), ((), ())), preferred_element_type=jnp.float32)


def prompt_kernel(heads, info_ref, q_ref, kv_ref, *rest):
    out_ref = rest[-2]
    length = q_ref.shape[0]

    @pl.when(jnp.logical_not(on_prefill(info_ref)))
    def _():
        out_ref[...] = jnp.zeros_like(out_ref)

    @pl.when(on_prefill(info_ref))
    def _():
        rows_all = lax.broadcasted_iota(jnp.int32, (TILE, TILE), 0)
        cols_all = lax.broadcasted_iota(jnp.int32, (TILE, TILE), 1)
        below = jnp.concatenate([rows_all >= cols_all] * heads, axis=0)
        ones = jnp.ones((length, HEADDIM), jnp.bfloat16)
        values = jnp.concatenate([kv_ref[:, HEADDIM:], ones], axis=1)
        for start in range(0, length, TILE):
            stop = start + TILE
            queries = jnp.concatenate(
                [q_ref[start:stop, h * HEADDIM : (h + 1) * HEADDIM] for h in range(heads)], axis=0
            )
            scores = dot_t(queries, kv_ref[:stop, :HEADDIM])
            last = jnp.where(below, scores[:, start:], NEG_FILL)
            scores = jnp.concatenate([scores[:, :start], last], axis=1) if start else last
            peak = jnp.max(scores, axis=1, keepdims=True)
            weights = jnp.exp2((scores - peak) * (SCALE * LOG2E)).astype(jnp.bfloat16)
            mixed = dot(weights, values[:stop])
            result = (mixed[:, :HEADDIM] / mixed[:, HEADDIM:]).astype(jnp.bfloat16)
            for h in range(heads):
                out_ref[start:stop, h * HEADDIM : (h + 1) * HEADDIM] = result[
                    h * TILE : (h + 1) * TILE
                ]


MARK = jax.ShapeDtypeStruct((8, 128), jnp.float32)
IN_HBM = pl.BlockSpec(memory_space=pltpu.HBM)
ANYWHERE = pl.BlockSpec(memory_space=pl.ANY)
IN_VMEM = pl.BlockSpec(memory_space=pltpu.VMEM)


def prompt_attention(info, queries, pairs, first, steps, heads, earlier, after):
    length, width = queries.shape
    per_kv = GROUP // heads

    def q_map(i, info_ref):
        return (0, jnp.where(on_prefill(info_ref), i + first, 0))

    def kv_map(i, info_ref):
        return (0, jnp.where(on_prefill(info_ref), (i + first) // per_kv, 0))

    in_specs = [
        pl.BlockSpec((length, heads * HEADDIM), q_map),
        pl.BlockSpec((length, 2 * HEADDIM), kv_map),
    ]
    operands = [info, queries, pairs]
    aliases = {}
    if earlier is not None:
        in_specs.append(ANYWHERE)
        operands.append(earlier)
        aliases = {3: 0}
    return pl.pallas_call(
        functools.partial(prompt_kernel, heads),
        out_shape=(jax.ShapeDtypeStruct((length, width), jnp.bfloat16), MARK),
        grid_spec=pltpu.PrefetchScalarGridSpec(
            num_scalar_prefetch=1,
            grid=(steps,),
            in_specs=in_specs + [IN_HBM] * len(after),
            out_specs=(
                pl.BlockSpec((length, heads * HEADDIM), lambda i, info_ref: (0, i + first)),
                IN_HBM,
            ),
        ),
        input_output_aliases=aliases,
        compiler_params=pltpu.CompilerParams(vmem_limit_bytes=LARGE),
        cost_estimate=COST,
        name="prompt_attention",
    )(*operands, *after)


def cache_kernel(page_len, info_ref, table_ref, lengths_ref, q_ref, kv_ref, *rest):
    out_ref, _, count_ref = rest[-3:]
    rows, slots = table_ref.shape

    @pl.when(jnp.logical_and(on_prefill(info_ref), pl.program_id(0) == 0))
    def _():
        out_ref[...] = jnp.zeros_like(out_ref)

    @pl.when(jnp.logical_and(jnp.logical_not(on_prefill(info_ref)), pl.program_id(0) == 0))
    def _():
        token = lax.broadcasted_iota(jnp.int32, (GROUP, count_ref.shape[1]), 1)
        page, offset = token // page_len, token % page_len
        for r in range(rows):
            count = jnp.zeros(token.shape, jnp.float32)
            for slot in range(slots):
                left = lengths_ref[r] - (info_ref[TP] * slots + slot) * page_len
                valid = jnp.logical_and(page == table_ref[r, slot], offset < left)
                count = count + jnp.where(valid, 1.0, 0.0)
            count_ref[r * GROUP : (r + 1) * GROUP] = count

    @pl.when(jnp.logical_not(on_prefill(info_ref)))
    def _():
        count = count_ref[...]
        here = count > 0.0
        queries = q_ref[...].astype(jnp.float32).reshape(rows * GROUP, HEADDIM)
        scores = dot_t(queries.astype(jnp.bfloat16), kv_ref[:, :HEADDIM]) * SCALE
        scores = jnp.where(here, scores, NEG_FILL)
        peak = jnp.max(scores, axis=1, keepdims=True)
        weights = jnp.where(here, jnp.exp(scores - peak), 0.0)
        total = jnp.sum(weights * count, axis=1, keepdims=True)
        rounded = weights.astype(jnp.bfloat16).astype(jnp.float32) * count
        out_ref[0, :, :HEADDIM] = dot(rounded.astype(jnp.bfloat16), kv_ref[:, HEADDIM:])
        lane = lax.broadcasted_iota(jnp.int32, (rows * GROUP, HEADDIM), 1)
        out_ref[0, :, HEADDIM:] = jnp.where(lane < HEADDIM // 2, peak, total)


def cache_attention(info, table, lengths, queries, pool, page_len, after):
    rows = queries.shape[0]
    tokens = pool.shape[0]

    def head(h, info):
        return jnp.where(on_prefill(info), 0, h)

    return pl.pallas_call(
        functools.partial(cache_kernel, page_len),
        out_shape=(
            jax.ShapeDtypeStruct((KVHEADS, rows * GROUP, 2 * HEADDIM), jnp.float32),
            MARK,
        ),
        grid_spec=pltpu.PrefetchScalarGridSpec(
            num_scalar_prefetch=3,
            grid=(KVHEADS,),
            in_specs=[
                pl.BlockSpec((rows, GROUP, HEADDIM), lambda h, info, *_: (0, head(h, info), 0)),
                pl.BlockSpec((tokens, 2 * HEADDIM), lambda h, info, *_: (0, head(h, info))),
            ]
            + [IN_HBM] * len(after),
            out_specs=(
                pl.BlockSpec((1, rows * GROUP, 2 * HEADDIM), lambda h, info, *_: (head(h, info), 0, 0)),
                IN_HBM,
            ),
            scratch_shapes=[pltpu.VMEM((rows * GROUP, tokens), jnp.float32)],
        ),
        compiler_params=pltpu.CompilerParams(vmem_limit_bytes=LARGE),
        cost_estimate=COST,
        name="cache_attention",
    )(info, table, lengths, queries, pool, *after)


def combine_kernel(count, info_ref, *refs):
    part_refs, out_ref = refs[:count], refs[-2]

    @pl.when(on_prefill(info_ref))
    def _():
        out_ref[...] = jnp.zeros_like(out_ref)

    @pl.when(jnp.logical_not(on_prefill(info_ref)))
    def _():
        parts = [ref[n] for ref in part_refs for n in range(ref.shape[0])]
        peaks = [part[:, HEADDIM : HEADDIM + 1] for part in parts]
        peak = functools.reduce(jnp.maximum, peaks)
        factors = [jnp.exp(p - peak) for p in peaks]
        total = sum(part[:, -1:] * f for part, f in zip(parts, factors))
        mixed = sum(part[:, :HEADDIM] * f for part, f in zip(parts, factors))
        out_ref[...] = (mixed / total).reshape(out_ref.shape).astype(jnp.bfloat16)


def combine_parts(info, parts, rows, after):
    return pl.pallas_call(
        functools.partial(combine_kernel, len(parts)),
        out_shape=(jax.ShapeDtypeStruct((rows, QHEADS, HEADDIM), jnp.bfloat16), MARK),
        grid_spec=pltpu.PrefetchScalarGridSpec(
            num_scalar_prefetch=1,
            grid=(KVHEADS,),
            in_specs=[
                pl.BlockSpec(
                    (part.shape[0], None, rows * GROUP, 2 * HEADDIM),
                    lambda h, info_ref: (0, h, 0, 0),
                )
                for part in parts
            ]
            + [IN_HBM] * len(after),
            out_specs=(
                pl.BlockSpec((rows, GROUP, HEADDIM), lambda h, info_ref: (0, h, 0)),
                IN_HBM,
            ),
        ),
        compiler_params=pltpu.CompilerParams(vmem_limit_bytes=LARGE),
        cost_estimate=COST,
        name="combine_parts",
    )(info, *parts, *after)


def fresh_kernel(info_ref, q_ref, kv_ref, *rest):
    out_ref = rest[-1]
    heads = kv_ref.shape[1] // (2 * HEADDIM)
    units = q_ref[...].astype(jnp.float32)
    row = lax.broadcasted_iota(jnp.int32, units.shape, 0)
    for h in range(heads):
        mine = jnp.where(row == info_ref[TP] * heads + h, units, 0.0)
        mine = jnp.sum(mine, axis=0, keepdims=True)
        queries = jnp.concatenate(
            [mine[:, g * HEADDIM : (g + 1) * HEADDIM] for g in range(GROUP)], axis=0
        )
        start = 2 * h * HEADDIM
        keys = kv_ref[:, start : start + HEADDIM]
        scores = dot_t(queries.astype(jnp.bfloat16), keys) * SCALE
        peak = jnp.max(scores, axis=1, keepdims=True)
        weights = jnp.exp(scores - peak)
        total = jnp.sum(weights, axis=1, keepdims=True)
        mixed = dot(
            weights.astype(jnp.bfloat16), kv_ref[:, start + HEADDIM : start + 2 * HEADDIM]
        )
        out_ref[:, start : start + HEADDIM] = (mixed / total).astype(jnp.bfloat16)
        out_ref[:, start + HEADDIM : start + 2 * HEADDIM] = jnp.zeros(mixed.shape, jnp.bfloat16)


def fresh_attention(info, queries, unit, pairs, after):
    length, width = pairs.shape
    return pl.pallas_call(
        fresh_kernel,
        out_shape=jax.ShapeDtypeStruct((GROUP, width), jnp.bfloat16),
        grid_spec=pltpu.PrefetchScalarGridSpec(
            num_scalar_prefetch=1,
            grid=(1,),
            in_specs=[
                pl.BlockSpec(
                    (None, None) + queries.shape[2:],
                    lambda n, info_ref: (info_ref[FIRST + order(info_ref)], unit, 0, 0),
                ),
                pl.BlockSpec((length, width), lambda n, info_ref: (0, 0)),
            ]
            + [IN_HBM] * len(after),
            out_specs=pl.BlockSpec((GROUP, width), lambda n, info_ref: (0, 0)),
        ),
        compiler_params=pltpu.CompilerParams(vmem_limit_bytes=VMEM),
        cost_estimate=COST,
        name="fresh_attention",
    )(info, queries, pairs, *after)


def results_kernel(info_ref, unit_ref, out_ref):
    heads = out_ref.shape[0] // GROUP
    for h in range(heads):
        result = unit_ref[:, 2 * h * HEADDIM : (2 * h + 1) * HEADDIM].astype(jnp.float32)
        result = jnp.where(on_prefill(info_ref), 0.0, result)
        out_ref[h * GROUP : (h + 1) * GROUP] = result


def arrival_results(info, slots):
    devices, _, units, _, width = slots.shape
    heads = width // (2 * HEADDIM)
    return pl.pallas_call(
        results_kernel,
        out_shape=jax.ShapeDtypeStruct((QHEADS, HEADDIM), jnp.float32),
        grid_spec=pltpu.PrefetchScalarGridSpec(
            num_scalar_prefetch=1,
            grid=(devices,),
            in_specs=[
                pl.BlockSpec(
                    (None, None, None, GROUP, width),
                    lambda t, info_ref: (t, source_of(info_ref, order(info_ref)), units - 1, 0, 0),
                )
            ],
            out_specs=pl.BlockSpec((heads * GROUP, HEADDIM), lambda t, info_ref: (t, 0)),
        ),
        compiler_params=pltpu.CompilerParams(vmem_limit_bytes=SMALL),
        cost_estimate=COST,
        name="arrival_results",
    )(info, slots)


def relay_handoff(pairs, assignment, inst_count):
    half = inst_count // 2
    decode_ids = jnp.arange(half, dtype=jnp.int32)
    matches = assignment[None, :] == decode_ids[:, None]
    source = jnp.sum(jnp.where(matches, decode_ids[None, :], 0), axis=1).astype(jnp.int32)
    moved = lax.all_to_all(pairs, "tp", split_axis=0, concat_axis=1, tiled=True)
    lanes = 1024 if moved.size % (inst_count * 1024) == 0 else HEADDIM
    pieces = moved.reshape(inst_count, -1, lanes)
    spread = lax.all_to_all(pieces, "inst", split_axis=0, concat_axis=0, tiled=True)
    chosen = jnp.stack(
        [lax.dynamic_index_in_dim(spread, source[d], 0, False) for d in range(half)], axis=0
    )
    outgoing = jnp.concatenate([jnp.zeros_like(chosen), chosen], axis=0)
    delivered = lax.all_to_all(outgoing, "inst", split_axis=0, concat_axis=0, tiled=True)
    return delivered.reshape(moved.shape)


UNIT = 8
PAIRS = 4
PREFILL, DECODE = True, False


def copy_kernel(plan, side, counts, info_ref, *refs):
    inputs, marks, outputs = counts
    sources, targets, sems = refs[:inputs], refs[inputs + marks : inputs + marks + outputs], refs[-1]

    @pl.when(on_prefill(info_ref) == side)
    def _():
        started = []
        for source, target in plan(info_ref, sources, targets):
            started.append(pltpu.make_async_copy(source, target, sems.at[len(started)]))
        for copy in started:
            copy.start()
        for copy in started:
            copy.wait()


def copies(plan, number, info, operands, shapes, name, after=(), inside=True, side=PREFILL):
    place = IN_VMEM if inside else ANYWHERE
    return pl.pallas_call(
        functools.partial(copy_kernel, plan, side, (len(operands), len(after), len(shapes))),
        out_shape=tuple(jax.ShapeDtypeStruct(shape, jnp.bfloat16) for shape in shapes) + (MARK,),
        grid_spec=pltpu.PrefetchScalarGridSpec(
            num_scalar_prefetch=1,
            grid=(1,),
            in_specs=[place] * len(operands) + [IN_HBM] * len(after),
            out_specs=tuple([ANYWHERE] * len(shapes)) + (IN_HBM,),
            scratch_shapes=[pltpu.SemaphoreType.DMA((number,))],
        ),
        compiler_params=pltpu.CompilerParams(vmem_limit_bytes=MEDIUM if inside else SMALL),
        cost_estimate=COST,
        name=name,
    )(info, *operands, *after)


def relay_slots_kernel(far, info_ref, keep_ref, recv_ref, fresh_ref, out_ref, sems, fresh_sems):
    half = 2 * PAIRS

    @pl.when(jnp.logical_not(on_prefill(info_ref)))
    def _():
        here = order(info_ref)
        waits = []
        for d in range(half):
            source = source_of(info_ref, d)
            same = lax.rem(source, 2) == lax.rem(here, 2)
            shift = lax.rem(lax.div(here, 2) + PAIRS - lax.div(source, 2), PAIRS)
            for tau in range(2):
                slot = tau * half + d
                target = out_ref.at[slot, pl.ds(0, far)]
                mine = pltpu.make_async_copy(keep_ref.at[shift, tau], target, sems.at[slot])
                other = pltpu.make_async_copy(recv_ref.at[shift, tau], target, sems.at[slot])
                pl.when(same)(mine.start)
                pl.when(jnp.logical_not(same))(other.start)
                extra = pltpu.make_async_copy(fresh_ref, out_ref.at[slot, far], fresh_sems.at[slot])
                extra.start()
                waits += [mine, extra]
        for copy in waits:
            copy.wait()


def rows_kernel(near, far, info_ref, slots_ref, *refs):
    *parts, out_ref, zero_ref, sems = refs
    half = 2 * PAIRS
    width = slots_ref.shape[-1]
    near_all = near * half

    @pl.when(jnp.logical_not(on_prefill(info_ref)))
    def _():
        waits = []
        for t in range(2):
            columns = pl.ds(t * width, width)
            for s, part in enumerate(parts):
                pair = lax.rem(lax.div(order(info_ref), 2) + PAIRS - s, PAIRS)
                target = out_ref.at[pl.ds(pair * 2 * near, 2 * near), :, columns]
                waits.append(pltpu.make_async_copy(part.at[t], target, sems.at[len(waits)]))
            for i in range(half):
                source = slots_ref.at[t * half + i, pl.ds(0, far)]
                target = out_ref.at[pl.ds(near_all + i * far, far), :, columns]
                waits.append(pltpu.make_async_copy(source, target, sems.at[len(waits)]))
        for copy in waits:
            copy.start()
        for copy in waits:
            copy.wait()

    @pl.when(on_prefill(info_ref))
    def _():
        zero_ref[...] = jnp.zeros_like(zero_ref)
        size = zero_ref.shape[0]
        waits = []
        for n in range(out_ref.shape[0] // size):
            target = out_ref.at[pl.ds(n * size, size)]
            waits.append(pltpu.make_async_copy(zero_ref, target, sems.at[n]))
        for copy in waits:
            copy.start()
        for copy in waits:
            copy.wait()


def two_way_handoff(pairs, info, always, arrival_query, fresh_of, results_of, prompt_part, extra):
    half = 2 * PAIRS
    rows, width = pairs.shape
    units = rows // (2 * UNIT)
    far_all = -(-units * 3 // (5 * half)) * half
    near_all = units - far_all
    near, far = near_all // half, far_all // half
    block = (UNIT, width)
    by_unit = pairs.reshape((rows // UNIT,) + block)
    groups = [[base + 2 * i + tau for tau in range(2) for i in range(half)] for base in (0, 2 * half)]

    def crossing(array, s):
        hops = [
            (2 * p + k, half + 2 * ((p + s) % PAIRS) + k) for p in range(PAIRS) for k in range(2)
        ]
        return lax.ppermute(array, "inst", hops)

    def beside(array, base):
        return lax.ppermute(array, "inst", [(base + i, base + (i ^ 1)) for i in range(half)])

    def spread_out(array):
        return lax.all_to_all(
            array, ("inst", "tp"), 0, 0, axis_index_groups=groups, tiled=True
        )

    def cut(pre, sources, targets):
        plan = []
        for s in range(PAIRS):
            start = near_all + lax.rem(lax.div(order(pre), 2) + s, PAIRS) * (2 * far)
            for tau in range(2):
                plan.append((sources[0].at[pl.ds(tau * units + start, 2 * far)], targets[s].at[tau]))
        return plan

    def near_slots(pre, sources, targets):
        plan = []
        for tau in range(2):
            for i in range(half):
                slot = tau * half + i
                rows_here = sources[0].at[pl.ds(tau * units + i * near, near)]
                plan.append((rows_here, targets[0].at[slot, pl.ds(0, near)]))
                plan.append((sources[1], targets[0].at[slot, near]))
        return plan

    def for_neighbour(pre, sources, targets):
        plan = []
        for s in range(PAIRS):
            receiver = lax.rem(lax.div(order(pre), 2) + s, PAIRS) * 2 + 1 - lax.rem(order(pre), 2)
            for t in range(2):
                origin = t * half + source_of(pre, receiver)
                plan.append((sources[0].at[origin, pl.ds(0, near)], targets[0].at[s, t]))
        return plan

    def for_receivers(pre, sources, targets):
        plan = []
        for s in range(PAIRS):
            receiver = lax.rem(lax.div(order(pre), 2) + s, PAIRS) * 2 + lax.rem(order(pre), 2)
            for t in range(2):
                origin = t * half + source_of(pre, receiver)
                mine = targets[s].at[t, pl.ds(lax.rem(order(pre), 2) * near, near)]
                other = targets[s].at[t, pl.ds((1 - lax.rem(order(pre), 2)) * near, near)]
                plan.append((sources[0].at[origin, pl.ds(0, near)], mine))
                plan.append((sources[1].at[s, t], other))
        return plan

    def split(pre, sources, targets):
        plan = []
        for s in range(PAIRS):
            for tau in range(2):
                mine = sources[s].at[tau, pl.ds(lax.rem(order(pre), 2) * far, far)]
                other = sources[s].at[tau, pl.ds((1 - lax.rem(order(pre), 2)) * far, far)]
                plan.append((mine, targets[0].at[s, tau]))
                plan.append((other, targets[1].at[s, tau]))
        return plan

    near_shape = (2, 2 * near) + block

    def first_stage(by_unit, asked):
        slots, _ = copies(
            near_slots,
            8 * PAIRS,
            info,
            [by_unit, asked.reshape(block)],
            [(2 * half, near + 1) + block],
            "near_slots",
        )
        prompt, mark = prompt_part(0, None, [slots])
        spread = spread_out(slots)
        fresh = fresh_of(spread, near, [mark])
        outgoing, _ = copies(
            for_neighbour, 2 * PAIRS, info, [spread], [(PAIRS, 2, near) + block], "for_neighbour", [fresh]
        )
        incoming = beside(outgoing, 0)
        *near_parts, _ = copies(
            for_receivers, 4 * PAIRS, info, [spread, incoming], [near_shape] * PAIRS, "for_receivers"
        )
        return *near_parts, prompt, fresh

    def second_stage(prompt, fresh, *far_here):
        keep, give, _ = copies(
            split,
            4 * PAIRS,
            info,
            list(far_here),
            [(PAIRS, 2, far) + block] * 2,
            "split_relays",
            side=DECODE,
        )
        taken = beside(give, half)
        slots = pl.pallas_call(
            functools.partial(relay_slots_kernel, far),
            out_shape=jax.ShapeDtypeStruct((2 * half, far + 1) + block, jnp.bfloat16),
            grid_spec=pltpu.PrefetchScalarGridSpec(
                num_scalar_prefetch=1,
                grid=(1,),
                in_specs=[IN_VMEM] * 3,
                out_specs=ANYWHERE,
                scratch_shapes=[pltpu.SemaphoreType.DMA((2 * half,))] * 2,
            ),
            compiler_params=pltpu.CompilerParams(vmem_limit_bytes=MEDIUM),
            cost_estimate=COST,
            name="relay_slots",
        )(info, keep, taken, fresh)
        parts, mark = extra[0]([slots])
        slots = spread_out(slots)
        prompt, mark = prompt_part(1, prompt, [mark])
        more, _ = extra[1](parts, [mark])
        return prompt, slots, results_of(slots.reshape((2, half, far + 1) + block)), more

    def staged(stage, *operands):
        def never(*operands):
            outs = [jnp.zeros(out.shape, out.dtype) for out in jax.eval_shape(stage, *operands)]
            return tuple(outs) if stage is first_stage else (operands[0], *outs[1:])

        return lax.cond(always, lambda *operands: tuple(stage(*operands)), never, *operands)

    asked = lax.ppermute(arrival_query, "inst", [(i + half, i) for i in range(half)])
    *far_parts, _ = copies(
        cut, 2 * PAIRS, info, [by_unit], [(2, 2 * far) + block] * PAIRS, "cut_far", inside=False
    )
    far_here = [crossing(part, s) for s, part in enumerate(far_parts)]
    *near_parts, prompt, fresh = staged(first_stage, by_unit, asked)
    near_here = [crossing(part, s) for s, part in enumerate(near_parts)]
    prompt, slots, results, more = staged(second_stage, prompt, fresh, *far_here)
    handed = pl.pallas_call(
        functools.partial(rows_kernel, near, far),
        out_shape=jax.ShapeDtypeStruct((units, UNIT, 2 * width), jnp.bfloat16),
        grid_spec=pltpu.PrefetchScalarGridSpec(
            num_scalar_prefetch=1,
            grid=(1,),
            in_specs=[IN_VMEM] * (PAIRS + 1),
            out_specs=ANYWHERE,
            scratch_shapes=[
                pltpu.VMEM((half, UNIT, 2 * width), jnp.bfloat16),
                pltpu.SemaphoreType.DMA((2 * (half + PAIRS),)),
            ],
        ),
        compiler_params=pltpu.CompilerParams(vmem_limit_bytes=MEDIUM),
        cost_estimate=COST,
        name="rows",
    )(info, slots, *near_here)
    return handed.reshape(rows // 2, 2 * width), results, prompt, more


def shards(
    prompt_query,
    prompt_pairs,
    decode_query,
    arrival_query,
    cache_pool,
    page_table,
    lengths,
    assignment,
):
    inst_count = lax.axis_size("inst")
    tp_count = lax.axis_size("tp")
    half = inst_count // 2
    inst = lax.axis_index("inst")
    tp_index = lax.axis_index("tp")
    info = jnp.concatenate([jnp.stack([inst, tp_index]), assignment])
    groups = [list(range(half)), list(range(half, inst_count))]

    rows = decode_query.shape[0]
    pages, page_len = cache_pool.shape[0], cache_pool.shape[1]
    by_token = cache_pool.reshape(pages * page_len, -1)
    by_head = decode_query.reshape(rows, QHEADS, HEADDIM)

    def cached(after=()):
        part, mark = cache_attention(info, page_table, lengths, by_head, by_token, page_len, after)
        part = part[None]
        if tp_count == 2:
            return (part, lax.ppermute(part, "tp", [(0, 1), (1, 0)])), mark
        return (lax.all_gather(part, "tp", axis=0, tiled=True),), mark

    def combined(parts, after=()):
        if tp_count == 2:
            here, there = parts
            parts = jnp.where(tp_index == 0, here, there), jnp.where(tp_index == 0, there, here)
        out, mark = combine_parts(info, parts, rows, after)
        return out.reshape(rows, QHEADS * HEADDIM), mark

    heads = GROUP // 2
    steps = prompt_query.shape[1] // (heads * HEADDIM)
    kv_here = prompt_pairs.shape[1] // (2 * HEADDIM)

    def fresh_of(queries, unit, after=()):
        fresh = fresh_attention(info, queries, unit, prompt_pairs, after)
        return lax.ppermute(fresh, "inst", [(i, i + half) for i in range(half)])

    def results_of(slots):
        found = arrival_results(info, slots)
        return found.astype(jnp.bfloat16).reshape(1, QHEADS * HEADDIM)

    def prompt_part(first, last, earlier, after=()):
        return prompt_attention(
            info, prompt_query, prompt_pairs, first, last - first, heads, earlier, after
        )

    row_units = prompt_pairs.shape[0] // (2 * UNIT)
    if inst_count == 4 * PAIRS and tp_count == 2 and row_units == 5 * half and steps == 8:
        cuts = (0, 3, 8)
        handed, arrival_out, prefill_out, decode_out = two_way_handoff(
            prompt_pairs,
            info,
            assignment[0] >= 0,
            arrival_query,
            fresh_of,
            results_of,
            lambda n, earlier, after: prompt_part(cuts[n], cuts[n + 1], earlier, after),
            (cached, combined),
        )
    else:
        handed = relay_handoff(prompt_pairs, assignment, inst_count)
        sent = lax.ppermute(arrival_query, "inst", [(i + half, i) for i in range(half)])
        every = lax.all_gather(sent, "inst", axis=0, tiled=True, axis_index_groups=groups)
        fresh = fresh_of(every.reshape(half, 1, KVHEADS, GROUP * HEADDIM), 0)
        results = lax.all_gather(fresh, "inst", axis_index_groups=groups)
        arrival_out = results_of(lax.all_gather(results, "tp")[:, :, None])
        prefill_out, _ = prompt_part(0, steps, None)
        decode_out, _ = combined(cached()[0])
    return (prefill_out, handed, decode_out, arrival_out)


def solution(mesh):
    return jax.shard_map(
        shards,
        mesh=mesh,
        in_specs=(
            P("inst", "tp"),
            P("inst", "tp"),
            P("inst", None),
            P("inst", None),
            P(("inst", "tp"), None, None),
            P("inst", "tp"),
            P("inst"),
            P(),
        ),
        out_specs=(P("inst", "tp"), P(("inst", "tp"), None), P("inst", None), P("inst", None)),
        check_vma=False,
    )
```

```python
import functools

import jax
import jax.numpy as jnp
from jax import lax
from jax.experimental import pallas as pl
from jax.experimental.pallas import tpu as pltpu
from jax.sharding import PartitionSpec as P

QHEADS = 64
KVHEADS = 8
HEADDIM = 128
GROUP = QHEADS // KVHEADS
SCALE = HEADDIM ** (-0.5)
LOG2E = 1.4426950408889634
NEG_FILL = -1e30
TILE = 128
VMEM = 24 * 1024 * 1024
SMALL = 1024 * 1024
MEDIUM = 8 * 1024 * 1024
LARGE = 57 * 1024 * 1024
COST = pl.CostEstimate(flops=1, bytes_accessed=1, transcendentals=0)


INST, TP, FIRST = 0, 1, 2


def on_prefill(info):
    return info[INST] < info.shape[0] - FIRST


def order(info):
    half = info.shape[0] - FIRST
    return info[INST] - jnp.where(on_prefill(info), 0, half)


def source_of(info, receiver):
    half = info.shape[0] - FIRST
    found = jnp.int32(0)
    for p in range(half):
        found = jnp.where(info[FIRST + p] == receiver, p, found)
    return found


def dot_t(a, b):
    return lax.dot_general(a, b, (((1,), (1,)), ((), ())), preferred_element_type=jnp.float32)


def dot(a, b):
    return lax.dot_general(a, b, (((1,), (0,)), ((), ())), preferred_element_type=jnp.float32)


def prompt_kernel(heads, info_ref, q_ref, kv_ref, *rest):
    out_ref = rest[-2]
    length = q_ref.shape[0]

    @pl.when(jnp.logical_not(on_prefill(info_ref)))
    def _():
        out_ref[...] = jnp.zeros_like(out_ref)

    @pl.when(on_prefill(info_ref))
    def _():
        rows_all = lax.broadcasted_iota(jnp.int32, (TILE, TILE), 0)
        cols_all = lax.broadcasted_iota(jnp.int32, (TILE, TILE), 1)
        below = jnp.concatenate([rows_all >= cols_all] * heads, axis=0)
        ones = jnp.ones((length, HEADDIM), jnp.bfloat16)
        values = jnp.concatenate([kv_ref[:, HEADDIM:], ones], axis=1)
        for start in range(0, length, TILE):
            stop = start + TILE
            queries = jnp.concatenate(
                [q_ref[start:stop, h * HEADDIM : (h + 1) * HEADDIM] for h in range(heads)], axis=0
            )
            scores = dot_t(queries, kv_ref[:stop, :HEADDIM])
            last = jnp.where(below, scores[:, start:], NEG_FILL)
            scores = jnp.concatenate([scores[:, :start], last], axis=1) if start else last
            peak = jnp.max(scores, axis=1, keepdims=True)
            weights = jnp.exp2((scores - peak) * (SCALE * LOG2E)).astype(jnp.bfloat16)
            mixed = dot(weights, values[:stop])
            result = (mixed[:, :HEADDIM] / mixed[:, HEADDIM:]).astype(jnp.bfloat16)
            for h in range(heads):
                out_ref[start:stop, h * HEADDIM : (h + 1) * HEADDIM] = result[
                    h * TILE : (h + 1) * TILE
                ]


MARK = jax.ShapeDtypeStruct((8, 128), jnp.float32)
IN_HBM = pl.BlockSpec(memory_space=pltpu.HBM)
ANYWHERE = pl.BlockSpec(memory_space=pl.ANY)
IN_VMEM = pl.BlockSpec(memory_space=pltpu.VMEM)


def prompt_attention(info, queries, pairs, first, steps, heads, earlier, after):
    length, width = queries.shape
    per_kv = GROUP // heads

    def q_map(i, info_ref):
        return (0, jnp.where(on_prefill(info_ref), i + first, 0))

    def kv_map(i, info_ref):
        return (0, jnp.where(on_prefill(info_ref), (i + first) // per_kv, 0))

    in_specs = [
        pl.BlockSpec((length, heads * HEADDIM), q_map),
        pl.BlockSpec((length, 2 * HEADDIM), kv_map),
    ]
    operands = [info, queries, pairs]
    aliases = {}
    if earlier is not None:
        in_specs.append(ANYWHERE)
        operands.append(earlier)
        aliases = {3: 0}
    return pl.pallas_call(
        functools.partial(prompt_kernel, heads),
        out_shape=(jax.ShapeDtypeStruct((length, width), jnp.bfloat16), MARK),
        grid_spec=pltpu.PrefetchScalarGridSpec(
            num_scalar_prefetch=1,
            grid=(steps,),
            in_specs=in_specs + [IN_HBM] * len(after),
            out_specs=(
                pl.BlockSpec((length, heads * HEADDIM), lambda i, info_ref: (0, i + first)),
                IN_HBM,
            ),
        ),
        input_output_aliases=aliases,
        compiler_params=pltpu.CompilerParams(vmem_limit_bytes=LARGE),
        cost_estimate=COST,
        name="prompt_attention",
    )(*operands, *after)


def head_queries(block, head):
    start = head * GROUP * HEADDIM
    return jnp.concatenate(
        [
            block[r : r + 1, start + g * HEADDIM : start + (g + 1) * HEADDIM]
            for r in range(block.shape[0])
            for g in range(GROUP)
        ],
        axis=0,
    ).astype(jnp.bfloat16)


def store_part(out_ref, head, mixed, peak, total):
    lane = lax.broadcasted_iota(jnp.int32, mixed.shape, 1)
    out_ref[head, :, :HEADDIM] = mixed
    out_ref[head, :, HEADDIM:] = jnp.where(lane < HEADDIM // 2, peak, total)


def merged(parts):
    peaks = [part[:, HEADDIM : HEADDIM + 1] for part in parts]
    peak = functools.reduce(jnp.maximum, peaks)
    factors = [jnp.exp(p - peak) for p in peaks]
    total = sum(part[:, -1:] * f for part, f in zip(parts, factors))
    mixed = sum(part[:, :HEADDIM] * f for part, f in zip(parts, factors))
    return mixed, peak, total


def cache_kernel(page_len, info_ref, table_ref, lengths_ref, q_ref, kv_ref, *rest):
    out_ref, _, count_ref = rest[-3:]
    rows, slots = table_ref.shape

    @pl.when(jnp.logical_and(jnp.logical_not(on_prefill(info_ref)), pl.program_id(0) == 0))
    def _():
        token = lax.broadcasted_iota(jnp.int32, (GROUP, count_ref.shape[1]), 1)
        page, offset = token // page_len, token % page_len
        for r in range(rows):
            count = jnp.zeros(token.shape, jnp.float32)
            for slot in range(slots):
                left = lengths_ref[r] - (info_ref[TP] * slots + slot) * page_len
                valid = jnp.logical_and(page == table_ref[r, slot], offset < left)
                count = count + jnp.where(valid, 1.0, 0.0)
            count_ref[r * GROUP : (r + 1) * GROUP] = count

    @pl.when(on_prefill(info_ref))
    def _():
        out_ref[...] = jnp.zeros_like(out_ref)

    @pl.when(jnp.logical_not(on_prefill(info_ref)))
    def _():
        count = count_ref[...]
        here = count > 0.0
        block = q_ref[...].astype(jnp.float32)
        for head in range(out_ref.shape[0]):
            start = 2 * head * HEADDIM
            keys = kv_ref[:, start : start + HEADDIM]
            values = kv_ref[:, start + HEADDIM : start + 2 * HEADDIM]
            scores = dot_t(head_queries(block, head), keys) * SCALE
            scores = jnp.where(here, scores, NEG_FILL)
            peak = jnp.max(scores, axis=1, keepdims=True)
            weights = jnp.where(here, jnp.exp(scores - peak), 0.0)
            total = jnp.sum(weights * count, axis=1, keepdims=True)
            rounded = weights.astype(jnp.bfloat16).astype(jnp.float32) * count
            store_part(out_ref, head, dot(rounded.astype(jnp.bfloat16), values), peak, total)


def cache_attention(info, table, lengths, queries, pool, page_len, after):
    rows = queries.shape[0]
    tokens = pool.shape[0]
    steps = 2
    heads = KVHEADS // steps

    def step(n, info):
        return jnp.where(on_prefill(info), 0, n)

    return pl.pallas_call(
        functools.partial(cache_kernel, page_len),
        out_shape=(
            jax.ShapeDtypeStruct((KVHEADS, rows * GROUP, 2 * HEADDIM), jnp.float32),
            MARK,
        ),
        grid_spec=pltpu.PrefetchScalarGridSpec(
            num_scalar_prefetch=3,
            grid=(steps,),
            in_specs=[
                pl.BlockSpec((rows, heads * GROUP * HEADDIM), lambda n, info, *_: (0, step(n, info))),
                pl.BlockSpec((tokens, 2 * heads * HEADDIM), lambda n, info, *_: (0, step(n, info))),
            ]
            + [IN_HBM] * len(after),
            out_specs=(
                pl.BlockSpec(
                    (heads, rows * GROUP, 2 * HEADDIM), lambda n, info, *_: (step(n, info), 0, 0)
                ),
                IN_HBM,
            ),
            scratch_shapes=[pltpu.VMEM((rows * GROUP, tokens), jnp.float32)],
        ),
        compiler_params=pltpu.CompilerParams(vmem_limit_bytes=LARGE),
        cost_estimate=COST,
        name="cache_attention",
    )(info, table, lengths, queries, pool, *after)


def rows_part(queries, rows, out_ref, earlier_ref):
    block = queries[...].astype(jnp.float32)
    heads = rows[0].shape[1] // (2 * HEADDIM)
    for head in range(KVHEADS):
        held = rows[head // heads]
        start = 2 * (head % heads) * HEADDIM
        scores = dot_t(head_queries(block, head), held[:, start : start + HEADDIM]) * SCALE
        peak = jnp.max(scores, axis=1, keepdims=True)
        weights = jnp.exp(scores - peak)
        total = jnp.sum(weights, axis=1, keepdims=True)
        values = held[:, start + HEADDIM : start + 2 * HEADDIM]
        mixed = dot(weights.astype(jnp.bfloat16), values)
        store_part(out_ref, head, mixed, peak, total)
        if earlier_ref is not None:
            store_part(out_ref, head, *merged([out_ref[head], earlier_ref[head]]))


def flat_rows(pieces):
    wide = [piece.astype(jnp.float32).reshape(-1, piece.shape[-1]) for piece in pieces]
    return jnp.concatenate(wide, axis=0).astype(jnp.bfloat16)


def whole_rows_kernel(info_ref, q_ref, rows_ref, out_ref):
    rows_part(q_ref, [rows_ref[...]], out_ref, None)


def far_rows_kernel(info_ref, q_ref, slots_ref, out_ref, held_ref, sem):
    @pl.when(jnp.logical_not(on_prefill(info_ref)))
    def _():
        copy = pltpu.make_async_copy(slots_ref, held_ref, sem)
        copy.start()
        copy.wait()
        half = 2 * PAIRS
        rows = [
            flat_rows([held_ref[t * half + i] for i in range(half)]) for t in range(2)
        ]
        rows_part(q_ref, rows, out_ref, None)


def near_rows_kernel(info_ref, q_ref, earlier_ref, *refs):
    *part_refs, out_ref = refs

    @pl.when(jnp.logical_not(on_prefill(info_ref)))
    def _():
        rows = [flat_rows([part[t] for part in part_refs]) for t in range(2)]
        rows_part(q_ref, rows, out_ref, earlier_ref)


def arrival_part(kernel, info, query, operands, places, scratch, name):
    return pl.pallas_call(
        kernel,
        out_shape=jax.ShapeDtypeStruct((KVHEADS, GROUP, 2 * HEADDIM), jnp.float32),
        grid_spec=pltpu.PrefetchScalarGridSpec(
            num_scalar_prefetch=1,
            grid=(1,),
            in_specs=[IN_VMEM] + places,
            out_specs=IN_VMEM,
            scratch_shapes=scratch,
        ),
        compiler_params=pltpu.CompilerParams(vmem_limit_bytes=VMEM),
        cost_estimate=COST,
        name=name,
    )(info, query, *operands)


def combine_kernel(count, info_ref, *refs):
    part_refs, out_ref = refs[:count], refs[-2]

    @pl.when(on_prefill(info_ref))
    def _():
        out_ref[...] = jnp.zeros_like(out_ref)

    @pl.when(jnp.logical_not(on_prefill(info_ref)))
    def _():
        results = []
        for head in range(KVHEADS):
            if count == 2:
                here, there = part_refs[0][head], part_refs[1][head]
                first = info_ref[TP] == 0
                parts = [jnp.where(first, here, there), jnp.where(first, there, here)]
            else:
                parts = [part_refs[0][n, head] for n in range(part_refs[0].shape[0])]
            mixed, _, total = merged(parts)
            results.append(mixed / total)
        for r in range(out_ref.shape[0]):
            row = [
                results[head][r * GROUP + g : r * GROUP + g + 1]
                for head in range(KVHEADS)
                for g in range(GROUP)
            ]
            out_ref[r : r + 1] = jnp.concatenate(row, axis=1).astype(jnp.bfloat16)


def combine_parts(info, parts, after=()):
    rows = parts[0].shape[-2] // GROUP
    return pl.pallas_call(
        functools.partial(combine_kernel, len(parts)),
        out_shape=(jax.ShapeDtypeStruct((rows, QHEADS * HEADDIM), jnp.bfloat16), MARK),
        grid_spec=pltpu.PrefetchScalarGridSpec(
            num_scalar_prefetch=1,
            grid=(1,),
            in_specs=[IN_VMEM] * len(parts) + [IN_HBM] * len(after),
            out_specs=(IN_VMEM, IN_HBM),
        ),
        compiler_params=pltpu.CompilerParams(vmem_limit_bytes=VMEM),
        cost_estimate=COST,
        name="combine_parts",
    )(info, *parts, *after)


def relay_handoff(pairs, assignment, inst_count):
    half = inst_count // 2
    decode_ids = jnp.arange(half, dtype=jnp.int32)
    matches = assignment[None, :] == decode_ids[:, None]
    source = jnp.sum(jnp.where(matches, decode_ids[None, :], 0), axis=1).astype(jnp.int32)
    moved = lax.all_to_all(pairs, "tp", split_axis=0, concat_axis=1, tiled=True)
    lanes = 1024 if moved.size % (inst_count * 1024) == 0 else HEADDIM
    pieces = moved.reshape(inst_count, -1, lanes)
    spread = lax.all_to_all(pieces, "inst", split_axis=0, concat_axis=0, tiled=True)
    chosen = jnp.stack(
        [lax.dynamic_index_in_dim(spread, source[d], 0, False) for d in range(half)], axis=0
    )
    outgoing = jnp.concatenate([jnp.zeros_like(chosen), chosen], axis=0)
    delivered = lax.all_to_all(outgoing, "inst", split_axis=0, concat_axis=0, tiled=True)
    return delivered.reshape(moved.shape)


UNIT = 8
PAIRS = 4
PREFILL, DECODE = True, False


def copy_kernel(plan, side, counts, info_ref, *refs):
    inputs, marks, outputs, stages = counts
    sources, targets = refs[:inputs], refs[inputs + marks : inputs + marks + outputs]
    held, sems = refs[-1 - stages : -1], refs[-1]

    @pl.when(on_prefill(info_ref) == side)
    def _():
        started = []
        for source, target in zip(sources, held):
            started.append(pltpu.make_async_copy(source, target, sems.at[len(started)]))
        for copy in started:
            copy.start()
        for copy in started:
            copy.wait()
        started = []
        for source, target in plan(info_ref, held or sources, targets):
            started.append(pltpu.make_async_copy(source, target, sems.at[len(started)]))
        for copy in started:
            copy.start()
        for copy in started:
            copy.wait()


def copies(plan, number, info, operands, shapes, name, after=(), stage=False, side=PREFILL):
    held = [pltpu.VMEM(x.shape, x.dtype) for x in operands] if stage else []
    return pl.pallas_call(
        functools.partial(copy_kernel, plan, side, (len(operands), len(after), len(shapes), len(held))),
        out_shape=tuple(jax.ShapeDtypeStruct(shape, jnp.bfloat16) for shape in shapes),
        grid_spec=pltpu.PrefetchScalarGridSpec(
            num_scalar_prefetch=1,
            grid=(1,),
            in_specs=[ANYWHERE] * len(operands) + [IN_HBM] * len(after),
            out_specs=tuple([ANYWHERE] * len(shapes)),
            scratch_shapes=held + [pltpu.SemaphoreType.DMA((number,))],
        ),
        compiler_params=pltpu.CompilerParams(vmem_limit_bytes=MEDIUM if stage else SMALL),
        cost_estimate=COST,
        name=name,
    )(info, *operands, *after)


def relay_slots_kernel(far, info_ref, keep_ref, recv_ref, out_ref, sems):
    half = 2 * PAIRS

    @pl.when(jnp.logical_not(on_prefill(info_ref)))
    def _():
        here = order(info_ref)
        waits = []
        for d in range(half):
            source = source_of(info_ref, d)
            same = lax.rem(source, 2) == lax.rem(here, 2)
            shift = lax.rem(lax.div(here, 2) + PAIRS - lax.div(source, 2), PAIRS)
            for tau in range(2):
                slot = tau * half + d
                target = out_ref.at[slot]
                mine = pltpu.make_async_copy(keep_ref.at[shift, tau], target, sems.at[slot])
                other = pltpu.make_async_copy(recv_ref.at[shift, tau], target, sems.at[slot])
                pl.when(same)(mine.start)
                pl.when(jnp.logical_not(same))(other.start)
                waits.append(mine)
        for copy in waits:
            copy.wait()


def rows_kernel(near, far, info_ref, slots_ref, *refs):
    *parts, out_ref, zero_ref, held_ref, sems = refs
    half = 2 * PAIRS
    width = slots_ref.shape[-1]
    near_all = near * half

    @pl.when(jnp.logical_not(on_prefill(info_ref)))
    def _():
        last = sems.shape[0] - 1
        staged = pltpu.make_async_copy(slots_ref, held_ref, sems.at[last])
        staged.start()
        waits = []
        for t in range(2):
            for s, part in enumerate(parts):
                pair = lax.rem(lax.div(order(info_ref), 2) + PAIRS - s, PAIRS)
                target = out_ref.at[pl.ds(pair * 2 * near, 2 * near), :, pl.ds(t * width, width)]
                waits.append(pltpu.make_async_copy(part.at[t], target, sems.at[len(waits)]))
                waits[-1].start()
        staged.wait()
        for t in range(2):
            for i in range(half):
                target = out_ref.at[pl.ds(near_all + i * far, far), :, pl.ds(t * width, width)]
                waits.append(
                    pltpu.make_async_copy(held_ref.at[t * half + i], target, sems.at[len(waits)])
                )
                waits[-1].start()
        for copy in waits:
            copy.wait()

    @pl.when(on_prefill(info_ref))
    def _():
        zero_ref[...] = jnp.zeros_like(zero_ref)
        size = zero_ref.shape[0]
        waits = []
        for n in range(out_ref.shape[0] // size):
            target = out_ref.at[pl.ds(n * size, size)]
            waits.append(pltpu.make_async_copy(zero_ref, target, sems.at[n]))
        for copy in waits:
            copy.start()
        for copy in waits:
            copy.wait()


def two_way_handoff(pairs, info, always, arrival_query, prompt_part, cached, combined):
    half = 2 * PAIRS
    rows, width = pairs.shape
    units = rows // (2 * UNIT)
    far_all = -(-units * 3 // (5 * half)) * half
    near_all = units - far_all
    near, far = near_all // half, far_all // half
    block = (UNIT, width)
    by_unit = pairs.reshape((rows // UNIT,) + block)
    groups = [[base + 2 * i + tau for tau in range(2) for i in range(half)] for base in (0, 2 * half)]

    def crossing(array, s):
        hops = [
            (2 * p + k, half + 2 * ((p + s) % PAIRS) + k) for p in range(PAIRS) for k in range(2)
        ]
        return lax.ppermute(array, "inst", hops)

    def beside(array, base):
        return lax.ppermute(array, "inst", [(base + i, base + (i ^ 1)) for i in range(half)])

    def spread_out(array):
        return lax.all_to_all(
            array, ("inst", "tp"), 0, 0, axis_index_groups=groups, tiled=True
        )

    def cut(pre, sources, targets):
        plan = []
        for s in range(PAIRS):
            start = near_all + lax.rem(lax.div(order(pre), 2) + s, PAIRS) * (2 * far)
            for tau in range(2):
                plan.append((sources[0].at[pl.ds(tau * units + start, 2 * far)], targets[s].at[tau]))
        for tau in range(2):
            plan.append((sources[0].at[pl.ds(tau * units, near_all)], targets[PAIRS].at[tau]))
        return plan

    def for_neighbour(pre, sources, targets):
        plan = []
        for s in range(PAIRS):
            receiver = lax.rem(lax.div(order(pre), 2) + s, PAIRS) * 2 + 1 - lax.rem(order(pre), 2)
            for t in range(2):
                origin = t * half + source_of(pre, receiver)
                plan.append((sources[0].at[origin], targets[0].at[s, t]))
        return plan

    def for_receivers(pre, sources, targets):
        plan = []
        for s in range(PAIRS):
            receiver = lax.rem(lax.div(order(pre), 2) + s, PAIRS) * 2 + lax.rem(order(pre), 2)
            for t in range(2):
                origin = t * half + source_of(pre, receiver)
                mine = targets[s].at[t, pl.ds(lax.rem(order(pre), 2) * near, near)]
                other = targets[s].at[t, pl.ds((1 - lax.rem(order(pre), 2)) * near, near)]
                plan.append((sources[0].at[origin], mine))
                plan.append((sources[1].at[s, t], other))
        return plan

    def split(pre, sources, targets):
        plan = []
        for s in range(PAIRS):
            for tau in range(2):
                mine = sources[s].at[tau, pl.ds(lax.rem(order(pre), 2) * far, far)]
                other = sources[s].at[tau, pl.ds((1 - lax.rem(order(pre), 2)) * far, far)]
                plan.append((mine, targets[0].at[s, tau]))
                plan.append((other, targets[1].at[s, tau]))
        return plan

    near_shape = (2, 2 * near) + block

    def first_stage(slots):
        parts, mark = cached([slots])
        prompt, mark = prompt_part(0, None, [mark])
        spread = spread_out(slots)
        (outgoing,) = copies(
            for_neighbour, 2 * PAIRS, info, [spread], [(PAIRS, 2, near) + block], "for_neighbour", [mark]
        )
        incoming = beside(outgoing, 0)
        near_parts = copies(
            for_receivers, 4 * PAIRS, info, [spread, incoming], [near_shape] * PAIRS, "for_receivers"
        )
        return *near_parts, prompt, parts

    def second_stage(prompt, parts, *far_here):
        keep, give = copies(
            split,
            4 * PAIRS,
            info,
            list(far_here),
            [(PAIRS, 2, far) + block] * 2,
            "split_relays",
            stage=True,
            side=DECODE,
        )
        taken = beside(give, half)
        slots = pl.pallas_call(
            functools.partial(relay_slots_kernel, far),
            out_shape=jax.ShapeDtypeStruct((2 * half, far) + block, jnp.bfloat16),
            grid_spec=pltpu.PrefetchScalarGridSpec(
                num_scalar_prefetch=1,
                grid=(1,),
                in_specs=[ANYWHERE] * 2,
                out_specs=ANYWHERE,
                scratch_shapes=[pltpu.SemaphoreType.DMA((2 * half,))],
            ),
            compiler_params=pltpu.CompilerParams(vmem_limit_bytes=SMALL),
            cost_estimate=COST,
            name="relay_slots",
        )(info, keep, taken)
        prompt, mark = prompt_part(1, prompt, [slots])
        decode_out = combined(parts, [mark])
        slots = spread_out(slots)
        arrival = arrival_part(
            far_rows_kernel,
            info,
            arrival_query,
            [slots],
            [ANYWHERE],
            [pltpu.VMEM(slots.shape, slots.dtype), pltpu.SemaphoreType.DMA],
            "far_rows",
        )
        return prompt, slots, decode_out, arrival

    def staged(stage, *operands):
        def never(*operands):
            outs = [jnp.zeros(out.shape, out.dtype) for out in jax.eval_shape(stage, *operands)]
            return tuple(outs) if stage is first_stage else (operands[0], *outs[1:])

        return lax.cond(always, lambda *operands: tuple(stage(*operands)), never, *operands)

    *far_parts, near_rows = copies(
        cut,
        2 * PAIRS + 2,
        info,
        [by_unit],
        [(2, 2 * far) + block] * PAIRS + [(2, near_all) + block],
        "cut_rows",
        stage=True,
    )
    far_here = [crossing(part, s) for s, part in enumerate(far_parts)]
    near_rows = near_rows.reshape((2 * half, near) + block)
    *near_parts, prompt, parts = staged(first_stage, near_rows)
    near_here = [crossing(part, s) for s, part in enumerate(near_parts)]
    prompt, slots, decode_out, arrival = staged(second_stage, prompt, parts, *far_here)
    arrival = arrival_part(
        near_rows_kernel,
        info,
        arrival_query,
        [arrival, *near_here],
        [IN_VMEM] * (PAIRS + 1),
        [],
        "near_rows",
    )
    handed = pl.pallas_call(
        functools.partial(rows_kernel, near, far),
        out_shape=jax.ShapeDtypeStruct((units, UNIT, 2 * width), jnp.bfloat16),
        grid_spec=pltpu.PrefetchScalarGridSpec(
            num_scalar_prefetch=1,
            grid=(1,),
            in_specs=[ANYWHERE] * (PAIRS + 1),
            out_specs=ANYWHERE,
            scratch_shapes=[
                pltpu.VMEM((half, UNIT, 2 * width), jnp.bfloat16),
                pltpu.VMEM(slots.shape, slots.dtype),
                pltpu.SemaphoreType.DMA((2 * (half + PAIRS) + 1,)),
            ],
        ),
        compiler_params=pltpu.CompilerParams(vmem_limit_bytes=MEDIUM),
        cost_estimate=COST,
        name="rows",
    )(info, slots, *near_here)
    return prompt, handed.reshape(rows // 2, 2 * width), decode_out, combined(arrival)


def shards(
    prompt_query,
    prompt_pairs,
    decode_query,
    arrival_query,
    cache_pool,
    page_table,
    lengths,
    assignment,
):
    inst_count = lax.axis_size("inst")
    tp_count = lax.axis_size("tp")
    half = inst_count // 2
    inst = lax.axis_index("inst")
    tp_index = lax.axis_index("tp")
    info = jnp.concatenate([jnp.stack([inst, tp_index]), assignment])
    pages, page_len = cache_pool.shape[0], cache_pool.shape[1]
    by_token = cache_pool.reshape(pages * page_len, -1)

    def cached(after=()):
        return cache_attention(info, page_table, lengths, decode_query, by_token, page_len, after)

    def combined(part, after=()):
        if tp_count == 2:
            parts = [part, lax.ppermute(part, "tp", [(0, 1), (1, 0)])]
        else:
            parts = [lax.all_gather(part, "tp")]
        return combine_parts(info, parts, after)[0]

    heads = GROUP // 2
    steps = prompt_query.shape[1] // (heads * HEADDIM)

    def prompt_part(first, last, earlier, after=()):
        return prompt_attention(
            info, prompt_query, prompt_pairs, first, last - first, heads, earlier, after
        )

    row_units = prompt_pairs.shape[0] // (2 * UNIT)
    if inst_count == 4 * PAIRS and tp_count == 2 and row_units == 5 * half and steps == 8:
        cuts = (0, 4, 8)
        return two_way_handoff(
            prompt_pairs,
            info,
            assignment[0] >= 0,
            arrival_query,
            lambda n, earlier, after: prompt_part(cuts[n], cuts[n + 1], earlier, after),
            cached,
            combined,
        )
    handed = relay_handoff(prompt_pairs, assignment, inst_count)
    arrival = arrival_part(
        whole_rows_kernel, info, arrival_query, [handed], [IN_VMEM], [], "whole_rows"
    )
    prefill_out, _ = prompt_part(0, steps, None)
    return prefill_out, handed, combined(cached()[0]), combined(arrival)


def solution(mesh):
    return jax.shard_map(
        shards,
        mesh=mesh,
        in_specs=(
            P("inst", "tp"),
            P("inst", "tp"),
            P("inst", None),
            P("inst", None),
            P(("inst", "tp"), None, None),
            P("inst", "tp"),
            P("inst"),
            P(),
        ),
        out_specs=(P("inst", "tp"), P(("inst", "tp"), None), P("inst", None), P("inst", None)),
        check_vma=False,
    )
```

```python
import functools

import jax
import jax.numpy as jnp
from jax import lax
from jax.experimental import pallas as pl
from jax.experimental.pallas import tpu as pltpu
from jax.sharding import PartitionSpec as P

QHEADS = 64
KVHEADS = 8
HEADDIM = 128
GROUP = QHEADS // KVHEADS
SCALE = HEADDIM ** (-0.5)
LOG2E = 1.4426950408889634
NEG_FILL = -1e30
TILE = 128
VMEM = 24 * 1024 * 1024
SMALL = 1024 * 1024
MEDIUM = 8 * 1024 * 1024
LARGE = 57 * 1024 * 1024
COST = pl.CostEstimate(flops=1, bytes_accessed=1, transcendentals=0)


INST, TP, FIRST = 0, 1, 2


def on_prefill(info):
    return info[INST] < info.shape[0] - FIRST


def order(info):
    half = info.shape[0] - FIRST
    return info[INST] - jnp.where(on_prefill(info), 0, half)


def source_of(info, receiver):
    half = info.shape[0] - FIRST
    found = jnp.int32(0)
    for p in range(half):
        found = jnp.where(info[FIRST + p] == receiver, p, found)
    return found


def dot_t(a, b):
    return lax.dot_general(a, b, (((1,), (1,)), ((), ())), preferred_element_type=jnp.float32)


def dot(a, b):
    return lax.dot_general(a, b, (((1,), (0,)), ((), ())), preferred_element_type=jnp.float32)


def prompt_kernel(heads, info_ref, q_ref, kv_ref, *rest):
    out_ref = rest[-2]
    length = q_ref.shape[0]

    @pl.when(jnp.logical_not(on_prefill(info_ref)))
    def _():
        out_ref[...] = jnp.zeros_like(out_ref)

    @pl.when(on_prefill(info_ref))
    def _():
        rows_all = lax.broadcasted_iota(jnp.int32, (TILE, TILE), 0)
        cols_all = lax.broadcasted_iota(jnp.int32, (TILE, TILE), 1)
        below = jnp.concatenate([rows_all >= cols_all] * heads, axis=0)
        ones = jnp.ones((length, HEADDIM), jnp.bfloat16)
        values = jnp.concatenate([kv_ref[:, HEADDIM:], ones], axis=1)
        for start in range(0, length, TILE):
            stop = start + TILE
            queries = jnp.concatenate(
                [q_ref[start:stop, h * HEADDIM : (h + 1) * HEADDIM] for h in range(heads)], axis=0
            )
            scores = dot_t(queries, kv_ref[:stop, :HEADDIM])
            last = jnp.where(below, scores[:, start:], NEG_FILL)
            scores = jnp.concatenate([scores[:, :start], last], axis=1) if start else last
            peak = jnp.max(scores, axis=1, keepdims=True)
            weights = jnp.exp2((scores - peak) * (SCALE * LOG2E)).astype(jnp.bfloat16)
            mixed = dot(weights, values[:stop])
            result = (mixed[:, :HEADDIM] / mixed[:, HEADDIM:]).astype(jnp.bfloat16)
            for h in range(heads):
                out_ref[start:stop, h * HEADDIM : (h + 1) * HEADDIM] = result[
                    h * TILE : (h + 1) * TILE
                ]


MARK = jax.ShapeDtypeStruct((8, 128), jnp.float32)
IN_HBM = pl.BlockSpec(memory_space=pltpu.HBM)
ANYWHERE = pl.BlockSpec(memory_space=pl.ANY)
IN_VMEM = pl.BlockSpec(memory_space=pltpu.VMEM)


def prompt_attention(info, queries, pairs, first, steps, heads, earlier, after):
    length, width = queries.shape
    per_kv = GROUP // heads

    def q_map(i, info_ref):
        return (0, jnp.where(on_prefill(info_ref), i + first, 0))

    def kv_map(i, info_ref):
        return (0, jnp.where(on_prefill(info_ref), (i + first) // per_kv, 0))

    in_specs = [
        pl.BlockSpec((length, heads * HEADDIM), q_map),
        pl.BlockSpec((length, 2 * HEADDIM), kv_map),
    ]
    operands = [info, queries, pairs]
    aliases = {}
    if earlier is not None:
        in_specs.append(ANYWHERE)
        operands.append(earlier)
        aliases = {3: 0}
    return pl.pallas_call(
        functools.partial(prompt_kernel, heads),
        out_shape=(jax.ShapeDtypeStruct((length, width), jnp.bfloat16), MARK),
        grid_spec=pltpu.PrefetchScalarGridSpec(
            num_scalar_prefetch=1,
            grid=(steps,),
            in_specs=in_specs + [IN_HBM] * len(after),
            out_specs=(
                pl.BlockSpec((length, heads * HEADDIM), lambda i, info_ref: (0, i + first)),
                IN_HBM,
            ),
        ),
        input_output_aliases=aliases,
        compiler_params=pltpu.CompilerParams(vmem_limit_bytes=LARGE),
        cost_estimate=COST,
        name="prompt_attention",
    )(*operands, *after)


def head_queries(block, head):
    start = head * GROUP * HEADDIM
    return jnp.concatenate(
        [
            block[r : r + 1, start + g * HEADDIM : start + (g + 1) * HEADDIM]
            for r in range(block.shape[0])
            for g in range(GROUP)
        ],
        axis=0,
    ).astype(jnp.bfloat16)


def store_part(out_ref, head, mixed, peak, total):
    lane = lax.broadcasted_iota(jnp.int32, mixed.shape, 1)
    out_ref[head, :, :HEADDIM] = mixed
    out_ref[head, :, HEADDIM:] = jnp.where(lane < HEADDIM // 2, peak, total)


def merged(parts):
    peaks = [part[:, HEADDIM : HEADDIM + 1] for part in parts]
    peak = functools.reduce(jnp.maximum, peaks)
    factors = [jnp.exp(p - peak) for p in peaks]
    total = sum(part[:, -1:] * f for part, f in zip(parts, factors))
    mixed = sum(part[:, :HEADDIM] * f for part, f in zip(parts, factors))
    return mixed, peak, total


def cache_kernel(page_len, info_ref, table_ref, lengths_ref, q_ref, kv_ref, *rest):
    out_ref, _, count_ref = rest[-3:]
    rows, slots = table_ref.shape

    @pl.when(jnp.logical_and(jnp.logical_not(on_prefill(info_ref)), pl.program_id(0) == 0))
    def _():
        token = lax.broadcasted_iota(jnp.int32, (GROUP, count_ref.shape[1]), 1)
        page, offset = token // page_len, token % page_len
        for r in range(rows):
            count = jnp.zeros(token.shape, jnp.float32)
            for slot in range(slots):
                left = lengths_ref[r] - (info_ref[TP] * slots + slot) * page_len
                valid = jnp.logical_and(page == table_ref[r, slot], offset < left)
                count = count + jnp.where(valid, 1.0, 0.0)
            count_ref[r * GROUP : (r + 1) * GROUP] = count

    @pl.when(jnp.logical_not(on_prefill(info_ref)))
    def _():
        count = count_ref[...]
        here = count > 0.0
        block = q_ref[...].astype(jnp.float32)
        for head in range(out_ref.shape[0]):
            start = 2 * head * HEADDIM
            keys = kv_ref[:, start : start + HEADDIM]
            values = kv_ref[:, start + HEADDIM : start + 2 * HEADDIM]
            scores = dot_t(head_queries(block, head), keys) * SCALE
            scores = jnp.where(here, scores, NEG_FILL)
            peak = jnp.max(scores, axis=1, keepdims=True)
            weights = jnp.where(here, jnp.exp(scores - peak), 0.0)
            total = jnp.sum(weights * count, axis=1, keepdims=True)
            rounded = weights.astype(jnp.bfloat16).astype(jnp.float32) * count
            store_part(out_ref, head, dot(rounded.astype(jnp.bfloat16), values), peak, total)


def cache_attention(info, table, lengths, queries, pool, page_len, after):
    rows = queries.shape[0]
    tokens = pool.shape[0]
    steps = 2
    heads = KVHEADS // steps

    def step(n, info):
        return jnp.where(on_prefill(info), 0, n)

    return pl.pallas_call(
        functools.partial(cache_kernel, page_len),
        out_shape=(
            jax.ShapeDtypeStruct((KVHEADS, rows * GROUP, 2 * HEADDIM), jnp.float32),
            MARK,
        ),
        grid_spec=pltpu.PrefetchScalarGridSpec(
            num_scalar_prefetch=3,
            grid=(steps,),
            in_specs=[
                pl.BlockSpec((rows, heads * GROUP * HEADDIM), lambda n, info, *_: (0, step(n, info))),
                pl.BlockSpec((tokens, 2 * heads * HEADDIM), lambda n, info, *_: (0, step(n, info))),
            ]
            + [IN_HBM] * len(after),
            out_specs=(
                pl.BlockSpec(
                    (heads, rows * GROUP, 2 * HEADDIM), lambda n, info, *_: (step(n, info), 0, 0)
                ),
                IN_HBM,
            ),
            scratch_shapes=[pltpu.VMEM((rows * GROUP, tokens), jnp.float32)],
        ),
        compiler_params=pltpu.CompilerParams(vmem_limit_bytes=LARGE),
        cost_estimate=COST,
        name="cache_attention",
    )(info, table, lengths, queries, pool, *after)


def rows_part(queries, rows, out_ref, earlier_ref):
    block = queries[...].astype(jnp.float32)
    heads = rows[0].shape[1] // (2 * HEADDIM)
    places = [(rows[head // heads], 2 * (head % heads) * HEADDIM) for head in range(KVHEADS)]
    scores = [
        dot_t(head_queries(block, head), held[:, start : start + HEADDIM]) * SCALE
        for head, (held, start) in enumerate(places)
    ]
    peaks = [jnp.max(score, axis=1, keepdims=True) for score in scores]
    weights = [jnp.exp(score - peak) for score, peak in zip(scores, peaks)]
    totals = [jnp.sum(weight, axis=1, keepdims=True) for weight in weights]
    mixes = [
        dot(weight.astype(jnp.bfloat16), held[:, start + HEADDIM : start + 2 * HEADDIM])
        for weight, (held, start) in zip(weights, places)
    ]
    for head in range(KVHEADS):
        store_part(out_ref, head, mixes[head], peaks[head], totals[head])
        if earlier_ref is not None:
            store_part(out_ref, head, *merged([out_ref[head], earlier_ref[head]]))


def flat_rows(pieces):
    wide = [piece.astype(jnp.float32).reshape(-1, piece.shape[-1]) for piece in pieces]
    return jnp.concatenate(wide, axis=0).astype(jnp.bfloat16)


def whole_rows_kernel(info_ref, q_ref, rows_ref, out_ref):
    rows_part(q_ref, [rows_ref[...]], out_ref, None)


def far_rows_kernel(info_ref, q_ref, slots_ref, out_ref, held_ref, sem):
    @pl.when(jnp.logical_not(on_prefill(info_ref)))
    def _():
        copy = pltpu.make_async_copy(slots_ref, held_ref, sem)
        copy.start()
        copy.wait()
        half = 2 * PAIRS
        rows = [
            flat_rows([held_ref[t * half + i] for i in range(half)]) for t in range(2)
        ]
        rows_part(q_ref, rows, out_ref, None)


def near_rows_kernel(info_ref, q_ref, earlier_ref, *refs):
    *part_refs, out_ref = refs

    @pl.when(jnp.logical_not(on_prefill(info_ref)))
    def _():
        rows = [flat_rows([part[t] for part in part_refs]) for t in range(2)]
        rows_part(q_ref, rows, out_ref, earlier_ref)


def arrival_part(kernel, info, query, operands, places, scratch, name):
    return pl.pallas_call(
        kernel,
        out_shape=jax.ShapeDtypeStruct((KVHEADS, GROUP, 2 * HEADDIM), jnp.float32),
        grid_spec=pltpu.PrefetchScalarGridSpec(
            num_scalar_prefetch=1,
            grid=(1,),
            in_specs=[IN_VMEM] + places,
            out_specs=IN_VMEM,
            scratch_shapes=scratch,
        ),
        compiler_params=pltpu.CompilerParams(vmem_limit_bytes=VMEM),
        cost_estimate=COST,
        name=name,
    )(info, query, *operands)


def combine_kernel(count, info_ref, *refs):
    part_refs, out_ref = refs[:count], refs[-2]

    @pl.when(on_prefill(info_ref))
    def _():
        out_ref[...] = jnp.zeros_like(out_ref)

    @pl.when(jnp.logical_not(on_prefill(info_ref)))
    def _():
        results = []
        for head in range(KVHEADS):
            if count == 2:
                here, there = part_refs[0][head], part_refs[1][head]
                first = info_ref[TP] == 0
                parts = [jnp.where(first, here, there), jnp.where(first, there, here)]
            else:
                parts = [part_refs[0][n, head] for n in range(part_refs[0].shape[0])]
            mixed, _, total = merged(parts)
            results.append(mixed / total)
        for r in range(out_ref.shape[0]):
            row = [
                results[head][r * GROUP + g : r * GROUP + g + 1]
                for head in range(KVHEADS)
                for g in range(GROUP)
            ]
            out_ref[r : r + 1] = jnp.concatenate(row, axis=1).astype(jnp.bfloat16)


def combine_parts(info, parts, after=()):
    rows = parts[0].shape[-2] // GROUP
    return pl.pallas_call(
        functools.partial(combine_kernel, len(parts)),
        out_shape=(jax.ShapeDtypeStruct((rows, QHEADS * HEADDIM), jnp.bfloat16), MARK),
        grid_spec=pltpu.PrefetchScalarGridSpec(
            num_scalar_prefetch=1,
            grid=(1,),
            in_specs=[IN_VMEM] * len(parts) + [IN_HBM] * len(after),
            out_specs=(IN_VMEM, IN_HBM),
        ),
        compiler_params=pltpu.CompilerParams(vmem_limit_bytes=VMEM),
        cost_estimate=COST,
        name="combine_parts",
    )(info, *parts, *after)


def relay_handoff(pairs, assignment, inst_count):
    half = inst_count // 2
    decode_ids = jnp.arange(half, dtype=jnp.int32)
    matches = assignment[None, :] == decode_ids[:, None]
    source = jnp.sum(jnp.where(matches, decode_ids[None, :], 0), axis=1).astype(jnp.int32)
    moved = lax.all_to_all(pairs, "tp", split_axis=0, concat_axis=1, tiled=True)
    lanes = 1024 if moved.size % (inst_count * 1024) == 0 else HEADDIM
    pieces = moved.reshape(inst_count, -1, lanes)
    spread = lax.all_to_all(pieces, "inst", split_axis=0, concat_axis=0, tiled=True)
    chosen = jnp.stack(
        [lax.dynamic_index_in_dim(spread, source[d], 0, False) for d in range(half)], axis=0
    )
    outgoing = jnp.concatenate([jnp.zeros_like(chosen), chosen], axis=0)
    delivered = lax.all_to_all(outgoing, "inst", split_axis=0, concat_axis=0, tiled=True)
    return delivered.reshape(moved.shape)


UNIT = 8
PAIRS = 4
PREFILL, DECODE = True, False


def copy_kernel(plan, side, counts, info_ref, *refs):
    inputs, marks, outputs, stages = counts
    sources, targets = refs[:inputs], refs[inputs + marks : inputs + marks + outputs]
    held, sems = refs[-1 - stages : -1], refs[-1]

    @pl.when(on_prefill(info_ref) == side)
    def _():
        started = []
        for source, target in zip(sources, held):
            started.append(pltpu.make_async_copy(source, target, sems.at[len(started)]))
        for copy in started:
            copy.start()
        for copy in started:
            copy.wait()
        started = []
        for source, target in plan(info_ref, held or sources, targets):
            started.append(pltpu.make_async_copy(source, target, sems.at[len(started)]))
        for copy in started:
            copy.start()
        for copy in started:
            copy.wait()


def copies(plan, number, info, operands, shapes, name, after=(), stage=False, side=PREFILL):
    held = [pltpu.VMEM(x.shape, x.dtype) for x in operands] if stage else []
    return pl.pallas_call(
        functools.partial(copy_kernel, plan, side, (len(operands), len(after), len(shapes), len(held))),
        out_shape=tuple(jax.ShapeDtypeStruct(shape, jnp.bfloat16) for shape in shapes),
        grid_spec=pltpu.PrefetchScalarGridSpec(
            num_scalar_prefetch=1,
            grid=(1,),
            in_specs=[ANYWHERE] * len(operands) + [IN_HBM] * len(after),
            out_specs=tuple([ANYWHERE] * len(shapes)),
            scratch_shapes=held + [pltpu.SemaphoreType.DMA((number,))],
        ),
        compiler_params=pltpu.CompilerParams(vmem_limit_bytes=MEDIUM if stage else SMALL),
        cost_estimate=COST,
        name=name,
    )(info, *operands, *after)


def relay_slots_kernel(far, info_ref, keep_ref, recv_ref, out_ref, sems):
    half = 2 * PAIRS

    @pl.when(jnp.logical_not(on_prefill(info_ref)))
    def _():
        here = order(info_ref)
        waits = []
        for d in range(half):
            source = source_of(info_ref, d)
            same = lax.rem(source, 2) == lax.rem(here, 2)
            shift = lax.rem(lax.div(here, 2) + PAIRS - lax.div(source, 2), PAIRS)
            for tau in range(2):
                slot = tau * half + d
                target = out_ref.at[slot]
                mine = pltpu.make_async_copy(keep_ref.at[shift, tau], target, sems.at[slot])
                other = pltpu.make_async_copy(recv_ref.at[shift, tau], target, sems.at[slot])
                pl.when(same)(mine.start)
                pl.when(jnp.logical_not(same))(other.start)
                waits.append(mine)
        for copy in waits:
            copy.wait()


def rows_kernel(near, far, info_ref, slots_ref, *refs):
    *parts, out_ref, zero_ref, held_ref, sems = refs
    half = 2 * PAIRS
    width = slots_ref.shape[-1]
    near_all = near * half

    @pl.when(jnp.logical_not(on_prefill(info_ref)))
    def _():
        last = sems.shape[0] - 1
        staged = pltpu.make_async_copy(slots_ref, held_ref, sems.at[last])
        staged.start()
        waits = []
        for t in range(2):
            for s, part in enumerate(parts):
                pair = lax.rem(lax.div(order(info_ref), 2) + PAIRS - s, PAIRS)
                target = out_ref.at[pl.ds(pair * 2 * near, 2 * near), :, pl.ds(t * width, width)]
                waits.append(pltpu.make_async_copy(part.at[t], target, sems.at[len(waits)]))
                waits[-1].start()
        staged.wait()
        for t in range(2):
            for i in range(half):
                target = out_ref.at[pl.ds(near_all + i * far, far), :, pl.ds(t * width, width)]
                waits.append(
                    pltpu.make_async_copy(held_ref.at[t * half + i], target, sems.at[len(waits)])
                )
                waits[-1].start()
        for copy in waits:
            copy.wait()

    @pl.when(on_prefill(info_ref))
    def _():
        zero_ref[...] = jnp.zeros_like(zero_ref)
        size = zero_ref.shape[0]
        waits = []
        for n in range(out_ref.shape[0] // size):
            target = out_ref.at[pl.ds(n * size, size)]
            waits.append(pltpu.make_async_copy(zero_ref, target, sems.at[n]))
        for copy in waits:
            copy.start()
        for copy in waits:
            copy.wait()


def two_way_handoff(pairs, info, always, arrival_query, prompt_part, cached, exchanged):
    half = 2 * PAIRS
    rows, width = pairs.shape
    units = rows // (2 * UNIT)
    far_all = units * 2 // (5 * half) * half
    near_all = units - far_all
    near, far = near_all // half, far_all // half
    block = (UNIT, width)
    by_unit = pairs.reshape((rows // UNIT,) + block)
    groups = [[base + 2 * i + tau for tau in range(2) for i in range(half)] for base in (0, 2 * half)]

    def crossing(array, s):
        hops = [
            (2 * p + k, half + 2 * ((p + s) % PAIRS) + k) for p in range(PAIRS) for k in range(2)
        ]
        return lax.ppermute(array, "inst", hops)

    def beside(array, base):
        return lax.ppermute(array, "inst", [(base + i, base + (i ^ 1)) for i in range(half)])

    def spread_out(array):
        return lax.all_to_all(
            array, ("inst", "tp"), 0, 0, axis_index_groups=groups, tiled=True
        )

    def cut_near(pre, sources, targets):
        return [
            (sources[0].at[pl.ds(tau * units, near_all)], targets[0].at[tau]) for tau in range(2)
        ]

    def cut_far(pre, sources, targets):
        plan = []
        for s in range(PAIRS):
            start = near_all + lax.rem(lax.div(order(pre), 2) + s, PAIRS) * (2 * far)
            for tau in range(2):
                plan.append((sources[0].at[pl.ds(tau * units + start, 2 * far)], targets[s].at[tau]))
        return plan

    def for_neighbour(pre, sources, targets):
        plan = []
        for s in range(PAIRS):
            receiver = lax.rem(lax.div(order(pre), 2) + s, PAIRS) * 2 + 1 - lax.rem(order(pre), 2)
            for t in range(2):
                origin = t * half + source_of(pre, receiver)
                plan.append((sources[0].at[origin], targets[0].at[s, t]))
        return plan

    def for_receivers(pre, sources, targets):
        plan = []
        for s in range(PAIRS):
            receiver = lax.rem(lax.div(order(pre), 2) + s, PAIRS) * 2 + lax.rem(order(pre), 2)
            for t in range(2):
                origin = t * half + source_of(pre, receiver)
                mine = targets[s].at[t, pl.ds(lax.rem(order(pre), 2) * near, near)]
                other = targets[s].at[t, pl.ds((1 - lax.rem(order(pre), 2)) * near, near)]
                plan.append((sources[0].at[origin], mine))
                plan.append((sources[1].at[s, t], other))
        return plan

    def split(pre, sources, targets):
        plan = []
        for s in range(PAIRS):
            for tau in range(2):
                mine = sources[s].at[tau, pl.ds(lax.rem(order(pre), 2) * far, far)]
                other = sources[s].at[tau, pl.ds((1 - lax.rem(order(pre), 2)) * far, far)]
                plan.append((mine, targets[0].at[s, tau]))
                plan.append((other, targets[1].at[s, tau]))
        return plan

    near_shape = (2, 2 * near) + block

    def first_stage(spread, *marks):
        (outgoing,) = copies(
            for_neighbour, 2 * PAIRS, info, [spread], [(PAIRS, 2, near) + block], "for_neighbour", marks
        )
        incoming = beside(outgoing, 0)
        return copies(
            for_receivers, 4 * PAIRS, info, [spread, incoming], [near_shape] * PAIRS, "for_receivers"
        )

    def second_stage(prompt, part, other, *far_here):
        keep, give = copies(
            split,
            4 * PAIRS,
            info,
            list(far_here),
            [(PAIRS, 2, far) + block] * 2,
            "split_relays",
            stage=True,
            side=DECODE,
        )
        taken = beside(give, half)
        slots = pl.pallas_call(
            functools.partial(relay_slots_kernel, far),
            out_shape=jax.ShapeDtypeStruct((2 * half, far) + block, jnp.bfloat16),
            grid_spec=pltpu.PrefetchScalarGridSpec(
                num_scalar_prefetch=1,
                grid=(1,),
                in_specs=[ANYWHERE] * 2,
                out_specs=ANYWHERE,
                scratch_shapes=[pltpu.SemaphoreType.DMA((2 * half,))],
            ),
            compiler_params=pltpu.CompilerParams(vmem_limit_bytes=SMALL),
            cost_estimate=COST,
            name="relay_slots",
        )(info, keep, taken)
        prompt, mark = prompt_part(1, prompt, [slots])
        decode_out, _ = combine_parts(info, [part, other], [mark])
        slots = spread_out(slots)
        arrival = arrival_part(
            far_rows_kernel,
            info,
            arrival_query,
            [slots],
            [ANYWHERE],
            [pltpu.VMEM(slots.shape, slots.dtype), pltpu.SemaphoreType.DMA],
            "far_rows",
        )
        return prompt, slots, decode_out, arrival

    def staged(stage, *operands):
        def never(*operands):
            outs = [jnp.zeros(out.shape, out.dtype) for out in jax.eval_shape(stage, *operands)]
            return tuple(outs) if stage is first_stage else (operands[0], *outs[1:])

        return lax.cond(always, lambda *operands: tuple(stage(*operands)), never, *operands)

    (near_rows,) = copies(
        cut_near, 2, info, [by_unit], [(2, near_all) + block], "cut_near", stage=True
    )
    far_parts = copies(
        cut_far, 2 * PAIRS, info, [by_unit], [(2, 2 * far) + block] * PAIRS, "cut_far", [near_rows]
    )
    spread = spread_out(near_rows.reshape((2 * half, near) + block))
    far_here = [crossing(part, s) for s, part in enumerate(far_parts)]
    part, mark = cached([near_rows])
    prompt, mark = prompt_part(0, None, [mark])
    other = exchanged(part)
    near_parts = staged(first_stage, spread, mark, other)
    near_here = [crossing(near_part, s) for s, near_part in enumerate(near_parts)]
    prompt, slots, decode_out, arrival = staged(second_stage, prompt, part, other, *far_here)
    arrival = arrival_part(
        near_rows_kernel,
        info,
        arrival_query,
        [arrival, *near_here],
        [IN_VMEM] * (PAIRS + 1),
        [],
        "near_rows",
    )
    handed = pl.pallas_call(
        functools.partial(rows_kernel, near, far),
        out_shape=jax.ShapeDtypeStruct((units, UNIT, 2 * width), jnp.bfloat16),
        grid_spec=pltpu.PrefetchScalarGridSpec(
            num_scalar_prefetch=1,
            grid=(1,),
            in_specs=[ANYWHERE] * (PAIRS + 1),
            out_specs=ANYWHERE,
            scratch_shapes=[
                pltpu.VMEM((half, UNIT, 2 * width), jnp.bfloat16),
                pltpu.VMEM(slots.shape, slots.dtype),
                pltpu.SemaphoreType.DMA((2 * (half + PAIRS) + 1,)),
            ],
        ),
        compiler_params=pltpu.CompilerParams(vmem_limit_bytes=MEDIUM),
        cost_estimate=COST,
        name="rows",
    )(info, slots, *near_here)
    arrival_out, _ = combine_parts(info, [arrival, exchanged(arrival)])
    return prompt, handed.reshape(rows // 2, 2 * width), decode_out, arrival_out


def shards(
    prompt_query,
    prompt_pairs,
    decode_query,
    arrival_query,
    cache_pool,
    page_table,
    lengths,
    assignment,
):
    inst_count = lax.axis_size("inst")
    tp_count = lax.axis_size("tp")
    half = inst_count // 2
    inst = lax.axis_index("inst")
    tp_index = lax.axis_index("tp")
    info = jnp.concatenate([jnp.stack([inst, tp_index]), assignment])
    pages, page_len = cache_pool.shape[0], cache_pool.shape[1]
    by_token = cache_pool.reshape(pages * page_len, -1)

    def cached(after=()):
        return cache_attention(info, page_table, lengths, decode_query, by_token, page_len, after)

    def exchanged(part):
        return lax.ppermute(part, "tp", [(0, 1), (1, 0)])

    def combined(part):
        return combine_parts(info, [lax.all_gather(part, "tp")])[0]

    heads = GROUP // 2
    steps = prompt_query.shape[1] // (heads * HEADDIM)

    def prompt_part(first, last, earlier, after=()):
        return prompt_attention(
            info, prompt_query, prompt_pairs, first, last - first, heads, earlier, after
        )

    row_units = prompt_pairs.shape[0] // (2 * UNIT)
    if inst_count == 4 * PAIRS and tp_count == 2 and row_units == 5 * half and steps == 8:
        cuts = (0, 2, 8)
        return two_way_handoff(
            prompt_pairs,
            info,
            assignment[0] >= 0,
            arrival_query,
            lambda n, earlier, after: prompt_part(cuts[n], cuts[n + 1], earlier, after),
            cached,
            exchanged,
        )
    handed = relay_handoff(prompt_pairs, assignment, inst_count)
    arrival = arrival_part(
        whole_rows_kernel, info, arrival_query, [handed], [IN_VMEM], [], "whole_rows"
    )
    prefill_out, _ = prompt_part(0, steps, None)
    return prefill_out, handed, combined(cached()[0]), combined(arrival)


def solution(mesh):
    return jax.shard_map(
        shards,
        mesh=mesh,
        in_specs=(
            P("inst", "tp"),
            P("inst", "tp"),
            P("inst", None),
            P("inst", None),
            P(("inst", "tp"), None, None),
            P("inst", "tp"),
            P("inst"),
            P(),
        ),
        out_specs=(P("inst", "tp"), P(("inst", "tp"), None), P("inst", None), P("inst", None)),
        check_vma=False,
    )
```

```python
import functools

import jax
import jax.numpy as jnp
from jax import lax
from jax.experimental import pallas as pl
from jax.experimental.pallas import tpu as pltpu
from jax.sharding import PartitionSpec as P

QHEADS = 64
KVHEADS = 8
HEADDIM = 128
GROUP = QHEADS // KVHEADS
SCALE = HEADDIM ** (-0.5)
LOG2E = 1.4426950408889634
NEG_FILL = -1e30
TILE = 128
VMEM = 24 * 1024 * 1024
SMALL = 1024 * 1024
MEDIUM = 8 * 1024 * 1024
LARGE = 57 * 1024 * 1024
COST = pl.CostEstimate(flops=1, bytes_accessed=1, transcendentals=0)


INST, TP, FIRST = 0, 1, 2


def on_prefill(info):
    return info[INST] < info.shape[0] - FIRST


def order(info):
    half = info.shape[0] - FIRST
    return info[INST] - jnp.where(on_prefill(info), 0, half)


def source_of(info, receiver):
    half = info.shape[0] - FIRST
    found = jnp.int32(0)
    for p in range(half):
        found = jnp.where(info[FIRST + p] == receiver, p, found)
    return found


def dot_t(a, b):
    return lax.dot_general(a, b, (((1,), (1,)), ((), ())), preferred_element_type=jnp.float32)


def dot(a, b):
    return lax.dot_general(a, b, (((1,), (0,)), ((), ())), preferred_element_type=jnp.float32)


def prompt_kernel(heads, info_ref, q_ref, kv_ref, *rest):
    out_ref = rest[-2]
    length = q_ref.shape[0]

    @pl.when(jnp.logical_not(on_prefill(info_ref)))
    def _():
        out_ref[...] = jnp.zeros_like(out_ref)

    @pl.when(on_prefill(info_ref))
    def _():
        rows_all = lax.broadcasted_iota(jnp.int32, (TILE, TILE), 0)
        cols_all = lax.broadcasted_iota(jnp.int32, (TILE, TILE), 1)
        below = jnp.concatenate([rows_all >= cols_all] * heads, axis=0)
        ones = jnp.ones((length, HEADDIM), jnp.bfloat16)
        values = jnp.concatenate([kv_ref[:, HEADDIM:], ones], axis=1)
        for start in range(0, length, TILE):
            stop = start + TILE
            queries = jnp.concatenate(
                [q_ref[start:stop, h * HEADDIM : (h + 1) * HEADDIM] for h in range(heads)], axis=0
            )
            scores = dot_t(queries, kv_ref[:stop, :HEADDIM])
            last = jnp.where(below, scores[:, start:], NEG_FILL)
            scores = jnp.concatenate([scores[:, :start], last], axis=1) if start else last
            peak = jnp.max(scores, axis=1, keepdims=True)
            weights = jnp.exp2((scores - peak) * (SCALE * LOG2E)).astype(jnp.bfloat16)
            mixed = dot(weights, values[:stop])
            result = (mixed[:, :HEADDIM] / mixed[:, HEADDIM:]).astype(jnp.bfloat16)
            for h in range(heads):
                out_ref[start:stop, h * HEADDIM : (h + 1) * HEADDIM] = result[
                    h * TILE : (h + 1) * TILE
                ]


MARK = jax.ShapeDtypeStruct((8, 128), jnp.float32)
IN_HBM = pl.BlockSpec(memory_space=pltpu.HBM)
ANYWHERE = pl.BlockSpec(memory_space=pl.ANY)
IN_VMEM = pl.BlockSpec(memory_space=pltpu.VMEM)


def prompt_attention(info, queries, pairs, first, steps, heads, earlier, after):
    length, width = queries.shape
    per_kv = GROUP // heads

    def q_map(i, info_ref):
        return (0, jnp.where(on_prefill(info_ref), i + first, 0))

    def kv_map(i, info_ref):
        return (0, jnp.where(on_prefill(info_ref), (i + first) // per_kv, 0))

    in_specs = [
        pl.BlockSpec((length, heads * HEADDIM), q_map),
        pl.BlockSpec((length, 2 * HEADDIM), kv_map),
    ]
    operands = [info, queries, pairs]
    aliases = {}
    if earlier is not None:
        in_specs.append(ANYWHERE)
        operands.append(earlier)
        aliases = {3: 0}
    return pl.pallas_call(
        functools.partial(prompt_kernel, heads),
        out_shape=(jax.ShapeDtypeStruct((length, width), jnp.bfloat16), MARK),
        grid_spec=pltpu.PrefetchScalarGridSpec(
            num_scalar_prefetch=1,
            grid=(steps,),
            in_specs=in_specs + [IN_HBM] * len(after),
            out_specs=(
                pl.BlockSpec((length, heads * HEADDIM), lambda i, info_ref: (0, i + first)),
                IN_HBM,
            ),
        ),
        input_output_aliases=aliases,
        compiler_params=pltpu.CompilerParams(vmem_limit_bytes=LARGE),
        cost_estimate=COST,
        name="prompt_attention",
    )(*operands, *after)


def head_queries(block, head):
    start = head * GROUP * HEADDIM
    return jnp.concatenate(
        [
            block[r : r + 1, start + g * HEADDIM : start + (g + 1) * HEADDIM]
            for r in range(block.shape[0])
            for g in range(GROUP)
        ],
        axis=0,
    ).astype(jnp.bfloat16)


def store_part(out_ref, head, mixed, peak, total):
    lane = lax.broadcasted_iota(jnp.int32, mixed.shape, 1)
    out_ref[head, :, :HEADDIM] = mixed
    out_ref[head, :, HEADDIM:] = jnp.where(lane < HEADDIM // 2, peak, total)


def merged(parts):
    peaks = [part[:, HEADDIM : HEADDIM + 1] for part in parts]
    peak = functools.reduce(jnp.maximum, peaks)
    factors = [jnp.exp(p - peak) for p in peaks]
    total = sum(part[:, -1:] * f for part, f in zip(parts, factors))
    mixed = sum(part[:, :HEADDIM] * f for part, f in zip(parts, factors))
    return mixed, peak, total


def cache_kernel(page_len, info_ref, table_ref, lengths_ref, q_ref, kv_ref, *rest):
    out_ref, _, count_ref = rest[-3:]
    rows, slots = table_ref.shape

    @pl.when(jnp.logical_and(jnp.logical_not(on_prefill(info_ref)), pl.program_id(0) == 0))
    def _():
        token = lax.broadcasted_iota(jnp.int32, (GROUP, count_ref.shape[1]), 1)
        page, offset = token // page_len, token % page_len
        for r in range(rows):
            count = jnp.zeros(token.shape, jnp.float32)
            for slot in range(slots):
                left = lengths_ref[r] - (info_ref[TP] * slots + slot) * page_len
                valid = jnp.logical_and(page == table_ref[r, slot], offset < left)
                count = count + jnp.where(valid, 1.0, 0.0)
            count_ref[r * GROUP : (r + 1) * GROUP] = count

    @pl.when(jnp.logical_not(on_prefill(info_ref)))
    def _():
        count = count_ref[...]
        here = count > 0.0
        block = q_ref[...].astype(jnp.float32)
        for head in range(out_ref.shape[0]):
            start = 2 * head * HEADDIM
            keys = kv_ref[:, start : start + HEADDIM]
            values = kv_ref[:, start + HEADDIM : start + 2 * HEADDIM]
            scores = dot_t(head_queries(block, head), keys) * SCALE
            scores = jnp.where(here, scores, NEG_FILL)
            peak = jnp.max(scores, axis=1, keepdims=True)
            weights = jnp.where(here, jnp.exp(scores - peak), 0.0)
            total = jnp.sum(weights * count, axis=1, keepdims=True)
            rounded = weights.astype(jnp.bfloat16).astype(jnp.float32) * count
            store_part(out_ref, head, dot(rounded.astype(jnp.bfloat16), values), peak, total)


def cache_attention(info, table, lengths, queries, pool, page_len, after):
    rows = queries.shape[0]
    tokens = pool.shape[0]
    steps = 2
    heads = KVHEADS // steps

    def step(n, info):
        return jnp.where(on_prefill(info), 0, n)

    return pl.pallas_call(
        functools.partial(cache_kernel, page_len),
        out_shape=(
            jax.ShapeDtypeStruct((KVHEADS, rows * GROUP, 2 * HEADDIM), jnp.float32),
            MARK,
        ),
        grid_spec=pltpu.PrefetchScalarGridSpec(
            num_scalar_prefetch=3,
            grid=(steps,),
            in_specs=[
                pl.BlockSpec((rows, heads * GROUP * HEADDIM), lambda n, info, *_: (0, step(n, info))),
                pl.BlockSpec((tokens, 2 * heads * HEADDIM), lambda n, info, *_: (0, step(n, info))),
            ]
            + [IN_HBM] * len(after),
            out_specs=(
                pl.BlockSpec(
                    (heads, rows * GROUP, 2 * HEADDIM), lambda n, info, *_: (step(n, info), 0, 0)
                ),
                IN_HBM,
            ),
            scratch_shapes=[pltpu.VMEM((rows * GROUP, tokens), jnp.float32)],
        ),
        compiler_params=pltpu.CompilerParams(vmem_limit_bytes=LARGE),
        cost_estimate=COST,
        name="cache_attention",
    )(info, table, lengths, queries, pool, *after)


def rows_part(queries, rows, out_ref, earlier_ref):
    block = queries[...].astype(jnp.float32)
    heads = rows[0].shape[1] // (2 * HEADDIM)
    places = [(rows[head // heads], 2 * (head % heads) * HEADDIM) for head in range(KVHEADS)]
    scores = [
        dot_t(head_queries(block, head), held[:, start : start + HEADDIM]) * SCALE
        for head, (held, start) in enumerate(places)
    ]
    peaks = [jnp.max(score, axis=1, keepdims=True) for score in scores]
    weights = [jnp.exp(score - peak) for score, peak in zip(scores, peaks)]
    totals = [jnp.sum(weight, axis=1, keepdims=True) for weight in weights]
    mixes = [
        dot(weight.astype(jnp.bfloat16), held[:, start + HEADDIM : start + 2 * HEADDIM])
        for weight, (held, start) in zip(weights, places)
    ]
    for head in range(KVHEADS):
        store_part(out_ref, head, mixes[head], peaks[head], totals[head])
        if earlier_ref is not None:
            store_part(out_ref, head, *merged([out_ref[head], earlier_ref[head]]))


def flat_rows(pieces):
    wide = [piece.astype(jnp.float32).reshape(-1, piece.shape[-1]) for piece in pieces]
    return jnp.concatenate(wide, axis=0).astype(jnp.bfloat16)


def whole_rows_kernel(info_ref, q_ref, rows_ref, out_ref):
    rows_part(q_ref, [rows_ref[...]], out_ref, None)


def far_rows_kernel(info_ref, q_ref, slots_ref, out_ref, held_ref, sem):
    @pl.when(jnp.logical_not(on_prefill(info_ref)))
    def _():
        copy = pltpu.make_async_copy(slots_ref, held_ref, sem)
        copy.start()
        copy.wait()
        half = 2 * PAIRS
        rows = [
            flat_rows([held_ref[t * half + i] for i in range(half)]) for t in range(2)
        ]
        rows_part(q_ref, rows, out_ref, None)


def near_rows_kernel(info_ref, q_ref, earlier_ref, *refs):
    *part_refs, out_ref = refs

    @pl.when(jnp.logical_not(on_prefill(info_ref)))
    def _():
        rows = [flat_rows([part[t] for part in part_refs]) for t in range(2)]
        rows_part(q_ref, rows, out_ref, earlier_ref)


def arrival_part(kernel, info, query, operands, places, scratch, name):
    return pl.pallas_call(
        kernel,
        out_shape=jax.ShapeDtypeStruct((KVHEADS, GROUP, 2 * HEADDIM), jnp.float32),
        grid_spec=pltpu.PrefetchScalarGridSpec(
            num_scalar_prefetch=1,
            grid=(1,),
            in_specs=[IN_VMEM] + places,
            out_specs=IN_VMEM,
            scratch_shapes=scratch,
        ),
        compiler_params=pltpu.CompilerParams(vmem_limit_bytes=VMEM),
        cost_estimate=COST,
        name=name,
    )(info, query, *operands)


def combine_kernel(count, info_ref, *refs):
    part_refs, out_ref = refs[:count], refs[-2]

    @pl.when(on_prefill(info_ref))
    def _():
        out_ref[...] = jnp.zeros_like(out_ref)

    @pl.when(jnp.logical_not(on_prefill(info_ref)))
    def _():
        results = []
        for head in range(KVHEADS):
            if count == 2:
                here, there = part_refs[0][head], part_refs[1][head]
                first = info_ref[TP] == 0
                parts = [jnp.where(first, here, there), jnp.where(first, there, here)]
            else:
                parts = [part_refs[0][n, head] for n in range(part_refs[0].shape[0])]
            mixed, _, total = merged(parts)
            results.append(mixed / total)
        for r in range(out_ref.shape[0]):
            row = [
                results[head][r * GROUP + g : r * GROUP + g + 1]
                for head in range(KVHEADS)
                for g in range(GROUP)
            ]
            out_ref[r : r + 1] = jnp.concatenate(row, axis=1).astype(jnp.bfloat16)


def combine_parts(info, parts, after=()):
    rows = parts[0].shape[-2] // GROUP
    return pl.pallas_call(
        functools.partial(combine_kernel, len(parts)),
        out_shape=(jax.ShapeDtypeStruct((rows, QHEADS * HEADDIM), jnp.bfloat16), MARK),
        grid_spec=pltpu.PrefetchScalarGridSpec(
            num_scalar_prefetch=1,
            grid=(1,),
            in_specs=[IN_VMEM] * len(parts) + [IN_HBM] * len(after),
            out_specs=(IN_VMEM, IN_HBM),
        ),
        compiler_params=pltpu.CompilerParams(vmem_limit_bytes=VMEM),
        cost_estimate=COST,
        name="combine_parts",
    )(info, *parts, *after)


def relay_handoff(pairs, assignment, inst_count):
    half = inst_count // 2
    decode_ids = jnp.arange(half, dtype=jnp.int32)
    matches = assignment[None, :] == decode_ids[:, None]
    source = jnp.sum(jnp.where(matches, decode_ids[None, :], 0), axis=1).astype(jnp.int32)
    moved = lax.all_to_all(pairs, "tp", split_axis=0, concat_axis=1, tiled=True)
    lanes = 1024 if moved.size % (inst_count * 1024) == 0 else HEADDIM
    pieces = moved.reshape(inst_count, -1, lanes)
    spread = lax.all_to_all(pieces, "inst", split_axis=0, concat_axis=0, tiled=True)
    chosen = jnp.stack(
        [lax.dynamic_index_in_dim(spread, source[d], 0, False) for d in range(half)], axis=0
    )
    outgoing = jnp.concatenate([jnp.zeros_like(chosen), chosen], axis=0)
    delivered = lax.all_to_all(outgoing, "inst", split_axis=0, concat_axis=0, tiled=True)
    return delivered.reshape(moved.shape)


UNIT = 8
PAIRS = 4
PREFILL, DECODE = True, False


def copy_kernel(plan, side, counts, info_ref, *refs):
    inputs, marks, outputs, stages = counts
    sources, targets = refs[:inputs], refs[inputs + marks : inputs + marks + outputs]
    held, sems = refs[-1 - stages : -1], refs[-1]

    @pl.when(on_prefill(info_ref) == side)
    def _():
        started = []
        for source, target in zip(sources, held):
            started.append(pltpu.make_async_copy(source, target, sems.at[len(started)]))
        for copy in started:
            copy.start()
        for copy in started:
            copy.wait()
        started = []
        for source, target in plan(info_ref, held or sources, targets):
            started.append(pltpu.make_async_copy(source, target, sems.at[len(started)]))
        for copy in started:
            copy.start()
        for copy in started:
            copy.wait()


def copies(plan, number, info, operands, shapes, name, after=(), stage=False, side=PREFILL):
    held = [pltpu.VMEM(x.shape, x.dtype) for x in operands] if stage else []
    return pl.pallas_call(
        functools.partial(copy_kernel, plan, side, (len(operands), len(after), len(shapes), len(held))),
        out_shape=tuple(jax.ShapeDtypeStruct(shape, jnp.bfloat16) for shape in shapes),
        grid_spec=pltpu.PrefetchScalarGridSpec(
            num_scalar_prefetch=1,
            grid=(1,),
            in_specs=[ANYWHERE] * len(operands) + [IN_HBM] * len(after),
            out_specs=tuple([ANYWHERE] * len(shapes)),
            scratch_shapes=held + [pltpu.SemaphoreType.DMA((number,))],
        ),
        compiler_params=pltpu.CompilerParams(vmem_limit_bytes=MEDIUM if stage else SMALL),
        cost_estimate=COST,
        name=name,
    )(info, *operands, *after)


def relay_slots_kernel(far, info_ref, keep_ref, recv_ref, out_ref, sems):
    half = 2 * PAIRS

    @pl.when(jnp.logical_not(on_prefill(info_ref)))
    def _():
        here = order(info_ref)
        waits = []
        for d in range(half):
            source = source_of(info_ref, d)
            same = lax.rem(source, 2) == lax.rem(here, 2)
            shift = lax.rem(lax.div(here, 2) + PAIRS - lax.div(source, 2), PAIRS)
            for tau in range(2):
                slot = tau * half + d
                target = out_ref.at[slot]
                mine = pltpu.make_async_copy(keep_ref.at[shift, tau], target, sems.at[slot])
                other = pltpu.make_async_copy(recv_ref.at[shift, tau], target, sems.at[slot])
                pl.when(same)(mine.start)
                pl.when(jnp.logical_not(same))(other.start)
                waits.append(mine)
        for copy in waits:
            copy.wait()


def rows_kernel(near, far, info_ref, slots_ref, *refs):
    *parts, out_ref, zero_ref, held_ref, sems = refs
    half = 2 * PAIRS
    width = slots_ref.shape[-1]
    near_all = near * half

    @pl.when(jnp.logical_not(on_prefill(info_ref)))
    def _():
        last = sems.shape[0] - 1
        staged = pltpu.make_async_copy(slots_ref, held_ref, sems.at[last])
        staged.start()
        waits = []
        for t in range(2):
            for s, part in enumerate(parts):
                pair = lax.rem(lax.div(order(info_ref), 2) + PAIRS - s, PAIRS)
                target = out_ref.at[pl.ds(pair * 2 * near, 2 * near), :, pl.ds(t * width, width)]
                waits.append(pltpu.make_async_copy(part.at[t], target, sems.at[len(waits)]))
                waits[-1].start()
        staged.wait()
        for t in range(2):
            for i in range(half):
                target = out_ref.at[pl.ds(near_all + i * far, far), :, pl.ds(t * width, width)]
                waits.append(
                    pltpu.make_async_copy(held_ref.at[t * half + i], target, sems.at[len(waits)])
                )
                waits[-1].start()
        for copy in waits:
            copy.wait()

    @pl.when(on_prefill(info_ref))
    def _():
        zero_ref[...] = jnp.zeros_like(zero_ref)
        size = zero_ref.shape[0]
        waits = []
        for n in range(out_ref.shape[0] // size):
            target = out_ref.at[pl.ds(n * size, size)]
            waits.append(pltpu.make_async_copy(zero_ref, target, sems.at[n]))
        for copy in waits:
            copy.start()
        for copy in waits:
            copy.wait()


def two_way_handoff(pairs, info, always, arrival_query, prompt_part, cached, exchanged):
    half = 2 * PAIRS
    rows, width = pairs.shape
    units = rows // (2 * UNIT)
    far_all = units * 2 // (5 * half) * half
    near_all = units - far_all
    near, far = near_all // half, far_all // half
    block = (UNIT, width)
    by_unit = pairs.reshape((rows // UNIT,) + block)
    groups = [[base + 2 * i + tau for tau in range(2) for i in range(half)] for base in (0, 2 * half)]

    def crossing(array, s):
        hops = [
            (2 * p + k, half + 2 * ((p + s) % PAIRS) + k) for p in range(PAIRS) for k in range(2)
        ]
        return lax.ppermute(array, "inst", hops)

    def beside(array, base):
        return lax.ppermute(array, "inst", [(base + i, base + (i ^ 1)) for i in range(half)])

    def spread_out(array):
        return lax.all_to_all(
            array, ("inst", "tp"), 0, 0, axis_index_groups=groups, tiled=True
        )

    def cut_near(pre, sources, targets):
        return [
            (sources[0].at[pl.ds(tau * units, near_all)], targets[0].at[tau]) for tau in range(2)
        ]

    def cut_far(pre, sources, targets):
        plan = []
        for s in range(PAIRS):
            start = near_all + lax.rem(lax.div(order(pre), 2) + s, PAIRS) * (2 * far)
            for tau in range(2):
                plan.append((sources[0].at[pl.ds(tau * units + start, 2 * far)], targets[s].at[tau]))
        return plan

    def for_neighbour(pre, sources, targets):
        plan = []
        for s in range(PAIRS):
            receiver = lax.rem(lax.div(order(pre), 2) + s, PAIRS) * 2 + 1 - lax.rem(order(pre), 2)
            for t in range(2):
                origin = t * half + source_of(pre, receiver)
                plan.append((sources[0].at[origin], targets[0].at[s, t]))
        return plan

    def for_receivers(pre, sources, targets):
        plan = []
        for s in range(PAIRS):
            receiver = lax.rem(lax.div(order(pre), 2) + s, PAIRS) * 2 + lax.rem(order(pre), 2)
            for t in range(2):
                origin = t * half + source_of(pre, receiver)
                mine = targets[s].at[t, pl.ds(lax.rem(order(pre), 2) * near, near)]
                other = targets[s].at[t, pl.ds((1 - lax.rem(order(pre), 2)) * near, near)]
                plan.append((sources[0].at[origin], mine))
                plan.append((sources[1].at[s, t], other))
        return plan

    def split(pre, sources, targets):
        plan = []
        for s in range(PAIRS):
            for tau in range(2):
                mine = sources[s].at[tau, pl.ds(lax.rem(order(pre), 2) * far, far)]
                other = sources[s].at[tau, pl.ds((1 - lax.rem(order(pre), 2)) * far, far)]
                plan.append((mine, targets[0].at[s, tau]))
                plan.append((other, targets[1].at[s, tau]))
        return plan

    near_shape = (2, 2 * near) + block

    def first_stage(spread, *marks):
        (outgoing,) = copies(
            for_neighbour, 2 * PAIRS, info, [spread], [(PAIRS, 2, near) + block], "for_neighbour", marks
        )
        incoming = beside(outgoing, 0)
        return copies(
            for_receivers, 4 * PAIRS, info, [spread, incoming], [near_shape] * PAIRS, "for_receivers"
        )

    def second_stage(prompt, part, other, *far_here):
        keep, give = copies(
            split,
            4 * PAIRS,
            info,
            list(far_here),
            [(PAIRS, 2, far) + block] * 2,
            "split_relays",
            stage=True,
            side=DECODE,
        )
        taken = beside(give, half)
        slots = pl.pallas_call(
            functools.partial(relay_slots_kernel, far),
            out_shape=jax.ShapeDtypeStruct((2 * half, far) + block, jnp.bfloat16),
            grid_spec=pltpu.PrefetchScalarGridSpec(
                num_scalar_prefetch=1,
                grid=(1,),
                in_specs=[ANYWHERE] * 2,
                out_specs=ANYWHERE,
                scratch_shapes=[pltpu.SemaphoreType.DMA((2 * half,))],
            ),
            compiler_params=pltpu.CompilerParams(vmem_limit_bytes=SMALL),
            cost_estimate=COST,
            name="relay_slots",
        )(info, keep, taken)
        prompt, mark = prompt_part(1, prompt, [slots])
        decode_out, _ = combine_parts(info, [part, other], [mark])
        slots = spread_out(slots)
        arrival = arrival_part(
            far_rows_kernel,
            info,
            arrival_query,
            [slots],
            [ANYWHERE],
            [pltpu.VMEM(slots.shape, slots.dtype), pltpu.SemaphoreType.DMA],
            "far_rows",
        )
        return prompt, slots, decode_out, arrival

    def staged(stage, *operands):
        def never(*operands):
            outs = [jnp.zeros(out.shape, out.dtype) for out in jax.eval_shape(stage, *operands)]
            return tuple(outs) if stage is first_stage else (operands[0], *outs[1:])

        return lax.cond(always, lambda *operands: tuple(stage(*operands)), never, *operands)

    (near_rows,) = copies(
        cut_near, 2, info, [by_unit], [(2, near_all) + block], "cut_near", stage=True
    )
    far_parts = copies(
        cut_far, 2 * PAIRS, info, [by_unit], [(2, 2 * far) + block] * PAIRS, "cut_far", [near_rows]
    )
    spread = spread_out(near_rows.reshape((2 * half, near) + block))
    far_here = [crossing(part, s) for s, part in enumerate(far_parts)]
    part, mark = cached([near_rows])
    prompt, mark = prompt_part(0, None, [mark])
    near_parts = staged(first_stage, spread, mark)
    near_here = [crossing(near_part, s) for s, near_part in enumerate(near_parts)]
    other = exchanged(part)
    prompt, slots, decode_out, arrival = staged(second_stage, prompt, part, other, *far_here)
    arrival = arrival_part(
        near_rows_kernel,
        info,
        arrival_query,
        [arrival, *near_here],
        [IN_VMEM] * (PAIRS + 1),
        [],
        "near_rows",
    )
    handed = pl.pallas_call(
        functools.partial(rows_kernel, near, far),
        out_shape=jax.ShapeDtypeStruct((units, UNIT, 2 * width), jnp.bfloat16),
        grid_spec=pltpu.PrefetchScalarGridSpec(
            num_scalar_prefetch=1,
            grid=(1,),
            in_specs=[ANYWHERE] * (PAIRS + 1),
            out_specs=ANYWHERE,
            scratch_shapes=[
                pltpu.VMEM((half, UNIT, 2 * width), jnp.bfloat16),
                pltpu.VMEM(slots.shape, slots.dtype),
                pltpu.SemaphoreType.DMA((2 * (half + PAIRS) + 1,)),
            ],
        ),
        compiler_params=pltpu.CompilerParams(vmem_limit_bytes=MEDIUM),
        cost_estimate=COST,
        name="rows",
    )(info, slots, *near_here)
    arrival_out, _ = combine_parts(info, [arrival, exchanged(arrival)])
    return prompt, handed.reshape(rows // 2, 2 * width), decode_out, arrival_out


def shards(
    prompt_query,
    prompt_pairs,
    decode_query,
    arrival_query,
    cache_pool,
    page_table,
    lengths,
    assignment,
):
    inst_count = lax.axis_size("inst")
    tp_count = lax.axis_size("tp")
    half = inst_count // 2
    inst = lax.axis_index("inst")
    tp_index = lax.axis_index("tp")
    info = jnp.concatenate([jnp.stack([inst, tp_index]), assignment])
    pages, page_len = cache_pool.shape[0], cache_pool.shape[1]
    by_token = cache_pool.reshape(pages * page_len, -1)

    def cached(after=()):
        return cache_attention(info, page_table, lengths, decode_query, by_token, page_len, after)

    def exchanged(part):
        return lax.ppermute(part, "tp", [(0, 1), (1, 0)])

    def combined(part):
        return combine_parts(info, [lax.all_gather(part, "tp")])[0]

    heads = GROUP // 2
    steps = prompt_query.shape[1] // (heads * HEADDIM)

    def prompt_part(first, last, earlier, after=()):
        return prompt_attention(
            info, prompt_query, prompt_pairs, first, last - first, heads, earlier, after
        )

    row_units = prompt_pairs.shape[0] // (2 * UNIT)
    if inst_count == 4 * PAIRS and tp_count == 2 and row_units == 5 * half and steps == 8:
        cuts = (0, 2, 8)
        return two_way_handoff(
            prompt_pairs,
            info,
            assignment[0] >= 0,
            arrival_query,
            lambda n, earlier, after: prompt_part(cuts[n], cuts[n + 1], earlier, after),
            cached,
            exchanged,
        )
    handed = relay_handoff(prompt_pairs, assignment, inst_count)
    arrival = arrival_part(
        whole_rows_kernel, info, arrival_query, [handed], [IN_VMEM], [], "whole_rows"
    )
    prefill_out, _ = prompt_part(0, steps, None)
    return prefill_out, handed, combined(cached()[0]), combined(arrival)


def solution(mesh):
    return jax.shard_map(
        shards,
        mesh=mesh,
        in_specs=(
            P("inst", "tp"),
            P("inst", "tp"),
            P("inst", None),
            P("inst", None),
            P(("inst", "tp"), None, None),
            P("inst", "tp"),
            P("inst"),
            P(),
        ),
        out_specs=(P("inst", "tp"), P(("inst", "tp"), None), P("inst", None), P("inst", None)),
        check_vma=False,
    )
```

```python
import functools

import jax
import jax.numpy as jnp
from jax import lax
from jax.experimental import pallas as pl
from jax.experimental.pallas import tpu as pltpu
from jax.sharding import PartitionSpec as P

QHEADS = 64
KVHEADS = 8
HEADDIM = 128
GROUP = QHEADS // KVHEADS
SCALE = HEADDIM ** (-0.5)
LOG2E = 1.4426950408889634
NEG_FILL = -1e30
TILE = 128
VMEM = 24 * 1024 * 1024
SMALL = 1024 * 1024
MEDIUM = 8 * 1024 * 1024
LARGE = 57 * 1024 * 1024
COST = pl.CostEstimate(flops=1, bytes_accessed=1, transcendentals=0)


INST, TP, FIRST = 0, 1, 2


def on_prefill(info):
    return info[INST] < info.shape[0] - FIRST


def order(info):
    half = info.shape[0] - FIRST
    return info[INST] - jnp.where(on_prefill(info), 0, half)


def source_of(info, receiver):
    half = info.shape[0] - FIRST
    found = jnp.int32(0)
    for p in range(half):
        found = jnp.where(info[FIRST + p] == receiver, p, found)
    return found


def dot_t(a, b):
    return lax.dot_general(a, b, (((1,), (1,)), ((), ())), preferred_element_type=jnp.float32)


def dot(a, b):
    return lax.dot_general(a, b, (((1,), (0,)), ((), ())), preferred_element_type=jnp.float32)


def prompt_kernel(heads, info_ref, q_ref, kv_ref, *rest):
    out_ref = rest[-2]
    length = q_ref.shape[0]

    @pl.when(jnp.logical_not(on_prefill(info_ref)))
    def _():
        out_ref[...] = jnp.zeros_like(out_ref)

    @pl.when(on_prefill(info_ref))
    def _():
        rows_all = lax.broadcasted_iota(jnp.int32, (TILE, TILE), 0)
        cols_all = lax.broadcasted_iota(jnp.int32, (TILE, TILE), 1)
        below = jnp.concatenate([rows_all >= cols_all] * heads, axis=0)
        ones = jnp.ones((length, HEADDIM), jnp.bfloat16)
        values = jnp.concatenate([kv_ref[:, HEADDIM:], ones], axis=1)
        def scores_of(start):
            stop = start + TILE
            queries = jnp.concatenate(
                [q_ref[start:stop, h * HEADDIM : (h + 1) * HEADDIM] for h in range(heads)], axis=0
            )
            last = jnp.where(below, dot_t(queries, kv_ref[start:stop, :HEADDIM]), NEG_FILL)
            return [dot_t(queries, kv_ref[:start, :HEADDIM]), last] if start else [last]

        coming = scores_of(0)
        for start in range(0, length, TILE):
            stop = start + TILE
            scores = coming
            if stop < length:
                coming = scores_of(stop)
            peak = functools.reduce(
                jnp.maximum, [jnp.max(part, axis=1, keepdims=True) for part in scores]
            )
            weights = [
                jnp.exp2((part - peak) * (SCALE * LOG2E)).astype(jnp.bfloat16) for part in scores
            ]
            mixed = dot(weights[-1], values[start:stop])
            if start:
                mixed = mixed + dot(weights[0], values[:start])
            result = (mixed[:, :HEADDIM] / mixed[:, HEADDIM:]).astype(jnp.bfloat16)
            for h in range(heads):
                out_ref[start:stop, h * HEADDIM : (h + 1) * HEADDIM] = result[
                    h * TILE : (h + 1) * TILE
                ]


MARK = jax.ShapeDtypeStruct((8, 128), jnp.float32)
IN_HBM = pl.BlockSpec(memory_space=pltpu.HBM)
ANYWHERE = pl.BlockSpec(memory_space=pl.ANY)
IN_VMEM = pl.BlockSpec(memory_space=pltpu.VMEM)


def prompt_attention(info, queries, pairs, first, steps, heads, earlier, after):
    length, width = queries.shape
    per_kv = GROUP // heads

    def q_map(i, info_ref):
        return (0, jnp.where(on_prefill(info_ref), i + first, 0))

    def kv_map(i, info_ref):
        return (0, jnp.where(on_prefill(info_ref), (i + first) // per_kv, 0))

    in_specs = [
        pl.BlockSpec((length, heads * HEADDIM), q_map),
        pl.BlockSpec((length, 2 * HEADDIM), kv_map),
    ]
    operands = [info, queries, pairs]
    aliases = {}
    if earlier is not None:
        in_specs.append(ANYWHERE)
        operands.append(earlier)
        aliases = {3: 0}
    return pl.pallas_call(
        functools.partial(prompt_kernel, heads),
        out_shape=(jax.ShapeDtypeStruct((length, width), jnp.bfloat16), MARK),
        grid_spec=pltpu.PrefetchScalarGridSpec(
            num_scalar_prefetch=1,
            grid=(steps,),
            in_specs=in_specs + [IN_HBM] * len(after),
            out_specs=(
                pl.BlockSpec((length, heads * HEADDIM), lambda i, info_ref: (0, i + first)),
                IN_HBM,
            ),
        ),
        input_output_aliases=aliases,
        compiler_params=pltpu.CompilerParams(vmem_limit_bytes=LARGE),
        cost_estimate=COST,
        name="prompt_attention",
    )(*operands, *after)


def head_queries(block, head):
    start = head * GROUP * HEADDIM
    return jnp.concatenate(
        [
            block[r : r + 1, start + g * HEADDIM : start + (g + 1) * HEADDIM]
            for r in range(block.shape[0])
            for g in range(GROUP)
        ],
        axis=0,
    ).astype(jnp.bfloat16)


def store_part(out_ref, head, mixed, peak, total):
    lane = lax.broadcasted_iota(jnp.int32, mixed.shape, 1)
    out_ref[head, :, :HEADDIM] = mixed
    out_ref[head, :, HEADDIM:] = jnp.where(lane < HEADDIM // 2, peak, total)


def merged(parts):
    peaks = [part[:, HEADDIM : HEADDIM + 1] for part in parts]
    peak = functools.reduce(jnp.maximum, peaks)
    factors = [jnp.exp(p - peak) for p in peaks]
    total = sum(part[:, -1:] * f for part, f in zip(parts, factors))
    mixed = sum(part[:, :HEADDIM] * f for part, f in zip(parts, factors))
    return mixed, peak, total


def cache_kernel(page_len, info_ref, table_ref, lengths_ref, q_ref, kv_ref, *rest):
    out_ref, _, count_ref = rest[-3:]
    rows, slots = table_ref.shape

    @pl.when(jnp.logical_and(jnp.logical_not(on_prefill(info_ref)), pl.program_id(0) == 0))
    def _():
        token = lax.broadcasted_iota(jnp.int32, (GROUP, count_ref.shape[1]), 1)
        page, offset = token // page_len, token % page_len
        for r in range(rows):
            count = jnp.zeros(token.shape, jnp.float32)
            for slot in range(slots):
                left = lengths_ref[r] - (info_ref[TP] * slots + slot) * page_len
                valid = jnp.logical_and(page == table_ref[r, slot], offset < left)
                count = count + jnp.where(valid, 1.0, 0.0)
            count_ref[r * GROUP : (r + 1) * GROUP] = count

    @pl.when(jnp.logical_not(on_prefill(info_ref)))
    def _():
        count = count_ref[...]
        here = count > 0.0
        block = q_ref[...].astype(jnp.float32)
        for head in range(out_ref.shape[0]):
            start = 2 * head * HEADDIM
            keys = kv_ref[:, start : start + HEADDIM]
            values = kv_ref[:, start + HEADDIM : start + 2 * HEADDIM]
            scores = dot_t(head_queries(block, head), keys) * SCALE
            scores = jnp.where(here, scores, NEG_FILL)
            peak = jnp.max(scores, axis=1, keepdims=True)
            weights = jnp.where(here, jnp.exp(scores - peak), 0.0)
            total = jnp.sum(weights * count, axis=1, keepdims=True)
            rounded = weights.astype(jnp.bfloat16).astype(jnp.float32) * count
            store_part(out_ref, head, dot(rounded.astype(jnp.bfloat16), values), peak, total)


def cache_attention(info, table, lengths, queries, pool, page_len, after):
    rows = queries.shape[0]
    tokens = pool.shape[0]
    steps = 2
    heads = KVHEADS // steps

    def step(n, info):
        return jnp.where(on_prefill(info), 0, n)

    return pl.pallas_call(
        functools.partial(cache_kernel, page_len),
        out_shape=(
            jax.ShapeDtypeStruct((KVHEADS, rows * GROUP, 2 * HEADDIM), jnp.float32),
            MARK,
        ),
        grid_spec=pltpu.PrefetchScalarGridSpec(
            num_scalar_prefetch=3,
            grid=(steps,),
            in_specs=[
                pl.BlockSpec((rows, heads * GROUP * HEADDIM), lambda n, info, *_: (0, step(n, info))),
                pl.BlockSpec((tokens, 2 * heads * HEADDIM), lambda n, info, *_: (0, step(n, info))),
            ]
            + [IN_HBM] * len(after),
            out_specs=(
                pl.BlockSpec(
                    (heads, rows * GROUP, 2 * HEADDIM), lambda n, info, *_: (step(n, info), 0, 0)
                ),
                IN_HBM,
            ),
            scratch_shapes=[pltpu.VMEM((rows * GROUP, tokens), jnp.float32)],
        ),
        compiler_params=pltpu.CompilerParams(vmem_limit_bytes=LARGE),
        cost_estimate=COST,
        name="cache_attention",
    )(info, table, lengths, queries, pool, *after)


def rows_part(queries, rows, out_ref, earlier_ref):
    block = queries[...].astype(jnp.float32)
    heads = rows[0].shape[1] // (2 * HEADDIM)
    places = [(rows[head // heads], 2 * (head % heads) * HEADDIM) for head in range(KVHEADS)]
    scores = [
        dot_t(head_queries(block, head), held[:, start : start + HEADDIM]) * SCALE
        for head, (held, start) in enumerate(places)
    ]
    peaks = [jnp.max(score, axis=1, keepdims=True) for score in scores]
    weights = [jnp.exp(score - peak) for score, peak in zip(scores, peaks)]
    totals = [jnp.sum(weight, axis=1, keepdims=True) for weight in weights]
    mixes = [
        dot(weight.astype(jnp.bfloat16), held[:, start + HEADDIM : start + 2 * HEADDIM])
        for weight, (held, start) in zip(weights, places)
    ]
    for head in range(KVHEADS):
        store_part(out_ref, head, mixes[head], peaks[head], totals[head])
        if earlier_ref is not None:
            store_part(out_ref, head, *merged([out_ref[head], earlier_ref[head]]))


def flat_rows(pieces):
    wide = [piece.astype(jnp.float32).reshape(-1, piece.shape[-1]) for piece in pieces]
    return jnp.concatenate(wide, axis=0).astype(jnp.bfloat16)


def whole_rows_kernel(info_ref, q_ref, rows_ref, out_ref):
    rows_part(q_ref, [rows_ref[...]], out_ref, None)


def far_rows_kernel(near, info_ref, q_ref, slots_ref, part_ref, handed_ref, held_ref, zero_ref, load, sems):
    half = 2 * PAIRS
    far, width = slots_ref.shape[1], slots_ref.shape[-1]

    @pl.when(jnp.logical_not(on_prefill(info_ref)))
    def _():
        staged = pltpu.make_async_copy(slots_ref, held_ref, load)
        staged.start()
        staged.wait()
        waits = []
        for t in range(2):
            for i in range(half):
                slot = t * half + i
                target = handed_ref.at[pl.ds(near + i * far, far), :, pl.ds(t * width, width)]
                waits.append(pltpu.make_async_copy(held_ref.at[slot], target, sems.at[slot]))
        for copy in waits:
            copy.start()
        rows = [flat_rows([held_ref[t * half + i] for i in range(half)]) for t in range(2)]
        rows_part(q_ref, rows, part_ref, None)
        for copy in waits:
            copy.wait()

    @pl.when(on_prefill(info_ref))
    def _():
        zero_ref[...] = jnp.zeros_like(zero_ref)
        size = zero_ref.shape[0]
        waits = []
        for n in range(handed_ref.shape[0] // size):
            target = handed_ref.at[pl.ds(n * size, size)]
            waits.append(pltpu.make_async_copy(zero_ref, target, sems.at[n]))
        for copy in waits:
            copy.start()
        for copy in waits:
            copy.wait()


def near_rows_kernel(info_ref, q_ref, earlier_ref, *refs):
    *part_refs, out_ref = refs

    @pl.when(jnp.logical_not(on_prefill(info_ref)))
    def _():
        rows = [flat_rows([part[t] for part in part_refs]) for t in range(2)]
        rows_part(q_ref, rows, out_ref, earlier_ref)


def arrival_part(kernel, info, query, operands, places, scratch, name):
    return pl.pallas_call(
        kernel,
        out_shape=jax.ShapeDtypeStruct((KVHEADS, GROUP, 2 * HEADDIM), jnp.float32),
        grid_spec=pltpu.PrefetchScalarGridSpec(
            num_scalar_prefetch=1,
            grid=(1,),
            in_specs=[IN_VMEM] + places,
            out_specs=IN_VMEM,
            scratch_shapes=scratch,
        ),
        compiler_params=pltpu.CompilerParams(vmem_limit_bytes=VMEM),
        cost_estimate=COST,
        name=name,
    )(info, query, *operands)


def combine_kernel(count, info_ref, *refs):
    part_refs, out_ref = refs[:count], refs[-2]

    @pl.when(on_prefill(info_ref))
    def _():
        out_ref[...] = jnp.zeros_like(out_ref)

    @pl.when(jnp.logical_not(on_prefill(info_ref)))
    def _():
        results = []
        for head in range(KVHEADS):
            if count == 2:
                here, there = part_refs[0][head], part_refs[1][head]
                first = info_ref[TP] == 0
                parts = [jnp.where(first, here, there), jnp.where(first, there, here)]
            else:
                parts = [part_refs[0][n, head] for n in range(part_refs[0].shape[0])]
            mixed, _, total = merged(parts)
            results.append(mixed / total)
        for r in range(out_ref.shape[0]):
            row = [
                results[head][r * GROUP + g : r * GROUP + g + 1]
                for head in range(KVHEADS)
                for g in range(GROUP)
            ]
            out_ref[r : r + 1] = jnp.concatenate(row, axis=1).astype(jnp.bfloat16)


def combine_parts(info, parts, after=()):
    rows = parts[0].shape[-2] // GROUP
    return pl.pallas_call(
        functools.partial(combine_kernel, len(parts)),
        out_shape=(jax.ShapeDtypeStruct((rows, QHEADS * HEADDIM), jnp.bfloat16), MARK),
        grid_spec=pltpu.PrefetchScalarGridSpec(
            num_scalar_prefetch=1,
            grid=(1,),
            in_specs=[IN_VMEM] * len(parts) + [IN_HBM] * len(after),
            out_specs=(IN_VMEM, IN_HBM),
        ),
        compiler_params=pltpu.CompilerParams(vmem_limit_bytes=VMEM),
        cost_estimate=COST,
        name="combine_parts",
    )(info, *parts, *after)


def relay_handoff(pairs, assignment, inst_count):
    half = inst_count // 2
    decode_ids = jnp.arange(half, dtype=jnp.int32)
    matches = assignment[None, :] == decode_ids[:, None]
    source = jnp.sum(jnp.where(matches, decode_ids[None, :], 0), axis=1).astype(jnp.int32)
    moved = lax.all_to_all(pairs, "tp", split_axis=0, concat_axis=1, tiled=True)
    lanes = 1024 if moved.size % (inst_count * 1024) == 0 else HEADDIM
    pieces = moved.reshape(inst_count, -1, lanes)
    spread = lax.all_to_all(pieces, "inst", split_axis=0, concat_axis=0, tiled=True)
    chosen = jnp.stack(
        [lax.dynamic_index_in_dim(spread, source[d], 0, False) for d in range(half)], axis=0
    )
    outgoing = jnp.concatenate([jnp.zeros_like(chosen), chosen], axis=0)
    delivered = lax.all_to_all(outgoing, "inst", split_axis=0, concat_axis=0, tiled=True)
    return delivered.reshape(moved.shape)


UNIT = 8
PAIRS = 4
PREFILL, DECODE = True, False


def copy_kernel(plan, side, counts, info_ref, *refs):
    inputs, marks, outputs, stages = counts
    sources, targets = refs[:inputs], refs[inputs + marks : inputs + marks + outputs]
    held, sems = refs[-1 - stages : -1], refs[-1]

    @pl.when(on_prefill(info_ref) == side)
    def _():
        started = []
        for source, target in zip(sources, held):
            started.append(pltpu.make_async_copy(source, target, sems.at[len(started)]))
        for copy in started:
            copy.start()
        for copy in started:
            copy.wait()
        started = []
        for source, target in plan(info_ref, held or sources, targets):
            started.append(pltpu.make_async_copy(source, target, sems.at[len(started)]))
        for copy in started:
            copy.start()
        for copy in started:
            copy.wait()


def copies(plan, number, info, operands, shapes, name, after=(), stage=False, side=PREFILL):
    held = [pltpu.VMEM(x.shape, x.dtype) for x in operands] if stage else []
    return pl.pallas_call(
        functools.partial(copy_kernel, plan, side, (len(operands), len(after), len(shapes), len(held))),
        out_shape=tuple(jax.ShapeDtypeStruct(shape, jnp.bfloat16) for shape in shapes),
        grid_spec=pltpu.PrefetchScalarGridSpec(
            num_scalar_prefetch=1,
            grid=(1,),
            in_specs=[ANYWHERE] * len(operands) + [IN_HBM] * len(after),
            out_specs=tuple([ANYWHERE] * len(shapes)),
            scratch_shapes=held + [pltpu.SemaphoreType.DMA((number,))],
        ),
        compiler_params=pltpu.CompilerParams(vmem_limit_bytes=MEDIUM if stage else SMALL),
        cost_estimate=COST,
        name=name,
    )(info, *operands, *after)


def cut_kernel(near, far, rows_ref, near_ref, *refs):
    *far_refs, held_ref, sems = refs
    inst, half = lax.axis_index("inst"), lax.axis_size("inst") // 2
    units = rows_ref.shape[0] // 2

    @pl.when(inst < half)
    def _():
        loads, stores, others = [], [], []
        for tau in range(2):
            first = tau * units
            held = held_ref.at[tau]
            loads.append(pltpu.make_async_copy(rows_ref.at[pl.ds(first, near)], held, sems.at[tau]))
            stores.append(pltpu.make_async_copy(held, near_ref.at[tau], sems.at[2 + tau]))
            loads[-1].start()
        for s, far_ref in enumerate(far_refs):
            relay = lax.rem(lax.div(inst, 2) + s, PAIRS)
            for tau in range(2):
                source = rows_ref.at[pl.ds(tau * units + near + relay * far, far)]
                others.append(
                    pltpu.make_async_copy(source, far_ref.at[tau], sems.at[4 + len(others)])
                )
                others[-1].start()
        for load, store in zip(loads, stores):
            load.wait()
            store.start()
        for copy in stores + others:
            copy.wait()


def relay_slots_kernel(far, info_ref, keep_ref, recv_ref, out_ref, sems):
    half = 2 * PAIRS

    @pl.when(jnp.logical_not(on_prefill(info_ref)))
    def _():
        here = order(info_ref)
        waits = []
        for d in range(half):
            source = source_of(info_ref, d)
            same = lax.rem(source, 2) == lax.rem(here, 2)
            shift = lax.rem(lax.div(here, 2) + PAIRS - lax.div(source, 2), PAIRS)
            for tau in range(2):
                slot = tau * half + d
                target = out_ref.at[slot]
                mine = pltpu.make_async_copy(keep_ref.at[shift, tau], target, sems.at[slot])
                other = pltpu.make_async_copy(recv_ref.at[shift, tau], target, sems.at[slot])
                pl.when(same)(mine.start)
                pl.when(jnp.logical_not(same))(other.start)
                waits.append(mine)
        for copy in waits:
            copy.wait()


def store_near_kernel(near, info_ref, *refs):
    *parts, _, handed_ref, sems = refs
    width = parts[0].shape[-1]

    @pl.when(jnp.logical_not(on_prefill(info_ref)))
    def _():
        waits = []
        for t in range(2):
            for s, part in enumerate(parts):
                pair = lax.rem(lax.div(order(info_ref), 2) + PAIRS - s, PAIRS)
                target = handed_ref.at[pl.ds(pair * 2 * near, 2 * near), :, pl.ds(t * width, width)]
                waits.append(pltpu.make_async_copy(part.at[t], target, sems.at[len(waits)]))
        for copy in waits:
            copy.start()
        for copy in waits:
            copy.wait()


def two_way_handoff(pairs, info, always, arrival_query, prompt_part, cached, exchanged):
    half = 2 * PAIRS
    rows, width = pairs.shape
    units = rows // (2 * UNIT)
    far_all = units * 2 // (5 * half) * half
    near_all = units - far_all
    near, far = near_all // half, far_all // half
    block = (UNIT, width)
    by_unit = pairs.reshape((rows // UNIT,) + block)
    groups = [[base + 2 * i + tau for tau in range(2) for i in range(half)] for base in (0, 2 * half)]

    def crossing(array, s):
        hops = [
            (2 * p + k, half + 2 * ((p + s) % PAIRS) + k) for p in range(PAIRS) for k in range(2)
        ]
        return lax.ppermute(array, "inst", hops)

    def beside(array, base):
        return lax.ppermute(array, "inst", [(base + i, base + (i ^ 1)) for i in range(half)])

    def spread_out(array):
        return lax.all_to_all(
            array, ("inst", "tp"), 0, 0, axis_index_groups=groups, tiled=True
        )

    def for_neighbour(pre, sources, targets):
        plan = []
        for s in range(PAIRS):
            receiver = lax.rem(lax.div(order(pre), 2) + s, PAIRS) * 2 + 1 - lax.rem(order(pre), 2)
            for t in range(2):
                origin = t * half + source_of(pre, receiver)
                plan.append((sources[0].at[origin], targets[0].at[s, t]))
        return plan

    def for_receivers(pre, sources, targets):
        plan = []
        for s in range(PAIRS):
            receiver = lax.rem(lax.div(order(pre), 2) + s, PAIRS) * 2 + lax.rem(order(pre), 2)
            for t in range(2):
                origin = t * half + source_of(pre, receiver)
                mine = targets[s].at[t, pl.ds(lax.rem(order(pre), 2) * near, near)]
                other = targets[s].at[t, pl.ds((1 - lax.rem(order(pre), 2)) * near, near)]
                plan.append((sources[0].at[origin], mine))
                plan.append((sources[1].at[s, t], other))
        return plan

    def split(pre, sources, targets):
        plan = []
        for s in range(PAIRS):
            for tau in range(2):
                mine = sources[s].at[tau, pl.ds(lax.rem(order(pre), 2) * far, far)]
                other = sources[s].at[tau, pl.ds((1 - lax.rem(order(pre), 2)) * far, far)]
                plan.append((mine, targets[0].at[s, tau]))
                plan.append((other, targets[1].at[s, tau]))
        return plan

    near_shape = (2, 2 * near) + block

    def first_stage(spread, *marks):
        (outgoing,) = copies(
            for_neighbour, 2 * PAIRS, info, [spread], [(PAIRS, 2, near) + block], "for_neighbour", marks
        )
        incoming = beside(outgoing, 0)
        return copies(
            for_receivers, 4 * PAIRS, info, [spread, incoming], [near_shape] * PAIRS, "for_receivers"
        )

    def second_stage(prompt, part, other, *far_here):
        keep, give = copies(
            split,
            4 * PAIRS,
            info,
            list(far_here),
            [(PAIRS, 2, far) + block] * 2,
            "split_relays",
            stage=True,
            side=DECODE,
        )
        taken = beside(give, half)
        slots = pl.pallas_call(
            functools.partial(relay_slots_kernel, far),
            out_shape=jax.ShapeDtypeStruct((2 * half, far) + block, jnp.bfloat16),
            grid_spec=pltpu.PrefetchScalarGridSpec(
                num_scalar_prefetch=1,
                grid=(1,),
                in_specs=[ANYWHERE] * 2,
                out_specs=ANYWHERE,
                scratch_shapes=[pltpu.SemaphoreType.DMA((2 * half,))],
            ),
            compiler_params=pltpu.CompilerParams(vmem_limit_bytes=SMALL),
            cost_estimate=COST,
            name="relay_slots",
        )(info, keep, taken)
        prompt, mark = prompt_part(1, prompt, [slots])
        decode_out, _ = combine_parts(info, [part, other], [mark])
        slots = spread_out(slots)
        arrival, handed = pl.pallas_call(
            functools.partial(far_rows_kernel, near_all),
            out_shape=(
                jax.ShapeDtypeStruct((KVHEADS, GROUP, 2 * HEADDIM), jnp.float32),
                jax.ShapeDtypeStruct((units, UNIT, 2 * width), jnp.bfloat16),
            ),
            grid_spec=pltpu.PrefetchScalarGridSpec(
                num_scalar_prefetch=1,
                grid=(1,),
                in_specs=[IN_VMEM, ANYWHERE],
                out_specs=(IN_VMEM, ANYWHERE),
                scratch_shapes=[
                    pltpu.VMEM(slots.shape, slots.dtype),
                    pltpu.VMEM((half, UNIT, 2 * width), jnp.bfloat16),
                    pltpu.SemaphoreType.DMA,
                    pltpu.SemaphoreType.DMA((2 * half,)),
                ],
            ),
            compiler_params=pltpu.CompilerParams(vmem_limit_bytes=VMEM),
            cost_estimate=COST,
            name="far_rows",
        )(info, arrival_query, slots)
        return prompt, handed, decode_out, arrival

    def staged(stage, *operands):
        def never(*operands):
            outs = [jnp.zeros(out.shape, out.dtype) for out in jax.eval_shape(stage, *operands)]
            return tuple(outs) if stage is first_stage else (operands[0], *outs[1:])

        return lax.cond(always, lambda *operands: tuple(stage(*operands)), never, *operands)

    near_rows, *far_parts = pl.pallas_call(
        functools.partial(cut_kernel, near_all, 2 * far),
        out_shape=tuple(
            jax.ShapeDtypeStruct(shape + block, jnp.bfloat16)
            for shape in [(2, near_all)] + [(2, 2 * far)] * PAIRS
        ),
        grid=(1,),
        in_specs=[ANYWHERE],
        out_specs=(ANYWHERE,) * (1 + PAIRS),
        scratch_shapes=[
            pltpu.VMEM((2, near_all) + block, jnp.bfloat16),
            pltpu.SemaphoreType.DMA((4 + 2 * PAIRS,)),
        ],
        compiler_params=pltpu.CompilerParams(vmem_limit_bytes=MEDIUM),
        cost_estimate=COST,
        name="cut_rows",
    )(by_unit)
    spread = spread_out(near_rows.reshape((2 * half, near) + block))
    far_here = [crossing(part, s) for s, part in enumerate(far_parts)]
    part, mark = cached([near_rows])
    prompt, mark = prompt_part(0, None, [mark])
    near_parts = staged(first_stage, spread, mark)
    near_parts, far_here = lax.optimization_barrier((near_parts, far_here))
    near_here = [crossing(near_part, s) for s, near_part in enumerate(near_parts)]
    other = exchanged(part)
    prompt, handed, decode_out, arrival = staged(second_stage, prompt, part, other, *far_here)
    arrival = arrival_part(
        near_rows_kernel,
        info,
        arrival_query,
        [arrival, *near_here],
        [IN_VMEM] * (PAIRS + 1),
        [],
        "near_rows",
    )
    handed = pl.pallas_call(
        functools.partial(store_near_kernel, near),
        out_shape=jax.ShapeDtypeStruct(handed.shape, handed.dtype),
        grid_spec=pltpu.PrefetchScalarGridSpec(
            num_scalar_prefetch=1,
            grid=(1,),
            in_specs=[ANYWHERE] * (PAIRS + 1),
            out_specs=ANYWHERE,
            scratch_shapes=[pltpu.SemaphoreType.DMA((2 * PAIRS,))],
        ),
        input_output_aliases={PAIRS + 1: 0},
        compiler_params=pltpu.CompilerParams(vmem_limit_bytes=SMALL),
        cost_estimate=COST,
        name="store_near",
    )(info, *near_here, handed)
    arrival_out, _ = combine_parts(info, [arrival, exchanged(arrival)])
    return prompt, handed.reshape(rows // 2, 2 * width), decode_out, arrival_out


def shards(
    prompt_query,
    prompt_pairs,
    decode_query,
    arrival_query,
    cache_pool,
    page_table,
    lengths,
    assignment,
):
    inst_count = lax.axis_size("inst")
    tp_count = lax.axis_size("tp")
    half = inst_count // 2
    inst = lax.axis_index("inst")
    tp_index = lax.axis_index("tp")
    info = jnp.concatenate([jnp.stack([inst, tp_index]), assignment])
    pages, page_len = cache_pool.shape[0], cache_pool.shape[1]
    by_token = cache_pool.reshape(pages * page_len, -1)

    def cached(after=()):
        return cache_attention(info, page_table, lengths, decode_query, by_token, page_len, after)

    def exchanged(part):
        return lax.ppermute(part, "tp", [(0, 1), (1, 0)])

    def combined(part):
        return combine_parts(info, [lax.all_gather(part, "tp")])[0]

    heads = GROUP
    steps = prompt_query.shape[1] // (heads * HEADDIM)

    def prompt_part(first, last, earlier, after=()):
        return prompt_attention(
            info, prompt_query, prompt_pairs, first, last - first, heads, earlier, after
        )

    row_units = prompt_pairs.shape[0] // (2 * UNIT)
    if inst_count == 4 * PAIRS and tp_count == 2 and row_units == 5 * half and steps == 4:
        cuts = (0, 1, 4)
        return two_way_handoff(
            prompt_pairs,
            info,
            assignment[0] >= 0,
            arrival_query,
            lambda n, earlier, after: prompt_part(cuts[n], cuts[n + 1], earlier, after),
            cached,
            exchanged,
        )
    handed = relay_handoff(prompt_pairs, assignment, inst_count)
    arrival = arrival_part(
        whole_rows_kernel, info, arrival_query, [handed], [IN_VMEM], [], "whole_rows"
    )
    prefill_out, _ = prompt_part(0, steps, None)
    return prefill_out, handed, combined(cached()[0]), combined(arrival)


def solution(mesh):
    return jax.shard_map(
        shards,
        mesh=mesh,
        in_specs=(
            P("inst", "tp"),
            P("inst", "tp"),
            P("inst", None),
            P("inst", None),
            P(("inst", "tp"), None, None),
            P("inst", "tp"),
            P("inst"),
            P(),
        ),
        out_specs=(P("inst", "tp"), P(("inst", "tp"), None), P("inst", None), P("inst", None)),
        check_vma=False,
    )
```

```python
import functools

import jax
import jax.numpy as jnp
from jax import lax
from jax.experimental import pallas as pl
from jax.experimental.pallas import tpu as pltpu
from jax.sharding import PartitionSpec as P

QHEADS = 64
KVHEADS = 8
HEADDIM = 128
GROUP = QHEADS // KVHEADS
SCALE = HEADDIM ** (-0.5)
LOG2E = 1.4426950408889634
NEG_FILL = -1e30
TILE = 128
VMEM = 24 * 1024 * 1024
SMALL = 1024 * 1024
MEDIUM = 8 * 1024 * 1024
LARGE = 57 * 1024 * 1024
COST = pl.CostEstimate(flops=1, bytes_accessed=1, transcendentals=0)


INST, TP, FIRST = 0, 1, 2


def on_prefill(info):
    return info[INST] < info.shape[0] - FIRST


def order(info):
    half = info.shape[0] - FIRST
    return info[INST] - jnp.where(on_prefill(info), 0, half)


def source_of(info, receiver):
    half = info.shape[0] - FIRST
    found = jnp.int32(0)
    for p in range(half):
        found = jnp.where(info[FIRST + p] == receiver, p, found)
    return found


def dot_t(a, b):
    return lax.dot_general(a, b, (((1,), (1,)), ((), ())), preferred_element_type=jnp.float32)


def dot(a, b):
    return lax.dot_general(a, b, (((1,), (0,)), ((), ())), preferred_element_type=jnp.float32)


def prompt_kernel(heads, info_ref, q_ref, kv_ref, *rest):
    out_ref = rest[-2]
    length = q_ref.shape[0]

    @pl.when(jnp.logical_not(on_prefill(info_ref)))
    def _():
        out_ref[...] = jnp.zeros_like(out_ref)

    @pl.when(on_prefill(info_ref))
    def _():
        rows_all = lax.broadcasted_iota(jnp.int32, (TILE, TILE), 0)
        cols_all = lax.broadcasted_iota(jnp.int32, (TILE, TILE), 1)
        below = jnp.concatenate([rows_all >= cols_all] * heads, axis=0)
        ones = jnp.ones((length, HEADDIM), jnp.bfloat16)
        values = jnp.concatenate([kv_ref[:, HEADDIM:], ones], axis=1)
        def scores_of(start):
            stop = start + TILE
            queries = jnp.concatenate(
                [q_ref[start:stop, h * HEADDIM : (h + 1) * HEADDIM] for h in range(heads)], axis=0
            )
            last = jnp.where(below, dot_t(queries, kv_ref[start:stop, :HEADDIM]), NEG_FILL)
            return [dot_t(queries, kv_ref[:start, :HEADDIM]), last] if start else [last]

        coming = scores_of(0)
        for start in range(0, length, TILE):
            stop = start + TILE
            scores = coming
            if stop < length:
                coming = scores_of(stop)
            peak = functools.reduce(
                jnp.maximum, [jnp.max(part, axis=1, keepdims=True) for part in scores]
            )
            weights = [
                jnp.exp2((part - peak) * (SCALE * LOG2E)).astype(jnp.bfloat16) for part in scores
            ]
            mixed = dot(weights[-1], values[start:stop])
            if start:
                mixed = mixed + dot(weights[0], values[:start])
            result = (mixed[:, :HEADDIM] / mixed[:, HEADDIM:]).astype(jnp.bfloat16)
            for h in range(heads):
                out_ref[start:stop, h * HEADDIM : (h + 1) * HEADDIM] = result[
                    h * TILE : (h + 1) * TILE
                ]


MARK = jax.ShapeDtypeStruct((8, 128), jnp.float32)
IN_HBM = pl.BlockSpec(memory_space=pltpu.HBM)
ANYWHERE = pl.BlockSpec(memory_space=pl.ANY)
IN_VMEM = pl.BlockSpec(memory_space=pltpu.VMEM)


def prompt_attention(info, queries, pairs, first, steps, heads, earlier, after):
    length, width = queries.shape
    per_kv = GROUP // heads

    def q_map(i, info_ref):
        return (0, jnp.where(on_prefill(info_ref), i + first, 0))

    def kv_map(i, info_ref):
        return (0, jnp.where(on_prefill(info_ref), (i + first) // per_kv, 0))

    in_specs = [
        pl.BlockSpec((length, heads * HEADDIM), q_map),
        pl.BlockSpec((length, 2 * HEADDIM), kv_map),
    ]
    operands = [info, queries, pairs]
    aliases = {}
    if earlier is not None:
        in_specs.append(ANYWHERE)
        operands.append(earlier)
        aliases = {3: 0}
    return pl.pallas_call(
        functools.partial(prompt_kernel, heads),
        out_shape=(jax.ShapeDtypeStruct((length, width), jnp.bfloat16), MARK),
        grid_spec=pltpu.PrefetchScalarGridSpec(
            num_scalar_prefetch=1,
            grid=(steps,),
            in_specs=in_specs + [IN_HBM] * len(after),
            out_specs=(
                pl.BlockSpec((length, heads * HEADDIM), lambda i, info_ref: (0, i + first)),
                IN_HBM,
            ),
        ),
        input_output_aliases=aliases,
        compiler_params=pltpu.CompilerParams(vmem_limit_bytes=LARGE),
        cost_estimate=COST,
        name="prompt_attention",
    )(*operands, *after)


def head_queries(block, head):
    start = head * GROUP * HEADDIM
    return jnp.concatenate(
        [
            block[r : r + 1, start + g * HEADDIM : start + (g + 1) * HEADDIM]
            for r in range(block.shape[0])
            for g in range(GROUP)
        ],
        axis=0,
    ).astype(jnp.bfloat16)


def store_part(out_ref, head, mixed, peak, total):
    lane = lax.broadcasted_iota(jnp.int32, mixed.shape, 1)
    out_ref[head, :, :HEADDIM] = mixed
    out_ref[head, :, HEADDIM:] = jnp.where(lane < HEADDIM // 2, peak, total)


def merged(parts):
    peaks = [part[:, HEADDIM : HEADDIM + 1] for part in parts]
    peak = functools.reduce(jnp.maximum, peaks)
    factors = [jnp.exp(p - peak) for p in peaks]
    total = sum(part[:, -1:] * f for part, f in zip(parts, factors))
    mixed = sum(part[:, :HEADDIM] * f for part, f in zip(parts, factors))
    return mixed, peak, total


def cache_kernel(page_len, info_ref, table_ref, lengths_ref, q_ref, kv_ref, *rest):
    out_ref, _, count_ref = rest[-3:]
    rows, slots = table_ref.shape

    @pl.when(jnp.logical_and(jnp.logical_not(on_prefill(info_ref)), pl.program_id(0) == 0))
    def _():
        token = lax.broadcasted_iota(jnp.int32, (GROUP, count_ref.shape[1]), 1)
        page, offset = token // page_len, token % page_len
        for r in range(rows):
            count = jnp.zeros(token.shape, jnp.float32)
            for slot in range(slots):
                left = lengths_ref[r] - (info_ref[TP] * slots + slot) * page_len
                valid = jnp.logical_and(page == table_ref[r, slot], offset < left)
                count = count + jnp.where(valid, 1.0, 0.0)
            count_ref[r * GROUP : (r + 1) * GROUP] = count

    @pl.when(jnp.logical_not(on_prefill(info_ref)))
    def _():
        count = count_ref[...]
        here = count > 0.0
        block = q_ref[...].astype(jnp.float32)
        for head in range(out_ref.shape[0]):
            start = 2 * head * HEADDIM
            keys = kv_ref[:, start : start + HEADDIM]
            values = kv_ref[:, start + HEADDIM : start + 2 * HEADDIM]
            scores = dot_t(head_queries(block, head), keys) * SCALE
            scores = jnp.where(here, scores, NEG_FILL)
            peak = jnp.max(scores, axis=1, keepdims=True)
            weights = jnp.where(here, jnp.exp(scores - peak), 0.0)
            total = jnp.sum(weights * count, axis=1, keepdims=True)
            rounded = weights.astype(jnp.bfloat16).astype(jnp.float32) * count
            store_part(out_ref, head, dot(rounded.astype(jnp.bfloat16), values), peak, total)


def cache_attention(info, table, lengths, queries, pool, page_len, after):
    rows = queries.shape[0]
    tokens = pool.shape[0]
    steps = 2
    heads = KVHEADS // steps

    def step(n, info):
        return jnp.where(on_prefill(info), 0, n)

    return pl.pallas_call(
        functools.partial(cache_kernel, page_len),
        out_shape=(
            jax.ShapeDtypeStruct((KVHEADS, rows * GROUP, 2 * HEADDIM), jnp.float32),
            MARK,
        ),
        grid_spec=pltpu.PrefetchScalarGridSpec(
            num_scalar_prefetch=3,
            grid=(steps,),
            in_specs=[
                pl.BlockSpec((rows, heads * GROUP * HEADDIM), lambda n, info, *_: (0, step(n, info))),
                pl.BlockSpec((tokens, 2 * heads * HEADDIM), lambda n, info, *_: (0, step(n, info))),
            ]
            + [IN_HBM] * len(after),
            out_specs=(
                pl.BlockSpec(
                    (heads, rows * GROUP, 2 * HEADDIM), lambda n, info, *_: (step(n, info), 0, 0)
                ),
                IN_HBM,
            ),
            scratch_shapes=[pltpu.VMEM((rows * GROUP, tokens), jnp.float32)],
        ),
        compiler_params=pltpu.CompilerParams(vmem_limit_bytes=LARGE),
        cost_estimate=COST,
        name="cache_attention",
    )(info, table, lengths, queries, pool, *after)


def rows_part(queries, rows, out_ref, earlier_ref):
    block = queries[...].astype(jnp.float32)
    heads = rows[0].shape[1] // (2 * HEADDIM)
    places = [(rows[head // heads], 2 * (head % heads) * HEADDIM) for head in range(KVHEADS)]
    scores = [
        dot_t(head_queries(block, head), held[:, start : start + HEADDIM]) * SCALE
        for head, (held, start) in enumerate(places)
    ]
    peaks = [jnp.max(score, axis=1, keepdims=True) for score in scores]
    weights = [jnp.exp(score - peak) for score, peak in zip(scores, peaks)]
    totals = [jnp.sum(weight, axis=1, keepdims=True) for weight in weights]
    mixes = [
        dot(weight.astype(jnp.bfloat16), held[:, start + HEADDIM : start + 2 * HEADDIM])
        for weight, (held, start) in zip(weights, places)
    ]
    for head in range(KVHEADS):
        store_part(out_ref, head, mixes[head], peaks[head], totals[head])
        if earlier_ref is not None:
            store_part(out_ref, head, *merged([out_ref[head], earlier_ref[head]]))


def flat_rows(pieces):
    wide = [piece.astype(jnp.float32).reshape(-1, piece.shape[-1]) for piece in pieces]
    return jnp.concatenate(wide, axis=0).astype(jnp.bfloat16)


def whole_rows_kernel(info_ref, q_ref, rows_ref, out_ref):
    rows_part(q_ref, [rows_ref[...]], out_ref, None)


def far_rows_kernel(near, info_ref, q_ref, slots_ref, part_ref, handed_ref, held_ref, zero_ref, load, sems):
    half = 2 * PAIRS
    far, width = slots_ref.shape[1], slots_ref.shape[-1]

    @pl.when(jnp.logical_not(on_prefill(info_ref)))
    def _():
        staged = pltpu.make_async_copy(slots_ref, held_ref, load)
        staged.start()
        staged.wait()
        waits = []
        for t in range(2):
            for i in range(half):
                slot = t * half + i
                target = handed_ref.at[pl.ds(near + i * far, far), :, pl.ds(t * width, width)]
                waits.append(pltpu.make_async_copy(held_ref.at[slot], target, sems.at[slot]))
        for copy in waits:
            copy.start()
        rows = [flat_rows([held_ref[t * half + i] for i in range(half)]) for t in range(2)]
        rows_part(q_ref, rows, part_ref, None)
        for copy in waits:
            copy.wait()

    @pl.when(on_prefill(info_ref))
    def _():
        zero_ref[...] = jnp.zeros_like(zero_ref)
        size = zero_ref.shape[0]
        waits = []
        for n in range(handed_ref.shape[0] // size):
            target = handed_ref.at[pl.ds(n * size, size)]
            waits.append(pltpu.make_async_copy(zero_ref, target, sems.at[n]))
        for copy in waits:
            copy.start()
        for copy in waits:
            copy.wait()


def near_rows_kernel(info_ref, q_ref, earlier_ref, *refs):
    *part_refs, out_ref = refs

    @pl.when(jnp.logical_not(on_prefill(info_ref)))
    def _():
        rows = [flat_rows([part[t] for part in part_refs]) for t in range(2)]
        rows_part(q_ref, rows, out_ref, earlier_ref)


def arrival_part(kernel, info, query, operands, places, scratch, name):
    return pl.pallas_call(
        kernel,
        out_shape=jax.ShapeDtypeStruct((KVHEADS, GROUP, 2 * HEADDIM), jnp.float32),
        grid_spec=pltpu.PrefetchScalarGridSpec(
            num_scalar_prefetch=1,
            grid=(1,),
            in_specs=[IN_VMEM] + places,
            out_specs=IN_VMEM,
            scratch_shapes=scratch,
        ),
        compiler_params=pltpu.CompilerParams(vmem_limit_bytes=VMEM),
        cost_estimate=COST,
        name=name,
    )(info, query, *operands)


def combine_kernel(count, info_ref, *refs):
    part_refs, out_ref = refs[:count], refs[-2]

    @pl.when(on_prefill(info_ref))
    def _():
        out_ref[...] = jnp.zeros_like(out_ref)

    @pl.when(jnp.logical_not(on_prefill(info_ref)))
    def _():
        results = []
        for head in range(KVHEADS):
            if count == 2:
                here, there = part_refs[0][head], part_refs[1][head]
                first = info_ref[TP] == 0
                parts = [jnp.where(first, here, there), jnp.where(first, there, here)]
            else:
                parts = [part_refs[0][n, head] for n in range(part_refs[0].shape[0])]
            mixed, _, total = merged(parts)
            results.append(mixed / total)
        rows = [
            jnp.concatenate(
                [
                    results[head][r * GROUP + g : r * GROUP + g + 1]
                    for head in range(KVHEADS)
                    for g in range(GROUP)
                ],
                axis=1,
            )
            for r in range(out_ref.shape[0])
        ]
        out_ref[...] = jnp.concatenate(rows, axis=0).astype(jnp.bfloat16)


def combine_parts(info, parts, after=()):
    rows = parts[0].shape[-2] // GROUP
    return pl.pallas_call(
        functools.partial(combine_kernel, len(parts)),
        out_shape=(jax.ShapeDtypeStruct((rows, QHEADS * HEADDIM), jnp.bfloat16), MARK),
        grid_spec=pltpu.PrefetchScalarGridSpec(
            num_scalar_prefetch=1,
            grid=(1,),
            in_specs=[IN_VMEM] * len(parts) + [IN_HBM] * len(after),
            out_specs=(IN_VMEM, IN_HBM),
        ),
        compiler_params=pltpu.CompilerParams(vmem_limit_bytes=VMEM),
        cost_estimate=COST,
        name="combine_parts",
    )(info, *parts, *after)


def relay_handoff(pairs, assignment, inst_count):
    half = inst_count // 2
    decode_ids = jnp.arange(half, dtype=jnp.int32)
    matches = assignment[None, :] == decode_ids[:, None]
    source = jnp.sum(jnp.where(matches, decode_ids[None, :], 0), axis=1).astype(jnp.int32)
    moved = lax.all_to_all(pairs, "tp", split_axis=0, concat_axis=1, tiled=True)
    lanes = 1024 if moved.size % (inst_count * 1024) == 0 else HEADDIM
    pieces = moved.reshape(inst_count, -1, lanes)
    spread = lax.all_to_all(pieces, "inst", split_axis=0, concat_axis=0, tiled=True)
    chosen = jnp.stack(
        [lax.dynamic_index_in_dim(spread, source[d], 0, False) for d in range(half)], axis=0
    )
    outgoing = jnp.concatenate([jnp.zeros_like(chosen), chosen], axis=0)
    delivered = lax.all_to_all(outgoing, "inst", split_axis=0, concat_axis=0, tiled=True)
    return delivered.reshape(moved.shape)


UNIT = 8
PAIRS = 4
PREFILL, DECODE = True, False


def copy_kernel(plan, side, counts, info_ref, *refs):
    inputs, marks, outputs, stages = counts
    sources, targets = refs[:inputs], refs[inputs + marks : inputs + marks + outputs]
    held, sems = refs[-1 - stages : -1], refs[-1]

    @pl.when(on_prefill(info_ref) == side)
    def _():
        started = []
        for source, target in zip(sources, held):
            started.append(pltpu.make_async_copy(source, target, sems.at[len(started)]))
        for copy in started:
            copy.start()
        for copy in started:
            copy.wait()
        started = []
        for source, target in plan(info_ref, held or sources, targets):
            started.append(pltpu.make_async_copy(source, target, sems.at[len(started)]))
        for copy in started:
            copy.start()
        for copy in started:
            copy.wait()


def copies(plan, number, info, operands, shapes, name, after=(), stage=False, side=PREFILL):
    held = [pltpu.VMEM(x.shape, x.dtype) for x in operands] if stage else []
    return pl.pallas_call(
        functools.partial(copy_kernel, plan, side, (len(operands), len(after), len(shapes), len(held))),
        out_shape=tuple(jax.ShapeDtypeStruct(shape, jnp.bfloat16) for shape in shapes),
        grid_spec=pltpu.PrefetchScalarGridSpec(
            num_scalar_prefetch=1,
            grid=(1,),
            in_specs=[ANYWHERE] * len(operands) + [IN_HBM] * len(after),
            out_specs=tuple([ANYWHERE] * len(shapes)),
            scratch_shapes=held + [pltpu.SemaphoreType.DMA((number,))],
        ),
        compiler_params=pltpu.CompilerParams(vmem_limit_bytes=MEDIUM if stage else SMALL),
        cost_estimate=COST,
        name=name,
    )(info, *operands, *after)


def cut_kernel(near, far, rows_ref, near_ref, *refs):
    *far_refs, held_ref, sems = refs
    inst, half = lax.axis_index("inst"), lax.axis_size("inst") // 2
    units = rows_ref.shape[0] // 2

    @pl.when(inst < half)
    def _():
        loads, stores, others = [], [], []
        for tau in range(2):
            first = tau * units
            held = held_ref.at[tau]
            loads.append(pltpu.make_async_copy(rows_ref.at[pl.ds(first, near)], held, sems.at[tau]))
            stores.append(pltpu.make_async_copy(held, near_ref.at[tau], sems.at[2 + tau]))
            loads[-1].start()
        for s, far_ref in enumerate(far_refs):
            relay = lax.rem(lax.div(inst, 2) + s, PAIRS)
            for tau in range(2):
                source = rows_ref.at[pl.ds(tau * units + near + relay * far, far)]
                others.append(
                    pltpu.make_async_copy(source, far_ref.at[tau], sems.at[4 + len(others)])
                )
                others[-1].start()
        for load, store in zip(loads, stores):
            load.wait()
            store.start()
        for copy in stores + others:
            copy.wait()


def relay_slots_kernel(far, info_ref, keep_ref, recv_ref, out_ref, sems):
    half = 2 * PAIRS

    @pl.when(jnp.logical_not(on_prefill(info_ref)))
    def _():
        here = order(info_ref)
        waits = []
        for d in range(half):
            source = source_of(info_ref, d)
            same = lax.rem(source, 2) == lax.rem(here, 2)
            shift = lax.rem(lax.div(here, 2) + PAIRS - lax.div(source, 2), PAIRS)
            for tau in range(2):
                slot = tau * half + d
                target = out_ref.at[slot]
                mine = pltpu.make_async_copy(keep_ref.at[shift, tau], target, sems.at[slot])
                other = pltpu.make_async_copy(recv_ref.at[shift, tau], target, sems.at[slot])
                pl.when(same)(mine.start)
                pl.when(jnp.logical_not(same))(other.start)
                waits.append(mine)
        for copy in waits:
            copy.wait()


def store_near_kernel(near, info_ref, *refs):
    *parts, _, handed_ref, sems = refs
    width = parts[0].shape[-1]

    @pl.when(jnp.logical_not(on_prefill(info_ref)))
    def _():
        waits = []
        for t in range(2):
            for s, part in enumerate(parts):
                pair = lax.rem(lax.div(order(info_ref), 2) + PAIRS - s, PAIRS)
                target = handed_ref.at[pl.ds(pair * 2 * near, 2 * near), :, pl.ds(t * width, width)]
                waits.append(pltpu.make_async_copy(part.at[t], target, sems.at[len(waits)]))
        for copy in waits:
            copy.start()
        for copy in waits:
            copy.wait()


def two_way_handoff(pairs, info, always, arrival_query, prompt_part, cached, exchanged):
    half = 2 * PAIRS
    rows, width = pairs.shape
    units = rows // (2 * UNIT)
    far_all = units * 2 // (5 * half) * half
    near_all = units - far_all
    near, far = near_all // half, far_all // half
    block = (UNIT, width)
    by_unit = pairs.reshape((rows // UNIT,) + block)
    groups = [[base + 2 * i + tau for tau in range(2) for i in range(half)] for base in (0, 2 * half)]

    def crossing(array, s):
        hops = [
            (2 * p + k, half + 2 * ((p + s) % PAIRS) + k) for p in range(PAIRS) for k in range(2)
        ]
        return lax.ppermute(array, "inst", hops)

    def beside(array, base):
        return lax.ppermute(array, "inst", [(base + i, base + (i ^ 1)) for i in range(half)])

    def spread_out(array):
        return lax.all_to_all(
            array, ("inst", "tp"), 0, 0, axis_index_groups=groups, tiled=True
        )

    def for_neighbour(pre, sources, targets):
        plan = []
        for s in range(PAIRS):
            receiver = lax.rem(lax.div(order(pre), 2) + s, PAIRS) * 2 + 1 - lax.rem(order(pre), 2)
            for t in range(2):
                origin = t * half + source_of(pre, receiver)
                plan.append((sources[0].at[origin], targets[0].at[s, t]))
        return plan

    def for_receivers(pre, sources, targets):
        plan = []
        for s in range(PAIRS):
            receiver = lax.rem(lax.div(order(pre), 2) + s, PAIRS) * 2 + lax.rem(order(pre), 2)
            for t in range(2):
                origin = t * half + source_of(pre, receiver)
                mine = targets[s].at[t, pl.ds(lax.rem(order(pre), 2) * near, near)]
                other = targets[s].at[t, pl.ds((1 - lax.rem(order(pre), 2)) * near, near)]
                plan.append((sources[0].at[origin], mine))
                plan.append((sources[1].at[s, t], other))
        return plan

    def split(pre, sources, targets):
        plan = []
        for s in range(PAIRS):
            for tau in range(2):
                mine = sources[s].at[tau, pl.ds(lax.rem(order(pre), 2) * far, far)]
                other = sources[s].at[tau, pl.ds((1 - lax.rem(order(pre), 2)) * far, far)]
                plan.append((mine, targets[0].at[s, tau]))
                plan.append((other, targets[1].at[s, tau]))
        return plan

    near_shape = (2, 2 * near) + block

    def gather_stage(spread, *marks):
        (outgoing,) = copies(
            for_neighbour, 2 * PAIRS, info, [spread], [(PAIRS, 2, near) + block], "for_neighbour", marks
        )
        incoming = beside(outgoing, 0)
        return copies(
            for_receivers, 4 * PAIRS, info, [spread, incoming], [near_shape] * PAIRS, "for_receivers"
        )

    def first_stage(near_rows, *far_parts):
        spread = spread_out(near_rows.reshape((2 * half, near) + block))
        far_here = [crossing(part, s) for s, part in enumerate(far_parts, 1)]
        part, mark = cached([near_rows])
        prompt, mark = prompt_part(0, None, [mark])
        return *staged(gather_stage, spread, mark), prompt, part, *far_here

    def second_stage(prompt, part, other, *far_here):
        keep, give = copies(
            split,
            4 * PAIRS,
            info,
            list(far_here),
            [(PAIRS, 2, far) + block] * 2,
            "split_relays",
            stage=True,
            side=DECODE,
        )
        taken = beside(give, half)
        slots = pl.pallas_call(
            functools.partial(relay_slots_kernel, far),
            out_shape=jax.ShapeDtypeStruct((2 * half, far) + block, jnp.bfloat16),
            grid_spec=pltpu.PrefetchScalarGridSpec(
                num_scalar_prefetch=1,
                grid=(1,),
                in_specs=[ANYWHERE] * 2,
                out_specs=ANYWHERE,
                scratch_shapes=[pltpu.SemaphoreType.DMA((2 * half,))],
            ),
            compiler_params=pltpu.CompilerParams(vmem_limit_bytes=SMALL),
            cost_estimate=COST,
            name="relay_slots",
        )(info, keep, taken)
        prompt, mark = prompt_part(1, prompt, [slots])
        decode_out, _ = combine_parts(info, [part, other], [mark])
        slots = spread_out(slots)
        arrival, handed = pl.pallas_call(
            functools.partial(far_rows_kernel, near_all),
            out_shape=(
                jax.ShapeDtypeStruct((KVHEADS, GROUP, 2 * HEADDIM), jnp.float32),
                jax.ShapeDtypeStruct((units, UNIT, 2 * width), jnp.bfloat16),
            ),
            grid_spec=pltpu.PrefetchScalarGridSpec(
                num_scalar_prefetch=1,
                grid=(1,),
                in_specs=[IN_VMEM, ANYWHERE],
                out_specs=(IN_VMEM, ANYWHERE),
                scratch_shapes=[
                    pltpu.VMEM(slots.shape, slots.dtype),
                    pltpu.VMEM((half, UNIT, 2 * width), jnp.bfloat16),
                    pltpu.SemaphoreType.DMA,
                    pltpu.SemaphoreType.DMA((2 * half,)),
                ],
            ),
            compiler_params=pltpu.CompilerParams(vmem_limit_bytes=VMEM),
            cost_estimate=COST,
            name="far_rows",
        )(info, arrival_query, slots)
        return prompt, handed, decode_out, arrival

    def staged(stage, *operands):
        def never(*operands):
            outs = [jnp.zeros(out.shape, out.dtype) for out in jax.eval_shape(stage, *operands)]
            return (operands[0], *outs[1:]) if stage is second_stage else tuple(outs)

        return lax.cond(always, lambda *operands: tuple(stage(*operands)), never, *operands)

    near_rows, *far_parts = pl.pallas_call(
        functools.partial(cut_kernel, near_all, 2 * far),
        out_shape=tuple(
            jax.ShapeDtypeStruct(shape + block, jnp.bfloat16)
            for shape in [(2, near_all)] + [(2, 2 * far)] * PAIRS
        ),
        grid=(1,),
        in_specs=[ANYWHERE],
        out_specs=(ANYWHERE,) * (1 + PAIRS),
        scratch_shapes=[
            pltpu.VMEM((2, near_all) + block, jnp.bfloat16),
            pltpu.SemaphoreType.DMA((4 + 2 * PAIRS,)),
        ],
        compiler_params=pltpu.CompilerParams(vmem_limit_bytes=MEDIUM),
        cost_estimate=COST,
        name="cut_rows",
    )(by_unit)
    first = crossing(far_parts[0], 0)
    outs = staged(first_stage, near_rows, *far_parts[1:])
    near_parts, (prompt, part), far_here = outs[:PAIRS], outs[PAIRS : PAIRS + 2], outs[PAIRS + 2 :]
    other = exchanged(part)
    near_parts, first = lax.optimization_barrier((near_parts, first))
    far_here = [first, *far_here]
    near_here = [crossing(near_part, s) for s, near_part in enumerate(near_parts)]
    prompt, handed, decode_out, arrival = staged(second_stage, prompt, part, other, *far_here)
    arrival = arrival_part(
        near_rows_kernel,
        info,
        arrival_query,
        [arrival, *near_here],
        [IN_VMEM] * (PAIRS + 1),
        [],
        "near_rows",
    )
    handed = pl.pallas_call(
        functools.partial(store_near_kernel, near),
        out_shape=jax.ShapeDtypeStruct(handed.shape, handed.dtype),
        grid_spec=pltpu.PrefetchScalarGridSpec(
            num_scalar_prefetch=1,
            grid=(1,),
            in_specs=[ANYWHERE] * (PAIRS + 1),
            out_specs=ANYWHERE,
            scratch_shapes=[pltpu.SemaphoreType.DMA((2 * PAIRS,))],
        ),
        input_output_aliases={PAIRS + 1: 0},
        compiler_params=pltpu.CompilerParams(vmem_limit_bytes=SMALL),
        cost_estimate=COST,
        name="store_near",
    )(info, *near_here, handed)
    arrival_out, _ = combine_parts(info, [arrival, exchanged(arrival)])
    return prompt, handed.reshape(rows // 2, 2 * width), decode_out, arrival_out


def shards(
    prompt_query,
    prompt_pairs,
    decode_query,
    arrival_query,
    cache_pool,
    page_table,
    lengths,
    assignment,
):
    inst_count = lax.axis_size("inst")
    tp_count = lax.axis_size("tp")
    half = inst_count // 2
    inst = lax.axis_index("inst")
    tp_index = lax.axis_index("tp")
    info = jnp.concatenate([jnp.stack([inst, tp_index]), assignment])
    pages, page_len = cache_pool.shape[0], cache_pool.shape[1]
    by_token = cache_pool.reshape(pages * page_len, -1)

    def cached(after=()):
        return cache_attention(info, page_table, lengths, decode_query, by_token, page_len, after)

    def exchanged(part):
        return lax.ppermute(part, "tp", [(0, 1), (1, 0)])

    def combined(part):
        return combine_parts(info, [lax.all_gather(part, "tp")])[0]

    heads = GROUP
    steps = prompt_query.shape[1] // (heads * HEADDIM)

    def prompt_part(first, last, earlier, after=()):
        return prompt_attention(
            info, prompt_query, prompt_pairs, first, last - first, heads, earlier, after
        )

    row_units = prompt_pairs.shape[0] // (2 * UNIT)
    if inst_count == 4 * PAIRS and tp_count == 2 and row_units == 5 * half and steps == 4:
        cuts = (0, 1, 4)
        return two_way_handoff(
            prompt_pairs,
            info,
            assignment[0] >= 0,
            arrival_query,
            lambda n, earlier, after: prompt_part(cuts[n], cuts[n + 1], earlier, after),
            cached,
            exchanged,
        )
    handed = relay_handoff(prompt_pairs, assignment, inst_count)
    arrival = arrival_part(
        whole_rows_kernel, info, arrival_query, [handed], [IN_VMEM], [], "whole_rows"
    )
    prefill_out, _ = prompt_part(0, steps, None)
    return prefill_out, handed, combined(cached()[0]), combined(arrival)


def solution(mesh):
    return jax.shard_map(
        shards,
        mesh=mesh,
        in_specs=(
            P("inst", "tp"),
            P("inst", "tp"),
            P("inst", None),
            P("inst", None),
            P(("inst", "tp"), None, None),
            P("inst", "tp"),
            P("inst"),
            P(),
        ),
        out_specs=(P("inst", "tp"), P(("inst", "tp"), None), P("inst", None), P("inst", None)),
        check_vma=False,
    )
```

```python
import functools

import jax
import jax.numpy as jnp
from jax import lax
from jax.experimental import pallas as pl
from jax.experimental.pallas import tpu as pltpu
from jax.sharding import PartitionSpec as P

QHEADS = 64
KVHEADS = 8
HEADDIM = 128
GROUP = QHEADS // KVHEADS
SCALE = HEADDIM ** (-0.5)
LOG2E = 1.4426950408889634
NEG_FILL = -1e30
TILE = 128
VMEM = 24 * 1024 * 1024
SMALL = 1024 * 1024
MEDIUM = 8 * 1024 * 1024
LARGE = 57 * 1024 * 1024
COST = pl.CostEstimate(flops=1, bytes_accessed=1, transcendentals=0)


INST, TP, FIRST = 0, 1, 2


def on_prefill(info):
    return info[INST] < info.shape[0] - FIRST


def order(info):
    half = info.shape[0] - FIRST
    return info[INST] - jnp.where(on_prefill(info), 0, half)


def source_of(info, receiver):
    half = info.shape[0] - FIRST
    found = jnp.int32(0)
    for p in range(half):
        found = jnp.where(info[FIRST + p] == receiver, p, found)
    return found


def dot_t(a, b):
    return lax.dot_general(a, b, (((1,), (1,)), ((), ())), preferred_element_type=jnp.float32)


def dot(a, b):
    return lax.dot_general(a, b, (((1,), (0,)), ((), ())), preferred_element_type=jnp.float32)


def prompt_kernel(heads, info_ref, q_ref, kv_ref, *rest):
    out_ref = rest[-2]
    length = q_ref.shape[0]

    @pl.when(jnp.logical_not(on_prefill(info_ref)))
    def _():
        out_ref[...] = jnp.zeros_like(out_ref)

    @pl.when(on_prefill(info_ref))
    def _():
        rows_all = lax.broadcasted_iota(jnp.int32, (TILE, TILE), 0)
        cols_all = lax.broadcasted_iota(jnp.int32, (TILE, TILE), 1)
        below = jnp.concatenate([rows_all >= cols_all] * heads, axis=0)
        ones = jnp.ones((length, HEADDIM), jnp.bfloat16)
        values = jnp.concatenate([kv_ref[:, HEADDIM:], ones], axis=1)
        def scores_of(start):
            stop = start + TILE
            queries = jnp.concatenate(
                [q_ref[start:stop, h * HEADDIM : (h + 1) * HEADDIM] for h in range(heads)], axis=0
            )
            last = jnp.where(below, dot_t(queries, kv_ref[start:stop, :HEADDIM]), NEG_FILL)
            return [dot_t(queries, kv_ref[:start, :HEADDIM]), last] if start else [last]

        coming = scores_of(0)
        for start in range(0, length, TILE):
            stop = start + TILE
            scores = coming
            if stop < length:
                coming = scores_of(stop)
            peak = functools.reduce(
                jnp.maximum, [jnp.max(part, axis=1, keepdims=True) for part in scores]
            )
            weights = [
                jnp.exp2((part - peak) * (SCALE * LOG2E)).astype(jnp.bfloat16) for part in scores
            ]
            mixed = dot(weights[-1], values[start:stop])
            if start:
                mixed = mixed + dot(weights[0], values[:start])
            result = (mixed[:, :HEADDIM] / mixed[:, HEADDIM:]).astype(jnp.bfloat16)
            for h in range(heads):
                out_ref[start:stop, h * HEADDIM : (h + 1) * HEADDIM] = result[
                    h * TILE : (h + 1) * TILE
                ]


MARK = jax.ShapeDtypeStruct((8, 128), jnp.float32)
IN_HBM = pl.BlockSpec(memory_space=pltpu.HBM)
ANYWHERE = pl.BlockSpec(memory_space=pl.ANY)
IN_VMEM = pl.BlockSpec(memory_space=pltpu.VMEM)


def prompt_attention(info, queries, pairs, first, steps, heads, earlier, after):
    length, width = queries.shape
    per_kv = GROUP // heads

    def q_map(i, info_ref):
        return (0, jnp.where(on_prefill(info_ref), i + first, 0))

    def kv_map(i, info_ref):
        return (0, jnp.where(on_prefill(info_ref), (i + first) // per_kv, 0))

    in_specs = [
        pl.BlockSpec((length, heads * HEADDIM), q_map),
        pl.BlockSpec((length, 2 * HEADDIM), kv_map),
    ]
    operands = [info, queries, pairs]
    aliases = {}
    if earlier is not None:
        in_specs.append(ANYWHERE)
        operands.append(earlier)
        aliases = {3: 0}
    return pl.pallas_call(
        functools.partial(prompt_kernel, heads),
        out_shape=(jax.ShapeDtypeStruct((length, width), jnp.bfloat16), MARK),
        grid_spec=pltpu.PrefetchScalarGridSpec(
            num_scalar_prefetch=1,
            grid=(steps,),
            in_specs=in_specs + [IN_HBM] * len(after),
            out_specs=(
                pl.BlockSpec((length, heads * HEADDIM), lambda i, info_ref: (0, i + first)),
                IN_HBM,
            ),
        ),
        input_output_aliases=aliases,
        compiler_params=pltpu.CompilerParams(vmem_limit_bytes=LARGE),
        cost_estimate=COST,
        name="prompt_attention",
    )(*operands, *after)


def head_queries(block, head):
    start = head * GROUP * HEADDIM
    return jnp.concatenate(
        [
            block[r : r + 1, start + g * HEADDIM : start + (g + 1) * HEADDIM]
            for r in range(block.shape[0])
            for g in range(GROUP)
        ],
        axis=0,
    ).astype(jnp.bfloat16)


def store_part(out_ref, head, mixed, peak, total):
    lane = lax.broadcasted_iota(jnp.int32, mixed.shape, 1)
    out_ref[head, :, :HEADDIM] = mixed
    out_ref[head, :, HEADDIM:] = jnp.where(lane < HEADDIM // 2, peak, total)


def store_short(out_ref, found):
    lane = lax.broadcasted_iota(jnp.int32, out_ref.shape[1:], 1)
    stats = jnp.zeros(out_ref.shape[1:], jnp.float32)
    for head, (mixed, peak, total) in enumerate(found):
        out_ref[head] = mixed
        stats = jnp.where(lane == head, peak, stats)
        stats = jnp.where(lane == KVHEADS + head, total, stats)
    out_ref[KVHEADS] = stats


def load_part(ref, head):
    if ref.shape[-1] == HEADDIM:
        stats = ref[KVHEADS]
        return ref[head], stats[:, head : head + 1], stats[:, KVHEADS + head : KVHEADS + head + 1]
    part = ref[head]
    return part[:, :HEADDIM], part[:, HEADDIM : HEADDIM + 1], part[:, -1:]


def merged(parts):
    peak = functools.reduce(jnp.maximum, [part[1] for part in parts])
    factors = [jnp.exp(part[1] - peak) for part in parts]
    total = sum(part[2] * f for part, f in zip(parts, factors))
    mixed = sum(part[0] * f for part, f in zip(parts, factors))
    return mixed, peak, total


def cache_kernel(page_len, info_ref, table_ref, lengths_ref, q_ref, kv_ref, *rest):
    out_ref, _, count_ref = rest[-3:]
    rows, slots = table_ref.shape

    @pl.when(jnp.logical_and(jnp.logical_not(on_prefill(info_ref)), pl.program_id(0) == 0))
    def _():
        token = lax.broadcasted_iota(jnp.int32, (GROUP, count_ref.shape[1]), 1)
        page, offset = token // page_len, token % page_len
        for r in range(rows):
            count = jnp.zeros(token.shape, jnp.float32)
            for slot in range(slots):
                left = lengths_ref[r] - (info_ref[TP] * slots + slot) * page_len
                valid = jnp.logical_and(page == table_ref[r, slot], offset < left)
                count = count + jnp.where(valid, 1.0, 0.0)
            count_ref[r * GROUP : (r + 1) * GROUP] = count

    @pl.when(jnp.logical_not(on_prefill(info_ref)))
    def _():
        count = count_ref[...]
        here = count > 0.0
        block = q_ref[...].astype(jnp.float32)
        for head in range(out_ref.shape[0]):
            start = 2 * head * HEADDIM
            keys = kv_ref[:, start : start + HEADDIM]
            values = kv_ref[:, start + HEADDIM : start + 2 * HEADDIM]
            scores = dot_t(head_queries(block, head), keys) * SCALE
            scores = jnp.where(here, scores, NEG_FILL)
            peak = jnp.max(scores, axis=1, keepdims=True)
            weights = jnp.where(here, jnp.exp(scores - peak), 0.0)
            total = jnp.sum(weights * count, axis=1, keepdims=True)
            rounded = weights.astype(jnp.bfloat16).astype(jnp.float32) * count
            store_part(out_ref, head, dot(rounded.astype(jnp.bfloat16), values), peak, total)


def cache_attention(info, table, lengths, queries, pool, page_len, after):
    rows = queries.shape[0]
    tokens = pool.shape[0]
    steps = 2
    heads = KVHEADS // steps

    def step(n, info):
        return jnp.where(on_prefill(info), 0, n)

    return pl.pallas_call(
        functools.partial(cache_kernel, page_len),
        out_shape=(
            jax.ShapeDtypeStruct((KVHEADS, rows * GROUP, 2 * HEADDIM), jnp.float32),
            MARK,
        ),
        grid_spec=pltpu.PrefetchScalarGridSpec(
            num_scalar_prefetch=3,
            grid=(steps,),
            in_specs=[
                pl.BlockSpec((rows, heads * GROUP * HEADDIM), lambda n, info, *_: (0, step(n, info))),
                pl.BlockSpec((tokens, 2 * heads * HEADDIM), lambda n, info, *_: (0, step(n, info))),
            ]
            + [IN_HBM] * len(after),
            out_specs=(
                pl.BlockSpec(
                    (heads, rows * GROUP, 2 * HEADDIM), lambda n, info, *_: (step(n, info), 0, 0)
                ),
                IN_HBM,
            ),
            scratch_shapes=[pltpu.VMEM((rows * GROUP, tokens), jnp.float32)],
        ),
        compiler_params=pltpu.CompilerParams(vmem_limit_bytes=LARGE),
        cost_estimate=COST,
        name="cache_attention",
    )(info, table, lengths, queries, pool, *after)


def rows_part(queries, rows, out_ref, earlier_ref):
    block = queries[...].astype(jnp.float32)
    heads = rows[0].shape[1] // (2 * HEADDIM)
    places = [(rows[head // heads], 2 * (head % heads) * HEADDIM) for head in range(KVHEADS)]
    scores = [
        dot_t(head_queries(block, head), held[:, start : start + HEADDIM]) * SCALE
        for head, (held, start) in enumerate(places)
    ]
    peaks = [jnp.max(score, axis=1, keepdims=True) for score in scores]
    weights = [jnp.exp(score - peak) for score, peak in zip(scores, peaks)]
    totals = [jnp.sum(weight, axis=1, keepdims=True) for weight in weights]
    mixes = [
        dot(weight.astype(jnp.bfloat16), held[:, start + HEADDIM : start + 2 * HEADDIM])
        for weight, (held, start) in zip(weights, places)
    ]
    found = list(zip(mixes, peaks, totals))
    if earlier_ref is not None:
        found = [merged([part, load_part(earlier_ref, head)]) for head, part in enumerate(found)]
    store_short(out_ref, found)


def flat_rows(pieces):
    wide = [piece.astype(jnp.float32).reshape(-1, piece.shape[-1]) for piece in pieces]
    return jnp.concatenate(wide, axis=0).astype(jnp.bfloat16)


def whole_rows_kernel(info_ref, q_ref, rows_ref, out_ref):
    rows_part(q_ref, [rows_ref[...]], out_ref, None)


def far_rows_kernel(near, info_ref, q_ref, slots_ref, part_ref, handed_ref, held_ref, zero_ref, load, sems):
    half = 2 * PAIRS
    far, width = slots_ref.shape[1], slots_ref.shape[-1]

    @pl.when(jnp.logical_not(on_prefill(info_ref)))
    def _():
        staged = pltpu.make_async_copy(slots_ref, held_ref, load)
        staged.start()
        staged.wait()
        waits = []
        for t in range(2):
            for i in range(half):
                slot = t * half + i
                target = handed_ref.at[pl.ds(near + i * far, far), :, pl.ds(t * width, width)]
                waits.append(pltpu.make_async_copy(held_ref.at[slot], target, sems.at[slot]))
        for copy in waits:
            copy.start()
        rows = [flat_rows([held_ref[t * half + i] for i in range(half)]) for t in range(2)]
        rows_part(q_ref, rows, part_ref, None)
        for copy in waits:
            copy.wait()

    @pl.when(on_prefill(info_ref))
    def _():
        zero_ref[...] = jnp.zeros_like(zero_ref)
        size = zero_ref.shape[0]
        waits = []
        for n in range(handed_ref.shape[0] // size):
            target = handed_ref.at[pl.ds(n * size, size)]
            waits.append(pltpu.make_async_copy(zero_ref, target, sems.at[n]))
        for copy in waits:
            copy.start()
        for copy in waits:
            copy.wait()


def near_rows_kernel(info_ref, q_ref, earlier_ref, *refs):
    *part_refs, out_ref = refs

    @pl.when(jnp.logical_not(on_prefill(info_ref)))
    def _():
        rows = [flat_rows([part[t] for part in part_refs]) for t in range(2)]
        rows_part(q_ref, rows, out_ref, earlier_ref)


def arrival_part(kernel, info, query, operands, places, scratch, name):
    return pl.pallas_call(
        kernel,
        out_shape=jax.ShapeDtypeStruct((KVHEADS + 1, GROUP, HEADDIM), jnp.float32),
        grid_spec=pltpu.PrefetchScalarGridSpec(
            num_scalar_prefetch=1,
            grid=(1,),
            in_specs=[IN_VMEM] + places,
            out_specs=IN_VMEM,
            scratch_shapes=scratch,
        ),
        compiler_params=pltpu.CompilerParams(vmem_limit_bytes=VMEM),
        cost_estimate=COST,
        name=name,
    )(info, query, *operands)


def combine_kernel(count, info_ref, *refs):
    part_refs, out_ref = refs[:count], refs[-2]

    @pl.when(on_prefill(info_ref))
    def _():
        out_ref[...] = jnp.zeros_like(out_ref)

    @pl.when(jnp.logical_not(on_prefill(info_ref)))
    def _():
        results = []
        for head in range(KVHEADS):
            if count == 2:
                here, there = [load_part(ref, head) for ref in part_refs]
                first = info_ref[TP] == 0
                parts = [
                    [jnp.where(first, x, y) for x, y in zip(here, there)],
                    [jnp.where(first, y, x) for x, y in zip(here, there)],
                ]
            else:
                every = part_refs[0]
                parts = [load_part(every.at[n], head) for n in range(every.shape[0])]
            mixed, _, total = merged(parts)
            results.append(mixed / total)
        rows = [
            jnp.concatenate(
                [
                    results[head][r * GROUP + g : r * GROUP + g + 1]
                    for head in range(KVHEADS)
                    for g in range(GROUP)
                ],
                axis=1,
            )
            for r in range(out_ref.shape[0])
        ]
        out_ref[...] = jnp.concatenate(rows, axis=0).astype(jnp.bfloat16)


def combine_parts(info, parts, after=()):
    rows = parts[0].shape[-2] // GROUP
    return pl.pallas_call(
        functools.partial(combine_kernel, len(parts)),
        out_shape=(jax.ShapeDtypeStruct((rows, QHEADS * HEADDIM), jnp.bfloat16), MARK),
        grid_spec=pltpu.PrefetchScalarGridSpec(
            num_scalar_prefetch=1,
            grid=(1,),
            in_specs=[IN_VMEM] * len(parts) + [IN_HBM] * len(after),
            out_specs=(IN_VMEM, IN_HBM),
        ),
        compiler_params=pltpu.CompilerParams(vmem_limit_bytes=VMEM),
        cost_estimate=COST,
        name="combine_parts",
    )(info, *parts, *after)


def relay_handoff(pairs, assignment, inst_count):
    half = inst_count // 2
    decode_ids = jnp.arange(half, dtype=jnp.int32)
    matches = assignment[None, :] == decode_ids[:, None]
    source = jnp.sum(jnp.where(matches, decode_ids[None, :], 0), axis=1).astype(jnp.int32)
    moved = lax.all_to_all(pairs, "tp", split_axis=0, concat_axis=1, tiled=True)
    lanes = 1024 if moved.size % (inst_count * 1024) == 0 else HEADDIM
    pieces = moved.reshape(inst_count, -1, lanes)
    spread = lax.all_to_all(pieces, "inst", split_axis=0, concat_axis=0, tiled=True)
    chosen = jnp.stack(
        [lax.dynamic_index_in_dim(spread, source[d], 0, False) for d in range(half)], axis=0
    )
    outgoing = jnp.concatenate([jnp.zeros_like(chosen), chosen], axis=0)
    delivered = lax.all_to_all(outgoing, "inst", split_axis=0, concat_axis=0, tiled=True)
    return delivered.reshape(moved.shape)


UNIT = 8
PAIRS = 4
PREFILL, DECODE = True, False


def copy_kernel(plan, side, counts, info_ref, *refs):
    inputs, marks, outputs, stages = counts
    sources, targets = refs[:inputs], refs[inputs + marks : inputs + marks + outputs]
    held, sems = refs[-1 - stages : -1], refs[-1]

    @pl.when(on_prefill(info_ref) == side)
    def _():
        started = []
        for source, target in zip(sources, held):
            started.append(pltpu.make_async_copy(source, target, sems.at[len(started)]))
        for copy in started:
            copy.start()
        for copy in started:
            copy.wait()
        started = []
        for source, target in plan(info_ref, held or sources, targets):
            started.append(pltpu.make_async_copy(source, target, sems.at[len(started)]))
        for copy in started:
            copy.start()
        for copy in started:
            copy.wait()


def copies(plan, number, info, operands, shapes, name, after=(), stage=False, side=PREFILL):
    held = [pltpu.VMEM(x.shape, x.dtype) for x in operands] if stage else []
    return pl.pallas_call(
        functools.partial(copy_kernel, plan, side, (len(operands), len(after), len(shapes), len(held))),
        out_shape=tuple(jax.ShapeDtypeStruct(shape, jnp.bfloat16) for shape in shapes),
        grid_spec=pltpu.PrefetchScalarGridSpec(
            num_scalar_prefetch=1,
            grid=(1,),
            in_specs=[ANYWHERE] * len(operands) + [IN_HBM] * len(after),
            out_specs=tuple([ANYWHERE] * len(shapes)),
            scratch_shapes=held + [pltpu.SemaphoreType.DMA((number,))],
        ),
        compiler_params=pltpu.CompilerParams(vmem_limit_bytes=MEDIUM if stage else SMALL),
        cost_estimate=COST,
        name=name,
    )(info, *operands, *after)


def cut_kernel(near, far, rows_ref, near_ref, *refs):
    *far_refs, held_ref, sems = refs
    inst, half = lax.axis_index("inst"), lax.axis_size("inst") // 2
    units = rows_ref.shape[0] // 2

    @pl.when(inst < half)
    def _():
        loads, stores, others = [], [], []
        for tau in range(2):
            first = tau * units
            held = held_ref.at[tau]
            loads.append(pltpu.make_async_copy(rows_ref.at[pl.ds(first, near)], held, sems.at[tau]))
            stores.append(pltpu.make_async_copy(held, near_ref.at[tau], sems.at[2 + tau]))
            loads[-1].start()
        for s, far_ref in enumerate(far_refs):
            relay = jnp.bitwise_xor(lax.div(inst, 2), s ^ 2)
            for tau in range(2):
                source = rows_ref.at[pl.ds(tau * units + near + relay * far, far)]
                others.append(
                    pltpu.make_async_copy(source, far_ref.at[tau], sems.at[4 + len(others)])
                )
                others[-1].start()
        for load, store in zip(loads, stores):
            load.wait()
            store.start()
        for copy in stores + others:
            copy.wait()


def relay_slots_kernel(far, info_ref, keep_ref, recv_ref, out_ref, sems):
    half = 2 * PAIRS

    @pl.when(jnp.logical_not(on_prefill(info_ref)))
    def _():
        here = order(info_ref)
        waits = []
        for d in range(half):
            source = source_of(info_ref, d)
            same = lax.rem(source, 2) == lax.rem(here, 2)
            shift = jnp.bitwise_xor(jnp.bitwise_xor(lax.div(here, 2), lax.div(source, 2)), 2)
            for tau in range(2):
                slot = tau * half + d
                target = out_ref.at[slot]
                mine = pltpu.make_async_copy(keep_ref.at[shift, tau], target, sems.at[slot])
                other = pltpu.make_async_copy(recv_ref.at[shift, tau], target, sems.at[slot])
                pl.when(same)(mine.start)
                pl.when(jnp.logical_not(same))(other.start)
                waits.append(mine)
        for copy in waits:
            copy.wait()


def store_near_kernel(near, info_ref, *refs):
    *parts, _, handed_ref, sems = refs
    width = parts[0].shape[-1]

    @pl.when(jnp.logical_not(on_prefill(info_ref)))
    def _():
        waits = []
        for t in range(2):
            for s, part in enumerate(parts):
                pair = jnp.bitwise_xor(lax.div(order(info_ref), 2), s ^ 2)
                target = handed_ref.at[pl.ds(pair * 2 * near, 2 * near), :, pl.ds(t * width, width)]
                waits.append(pltpu.make_async_copy(part.at[t], target, sems.at[len(waits)]))
        for copy in waits:
            copy.start()
        for copy in waits:
            copy.wait()


def two_way_handoff(pairs, info, always, arrival_query, prompt_part, cached, exchanged):
    half = 2 * PAIRS
    rows, width = pairs.shape
    units = rows // (2 * UNIT)
    far_all = units * 2 // (5 * half) * half
    near_all = units - far_all
    near, far = near_all // half, far_all // half
    block = (UNIT, width)
    by_unit = pairs.reshape((rows // UNIT,) + block)
    groups = [[base + 2 * i + tau for tau in range(2) for i in range(half)] for base in (0, 2 * half)]

    def crossing(array, s):
        hops = [
            (2 * p + k, half + 2 * (p ^ s ^ 2) + k) for p in range(PAIRS) for k in range(2)
        ]
        return lax.ppermute(array, "inst", hops)

    def beside(array, base):
        return lax.ppermute(array, "inst", [(base + i, base + (i ^ 1)) for i in range(half)])

    def spread_out(array):
        return lax.all_to_all(
            array, ("inst", "tp"), 0, 0, axis_index_groups=groups, tiled=True
        )

    def for_neighbour(pre, sources, targets):
        plan = []
        for s in range(PAIRS):
            receiver = jnp.bitwise_xor(lax.div(order(pre), 2), s ^ 2) * 2 + 1 - lax.rem(order(pre), 2)
            for t in range(2):
                origin = t * half + source_of(pre, receiver)
                plan.append((sources[0].at[origin], targets[0].at[s, t]))
        return plan

    def for_receivers(pre, sources, targets):
        plan = []
        for s in range(PAIRS):
            receiver = jnp.bitwise_xor(lax.div(order(pre), 2), s ^ 2) * 2 + lax.rem(order(pre), 2)
            for t in range(2):
                origin = t * half + source_of(pre, receiver)
                mine = targets[s].at[t, pl.ds(lax.rem(order(pre), 2) * near, near)]
                other = targets[s].at[t, pl.ds((1 - lax.rem(order(pre), 2)) * near, near)]
                plan.append((sources[0].at[origin], mine))
                plan.append((sources[1].at[s, t], other))
        return plan

    def split(pre, sources, targets):
        plan = []
        for s in range(PAIRS):
            for tau in range(2):
                mine = sources[s].at[tau, pl.ds(lax.rem(order(pre), 2) * far, far)]
                other = sources[s].at[tau, pl.ds((1 - lax.rem(order(pre), 2)) * far, far)]
                plan.append((mine, targets[0].at[s, tau]))
                plan.append((other, targets[1].at[s, tau]))
        return plan

    near_shape = (2, 2 * near) + block

    def gather_stage(spread, *marks):
        (outgoing,) = copies(
            for_neighbour, 2 * PAIRS, info, [spread], [(PAIRS, 2, near) + block], "for_neighbour", marks
        )
        incoming = beside(outgoing, 0)
        return copies(
            for_receivers, 4 * PAIRS, info, [spread, incoming], [near_shape] * PAIRS, "for_receivers"
        )

    def first_stage(near_rows, *far_parts):
        spread = spread_out(near_rows.reshape((2 * half, near) + block))
        far_here = [crossing(part, s) for s, part in enumerate(far_parts, 1)]
        part, mark = cached([near_rows])
        prompt, mark = prompt_part(0, None, [mark])
        return *staged(gather_stage, spread, mark), prompt, part, *far_here

    def second_stage(prompt, part, other, *far_here):
        keep, give = copies(
            split,
            4 * PAIRS,
            info,
            list(far_here),
            [(PAIRS, 2, far) + block] * 2,
            "split_relays",
            stage=True,
            side=DECODE,
        )
        taken = beside(give, half)
        slots = pl.pallas_call(
            functools.partial(relay_slots_kernel, far),
            out_shape=jax.ShapeDtypeStruct((2 * half, far) + block, jnp.bfloat16),
            grid_spec=pltpu.PrefetchScalarGridSpec(
                num_scalar_prefetch=1,
                grid=(1,),
                in_specs=[ANYWHERE] * 2,
                out_specs=ANYWHERE,
                scratch_shapes=[pltpu.SemaphoreType.DMA((2 * half,))],
            ),
            compiler_params=pltpu.CompilerParams(vmem_limit_bytes=SMALL),
            cost_estimate=COST,
            name="relay_slots",
        )(info, keep, taken)
        prompt, mark = prompt_part(1, prompt, [slots])
        decode_out, _ = combine_parts(info, [part, other], [mark])
        slots = spread_out(slots)
        arrival, handed = pl.pallas_call(
            functools.partial(far_rows_kernel, near_all),
            out_shape=(
                jax.ShapeDtypeStruct((KVHEADS + 1, GROUP, HEADDIM), jnp.float32),
                jax.ShapeDtypeStruct((units, UNIT, 2 * width), jnp.bfloat16),
            ),
            grid_spec=pltpu.PrefetchScalarGridSpec(
                num_scalar_prefetch=1,
                grid=(1,),
                in_specs=[IN_VMEM, ANYWHERE],
                out_specs=(IN_VMEM, ANYWHERE),
                scratch_shapes=[
                    pltpu.VMEM(slots.shape, slots.dtype),
                    pltpu.VMEM((half, UNIT, 2 * width), jnp.bfloat16),
                    pltpu.SemaphoreType.DMA,
                    pltpu.SemaphoreType.DMA((2 * half,)),
                ],
            ),
            compiler_params=pltpu.CompilerParams(vmem_limit_bytes=VMEM),
            cost_estimate=COST,
            name="far_rows",
        )(info, arrival_query, slots)
        return prompt, handed, decode_out, arrival

    def staged(stage, *operands):
        def never(*operands):
            outs = [jnp.zeros(out.shape, out.dtype) for out in jax.eval_shape(stage, *operands)]
            return (operands[0], *outs[1:]) if stage is second_stage else tuple(outs)

        return lax.cond(always, lambda *operands: tuple(stage(*operands)), never, *operands)

    near_rows, *far_parts = pl.pallas_call(
        functools.partial(cut_kernel, near_all, 2 * far),
        out_shape=tuple(
            jax.ShapeDtypeStruct(shape + block, jnp.bfloat16)
            for shape in [(2, near_all)] + [(2, 2 * far)] * PAIRS
        ),
        grid=(1,),
        in_specs=[ANYWHERE],
        out_specs=(ANYWHERE,) * (1 + PAIRS),
        scratch_shapes=[
            pltpu.VMEM((2, near_all) + block, jnp.bfloat16),
            pltpu.SemaphoreType.DMA((4 + 2 * PAIRS,)),
        ],
        compiler_params=pltpu.CompilerParams(vmem_limit_bytes=MEDIUM),
        cost_estimate=COST,
        name="cut_rows",
    )(by_unit)
    first = crossing(far_parts[0], 0)
    outs = staged(first_stage, near_rows, *far_parts[1:])
    near_parts, (prompt, part), far_here = outs[:PAIRS], outs[PAIRS : PAIRS + 2], outs[PAIRS + 2 :]
    other = exchanged(part)
    near_parts, first = lax.optimization_barrier((near_parts, first))
    far_here = [first, *far_here]
    near_here = [crossing(near_part, s) for s, near_part in enumerate(near_parts)]
    prompt, handed, decode_out, arrival = staged(second_stage, prompt, part, other, *far_here)
    arrival = arrival_part(
        near_rows_kernel,
        info,
        arrival_query,
        [arrival, *near_here],
        [IN_VMEM] * (PAIRS + 1),
        [],
        "near_rows",
    )
    handed = pl.pallas_call(
        functools.partial(store_near_kernel, near),
        out_shape=jax.ShapeDtypeStruct(handed.shape, handed.dtype),
        grid_spec=pltpu.PrefetchScalarGridSpec(
            num_scalar_prefetch=1,
            grid=(1,),
            in_specs=[ANYWHERE] * (PAIRS + 1),
            out_specs=ANYWHERE,
            scratch_shapes=[pltpu.SemaphoreType.DMA((2 * PAIRS,))],
        ),
        input_output_aliases={PAIRS + 1: 0},
        compiler_params=pltpu.CompilerParams(vmem_limit_bytes=SMALL),
        cost_estimate=COST,
        name="store_near",
    )(info, *near_here, handed)
    arrival_out, _ = combine_parts(info, [arrival, exchanged(arrival)])
    return prompt, handed.reshape(rows // 2, 2 * width), decode_out, arrival_out


def shards(
    prompt_query,
    prompt_pairs,
    decode_query,
    arrival_query,
    cache_pool,
    page_table,
    lengths,
    assignment,
):
    inst_count = lax.axis_size("inst")
    tp_count = lax.axis_size("tp")
    half = inst_count // 2
    inst = lax.axis_index("inst")
    tp_index = lax.axis_index("tp")
    info = jnp.concatenate([jnp.stack([inst, tp_index]), assignment])
    pages, page_len = cache_pool.shape[0], cache_pool.shape[1]
    by_token = cache_pool.reshape(pages * page_len, -1)

    def cached(after=()):
        return cache_attention(info, page_table, lengths, decode_query, by_token, page_len, after)

    def exchanged(part):
        return lax.ppermute(part, "tp", [(0, 1), (1, 0)])

    def combined(part):
        return combine_parts(info, [lax.all_gather(part, "tp")])[0]

    heads = GROUP
    steps = prompt_query.shape[1] // (heads * HEADDIM)

    def prompt_part(first, last, earlier, after=()):
        return prompt_attention(
            info, prompt_query, prompt_pairs, first, last - first, heads, earlier, after
        )

    row_units = prompt_pairs.shape[0] // (2 * UNIT)
    if inst_count == 4 * PAIRS and tp_count == 2 and row_units == 5 * half and steps == 4:
        cuts = (0, 1, 4)
        return two_way_handoff(
            prompt_pairs,
            info,
            assignment[0] >= 0,
            arrival_query,
            lambda n, earlier, after: prompt_part(cuts[n], cuts[n + 1], earlier, after),
            cached,
            exchanged,
        )
    handed = relay_handoff(prompt_pairs, assignment, inst_count)
    arrival = arrival_part(
        whole_rows_kernel, info, arrival_query, [handed], [IN_VMEM], [], "whole_rows"
    )
    prefill_out, _ = prompt_part(0, steps, None)
    return prefill_out, handed, combined(cached()[0]), combined(arrival)


def solution(mesh):
    return jax.shard_map(
        shards,
        mesh=mesh,
        in_specs=(
            P("inst", "tp"),
            P("inst", "tp"),
            P("inst", None),
            P("inst", None),
            P(("inst", "tp"), None, None),
            P("inst", "tp"),
            P("inst"),
            P(),
        ),
        out_specs=(P("inst", "tp"), P(("inst", "tp"), None), P("inst", None), P("inst", None)),
        check_vma=False,
    )
```
